32 devices in a mesh: rep: 4 (over x, core), shard: 8 (over z, y).
Axes of the slice: x: 2, y: 2, z: 4, core: 2. Of those that a mesh axis runs over, the one named last changes fastest.
Arguments:
- hidden: bfloat16 [2048, 3584], P(('rep', 'shard')), may hold values from -6 to 6
- norm_gain: float32 [3584], replicated, may hold values from 0.5 to 1.5
- input_ids: int32 [2048], replicated, may hold values from 0 to 16383
- sampled_ids: int32 [2048], replicated, may hold values from 0 to 16383
- head_weight: bfloat16 [3584, 16384], P(None, 'shard'), as said below
- moment: bfloat16 [3584, 16384], P('rep', 'shard'), may hold values from -0.29882812 to 0.29882812
- curvature: bfloat16 [3584, 16384], P('rep', 'shard'), may hold values from 0.049804688 to 5
Outputs:
- moment_new: bfloat16 [3584, 16384], P('rep', 'shard')
- curvature_new: bfloat16 [3584, 16384], P('rep', 'shard')
- update_direction: bfloat16 [3584, 16384], P('rep', 'shard')
The draws below stay inside these ranges and needn't reach their ends.
Inputs may be any that keep to these rules, and one draw needn't show every extreme that they name: Entries of head_weight are finite.
All inputs are finite; a program needn't handle non-finite values.
Results may differ from the reference program's by a relative error of at most 0.039.
Values may be sent and summed in bfloat16 or wider, within the bound.
No kernel may reach another device: no remote copies, remote signals or barrier semaphores. Data moves between devices by JAX's collectives and lax.ppermute only.
A program may use at most 192 MiB of HBM per device.

```python
import math
import jax
import jax.numpy as jnp
import numpy as np
from jax import lax

D = 3584
V = 16384
GROUP_TOK = 512
TOKENS = 2048
N_REP = 4


def draw_head_weight(key, part):
    key = jax.random.fold_in(key, 7)
    key_entries = jax.random.fold_in(key, 0)
    key_scale = jax.random.fold_in(key, 2)
    entries = jax.random.truncated_normal(key_entries, -4.0, 4.0, (D, V), jnp.float32)
    col_scale = jnp.exp(jax.random.uniform(key_scale, (V,), jnp.float32, math.log(0.3), math.log(3.0)))
    result = col_scale * entries
    return (result * (3.0 / math.sqrt(D))).astype(jnp.bfloat16)


def with_ends(values, rng, least, top_value):
    place = [jax.random.randint(jax.random.fold_in(rng, axis), (), 0, length) for axis, length in enumerate(values.shape)]
    longest = values.shape.index(max(values.shape))
    next_to = place[:longest] + [(place[longest] + 1) % values.shape[longest]] + place[longest + 1:]
    return values.at[tuple(place)].set(least).at[tuple(next_to)].set(top_value)


def levels(rng, dims, pieces, least, high):
    factor_of, own = 1.0, jax.random.fold_in(rng, 6)
    for dim, blocks in pieces:
        steps = jnp.exp(jax.random.uniform(jax.random.fold_in(own, dim), (blocks,), jnp.float32, least / len(pieces), high / len(pieces)))
        factor_of = factor_of * jnp.repeat(steps, dims[dim] // blocks).reshape([-1 if axis == dim else 1 for axis in range(len(dims))])
    return factor_of


def cumulative_ranks(amount, slope):
    portions = [(1 << 20) // math.isqrt(grade ** slope) + 1 for grade in range(1, amount + 1)]
    scale = 1 + sum(portions) // (1 << 30)
    return np.cumsum(np.array([max(1, weight // scale) for weight in portions]))


def skewed_ids(rng, extent, count, skew):
    listing = cumulative_ranks(count, skew)
    ticket = jax.random.randint(jax.random.fold_in(rng, 1), extent, 0, int(listing[count - 1]))
    standing = jnp.searchsorted(jnp.asarray(listing, jnp.int32), ticket, side="right")
    return jax.random.permutation(jax.random.fold_in(rng, 2), count)[standing].astype(jnp.int32)


def centred(own_key, shape, spread, reach, cuts=(), kind=jnp.bfloat16):
    values = jax.random.normal(own_key, shape, jnp.float32) * spread
    if len(cuts) > 0:
        values = levels(own_key, shape, cuts, -0.22, 0.18) * values
    return jnp.clip(values, min=-reach, max=reach).astype(kind)


def setup_inputs(seed: int = 0) -> dict:
    streams_of = jax.random.split(jax.random.key(seed), 8)
    return {
        "hidden": centred(streams_of[0], (TOKENS, D), 1.0, 6.0, ((0, 32),)),
        "norm_gain": jnp.clip(1.0 + 0.1 * jax.random.normal(streams_of[1], (D,), jnp.float32), 0.5, 1.5),
        "input_ids": with_ends(skewed_ids(streams_of[2], (TOKENS,), V, 2), jax.random.fold_in(streams_of[2], 3), 0, V - 1).astype(jnp.int32),
        "sampled_ids": with_ends(skewed_ids(streams_of[3], (TOKENS,), V, 1), jax.random.fold_in(streams_of[3], 3), 0, V - 1).astype(jnp.int32),
        "head_weight": draw_head_weight(jax.random.fold_in(streams_of[7], 71), 0),
        "moment": centred(streams_of[5], (D, V), 0.05, 0.29882812, ((0, 4), (1, 8))),
        "curvature": jnp.clip(jnp.exp(math.log(5.0) - 4.609084 * jax.random.uniform(streams_of[6], (D, V), jnp.float32) ** levels(streams_of[6], (D, V), ((0, 4), (1, 8)), -0.2, 0.2)), 0.049804688, 5.0).astype(jnp.bfloat16),
    }


EPS_NORM = 1e-05
BETA_ONE = 0.96
BETA_TWO = 0.95
RHO_SCALE = 0.05

def normalize(hidden, norm_gain):
    values = hidden.astype(jnp.float32)
    row_scale = lax.rsqrt(lax.optimization_barrier(jnp.mean(values * values, axis=-1, keepdims=True)) + EPS_NORM)
    return (values * row_scale * norm_gain).astype(jnp.bfloat16)

def group_gradients(normed, token_ids, sample_ids, head_weight):
    logits = jnp.dot(normed, head_weight, preferred_element_type=jnp.float32)
    row_peak = lax.optimization_barrier(jnp.max(logits, axis=-1, keepdims=True))
    scaled_exp = jnp.exp(logits - row_peak)
    probabilities = (scaled_exp / lax.optimization_barrier(jnp.sum(scaled_exp, axis=-1, keepdims=True))).astype(jnp.bfloat16)
    shared = jnp.dot(normed.T, probabilities, preferred_element_type=jnp.float32)
    position = jnp.arange(GROUP_TOK)
    targets = jnp.where(position < GROUP_TOK - 1, jnp.roll(token_ids, -1), V).astype(jnp.int32)
    widened = normed.astype(jnp.float32)
    true_sums = jax.ops.segment_sum(widened, targets, num_segments=V + 1)[:V]
    sample_sums = jax.ops.segment_sum(widened, sample_ids, num_segments=V)
    true_part = (shared - true_sums.T).astype(jnp.bfloat16)
    sample_part = (shared - sample_sums.T).astype(jnp.bfloat16)
    return (true_part, sample_part)

def reference(hidden, norm_gain, input_ids, sampled_ids, head_weight, moment, curvature):
    normed = normalize(hidden, norm_gain).reshape(N_REP, GROUP_TOK, D)
    token_ids = input_ids.reshape(N_REP, GROUP_TOK)
    sample_ids = sampled_ids.reshape(N_REP, GROUP_TOK)

    def accumulate(running, inputs):
        true_part, sample_part = group_gradients(inputs[0], inputs[1], inputs[2], head_weight)
        return ((running[0] + true_part.astype(jnp.float32), running[1] + sample_part.astype(jnp.float32)), None)
    empty_sum = jnp.zeros((D, V), jnp.float32)
    (gradient, sample_grad), leftover = lax.scan(accumulate, (empty_sum, empty_sum), (normed, token_ids, sample_ids))
    moment_new = BETA_ONE * moment.astype(jnp.float32) + (1.0 - BETA_ONE) * gradient
    curvature_new = BETA_TWO * curvature.astype(jnp.float32) + (1.0 - BETA_TWO) * sample_grad * sample_grad
    update_direction = jnp.clip(moment_new / (RHO_SCALE * curvature_new), -1.0, 1.0)
    return (moment_new.astype(jnp.bfloat16), curvature_new.astype(jnp.bfloat16), update_direction.astype(jnp.bfloat16))
```

```python
import functools

import jax
import jax.numpy as jnp
import numpy as np
from jax import lax
from jax.experimental import pallas as pl
from jax.experimental.pallas import tpu as pltpu
from jax.sharding import PartitionSpec as P

EPS_NORM = 1e-05
BETA_ONE = 0.96
BETA_TWO = 0.95
RHO_SCALE = 0.05
GATHER_BYTES = 32 * 1024 * 1024


def normalize(hidden, norm_gain):
    values = hidden.astype(jnp.float32)
    row_scale = lax.rsqrt(jnp.mean(values * values, axis=-1, keepdims=True) + EPS_NORM)
    return (values * row_scale * norm_gain).astype(jnp.bfloat16)


def refresh(gradient, sample_grad, moment, curvature):
    moment_new = BETA_ONE * moment.astype(jnp.float32) + (1.0 - BETA_ONE) * gradient
    curvature_new = (
        BETA_TWO * curvature.astype(jnp.float32) + (1.0 - BETA_TWO) * sample_grad * sample_grad
    )
    update_direction = jnp.clip(moment_new / (RHO_SCALE * curvature_new), -1.0, 1.0)
    return (
        moment_new.astype(jnp.bfloat16),
        curvature_new.astype(jnp.bfloat16),
        update_direction.astype(jnp.bfloat16),
    )


def by_groups(hidden, norm_gain, input_ids, sampled_ids, head_weight, moment, curvature):
    normed = normalize(hidden, norm_gain)
    gathered = lax.all_gather(normed, "shard", axis=0, tiled=True)
    group_len = gathered.shape[0]
    columns = head_weight.shape[1]
    first_col = lax.axis_index("shard") * columns
    logits = jnp.dot(gathered, head_weight, preferred_element_type=jnp.float32)
    row_peak = lax.pmax(jnp.max(logits, axis=-1), "shard")
    scaled_exp = jnp.exp(logits - row_peak[:, None])
    row_sum = lax.psum(jnp.sum(scaled_exp, axis=-1), "shard")
    probabilities = (scaled_exp / row_sum[:, None]).astype(jnp.bfloat16)
    group_start = lax.axis_index("rep") * group_len
    token_ids = lax.dynamic_slice_in_dim(input_ids, group_start, group_len, 0)
    sample_ids = lax.dynamic_slice_in_dim(sampled_ids, group_start, group_len, 0)
    position = jnp.arange(group_len)
    shifted = jnp.roll(token_ids, -1) - first_col
    usable = (position < group_len - 1) & (shifted >= 0) & (shifted < columns)
    true_slot = jnp.where(usable, shifted, columns)
    sample_local = sample_ids - first_col
    inside = (sample_local >= 0) & (sample_local < columns)
    sample_slot = jnp.where(inside, sample_local, columns)
    shared = lax.dot_general(
        gathered, probabilities, (((0,), (0,)), ((), ())), preferred_element_type=jnp.float32
    )
    widened = gathered.astype(jnp.float32)
    true_sums = jax.ops.segment_sum(widened, true_slot, num_segments=columns + 1)[:columns]
    sample_sums = jax.ops.segment_sum(widened, sample_slot, num_segments=columns + 1)[:columns]
    true_part = (shared - true_sums.T).astype(jnp.bfloat16)
    sample_part = (shared - sample_sums.T).astype(jnp.bfloat16)
    gradient = lax.psum_scatter(true_part, "rep", scatter_dimension=0, tiled=True)
    sample_grad = lax.psum_scatter(sample_part, "rep", scatter_dimension=0, tiled=True)
    return refresh(
        gradient.astype(jnp.float32), sample_grad.astype(jnp.float32), moment, curvature
    )


def swap_pairs(count, bit):
    return [(index, index ^ bit) for index in range(count)]


def shift_pairs(lines, along, across):
    pairs = []
    for place in range(lines):
        for side in range(2):
            source = 2 * place + side
            pairs.append((source, 2 * ((place + along) % lines) + (side ^ across)))
    return pairs


def logits_kernel(start, sizes, *refs):
    block_refs, refs = refs[:len(sizes)], refs[len(sizes):]
    weight_ref, before_ref, exp_ref, stats_ref, tokens, logits, highs, sums = refs
    step = pl.program_id(0)
    count, columns = logits.shape
    width = weight_ref.shape[1]
    shift = start % 128
    half = stats_ref.shape[0] // 2

    @pl.when(step == 0)
    def _():
        place = 0
        for size, ref in zip(sizes, block_refs):
            tokens[place:place + size] = ref[...]
            place += size
        highs[...] = jnp.full(highs.shape, -jnp.inf, jnp.float32)

    tile = jnp.dot(tokens[...], weight_ref[...], preferred_element_type=jnp.float32)
    logits[:, pl.ds(pl.multiple_of(step * width, 128), width)] = tile
    high = functools.reduce(
        jnp.maximum, [tile[:, lane:lane + 128] for lane in range(0, width, 128)]
    )
    highs[shift:shift + count] = jnp.maximum(highs[shift:shift + count], high)

    @pl.when(step == pl.num_programs(0) - 1)
    def _():
        highs[...] = jnp.broadcast_to(jnp.max(highs[...], axis=1, keepdims=True), highs.shape)
        chunk = 16

        def body(index, carry):
            place = pl.ds(pl.multiple_of(index * chunk, chunk), chunk)
            outer = pl.ds(pl.multiple_of(shift + index * chunk, chunk), chunk)
            peak = highs[outer, :]
            total = jnp.zeros((chunk, 128), jnp.float32)
            for lane in range(0, columns, 128):
                scaled = jnp.exp(logits[place, lane:lane + 128] - peak)
                exp_ref[place, lane:lane + 128] = scaled.astype(jnp.bfloat16)
                total += scaled
            sums[outer, :] = total
            return carry

        lax.fori_loop(0, count // chunk, body, 0, unroll=2)
        totals = jnp.broadcast_to(jnp.sum(sums[...], axis=1, keepdims=True), sums.shape)
        stats_ref[...] = before_ref[...]
        for base, rows in ((0, highs[...].T[0:1]), (half, totals.T[0:1])):
            for lane in range(shift, shift + count, 64):
                row = base + (start - shift + lane) // 128
                inner = lane % 128
                stats_ref[row:row + 1, inner:inner + 64] = rows[:, lane:lane + 64]


def round_logits(start, blocks, head_weight, before):
    depth, columns = head_weight.shape
    sizes = [block.shape[0] for block in blocks]
    count = sum(sizes)
    width = min(256, columns)
    spread = -(-(start % 128 + count) // 128) * 128
    whole = lambda array: pl.BlockSpec(array.shape, lambda step: (0, 0))
    return pl.pallas_call(
        functools.partial(logits_kernel, start, sizes),
        grid=(columns // width,),
        in_specs=[whole(block) for block in blocks]
        + [pl.BlockSpec((depth, width), lambda step: (0, step)), whole(before)],
        out_specs=[pl.BlockSpec((count, columns), lambda step: (0, 0)), whole(before)],
        out_shape=[
            jax.ShapeDtypeStruct((count, columns), jnp.bfloat16),
            jax.ShapeDtypeStruct(before.shape, jnp.float32),
        ],
        scratch_shapes=[
            pltpu.VMEM((count, depth), jnp.bfloat16),
            pltpu.VMEM((count, columns), jnp.float32),
            pltpu.VMEM((spread, 128), jnp.float32),
            pltpu.VMEM((spread, 128), jnp.float32),
        ],
        compiler_params=pltpu.CompilerParams(vmem_limit_bytes=40 * 1024 * 1024),
        cost_estimate=pl.CostEstimate(
            flops=2 * count * depth * columns,
            bytes_accessed=2 * depth * columns,
            transcendentals=count * columns,
        ),
        name="round_logits",
    )(*blocks, head_weight, before)


def turn_kernel(sizes, rep_ref, *refs):
    block_refs = refs[:len(sizes)]
    mine_ref, other_ref, tokens = refs[len(sizes):]
    step = pl.program_id(0)
    place = 0
    for size, ref in zip(sizes, block_refs):
        tokens[place:place + size] = ref[...]
        place += size
    turned = tokens[...].T

    @pl.when(step == 0)
    def _():
        mine_ref[...] = turned

    @pl.when(step == 1)
    def _():
        other_ref[...] = turned


def turned_features(rep, blocks, rows):
    sizes = [block.shape[0] for block in blocks]
    count = sum(sizes)
    whole = pl.BlockSpec((rows, count), lambda step, rep_ref: (0, 0))
    return pl.pallas_call(
        functools.partial(turn_kernel, sizes),
        grid_spec=pltpu.PrefetchScalarGridSpec(
            num_scalar_prefetch=1,
            grid=(2,),
            in_specs=[
                pl.BlockSpec((size, rows), lambda step, rep_ref: (0, rep_ref[0] ^ step))
                for size in sizes
            ],
            out_specs=[whole, whole],
            scratch_shapes=[pltpu.VMEM((count, rows), jnp.bfloat16)],
        ),
        out_shape=[jax.ShapeDtypeStruct((rows, count), jnp.bfloat16)] * 2,
        compiler_params=pltpu.CompilerParams(vmem_limit_bytes=24 * 1024 * 1024),
        cost_estimate=pl.CostEstimate(
            flops=0, bytes_accessed=8 * rows * count, transcendentals=0
        ),
        name="turned_features",
    )(rep, *blocks)


def one_hot_kernel(count, *refs):
    feature_refs, refs = refs[:count], refs[count:]
    (true_ref, sample_ref), refs = refs[:2], refs[2:]
    before_refs, refs = refs[:-3], refs[-3:]
    true_out, sample_out, features = refs
    step = pl.program_id(0)
    width = true_out.shape[1]
    part = feature_refs[0].shape[1]

    @pl.when(step == 0)
    def _():
        for index, ref in enumerate(feature_refs):
            features[:, index * part:(index + 1) * part] = ref[...]

    tokens = part * count
    columns = step * width + lax.broadcasted_iota(jnp.int32, (width, tokens), 0)
    for index, (ids_ref, out_ref) in enumerate(((true_ref, true_out), (sample_ref, sample_out))):
        hot = (columns == ids_ref[...]).astype(jnp.float32).astype(jnp.bfloat16)
        total = lax.dot_general(
            features[...], hot, (((1,), (1,)), ((), ())), preferred_element_type=jnp.float32
        )
        if before_refs:
            total += before_refs[index][...].astype(jnp.float32)
        out_ref[...] = total.astype(jnp.bfloat16)


def one_hot_sums(features, ids, columns, before=()):
    rows, part = features[0].shape
    tokens = part * len(features)
    width = min(256, columns)
    whole = lambda array: pl.BlockSpec(array.shape, lambda step: (0, 0))
    tile = pl.BlockSpec((rows, width), lambda step: (0, step))
    return pl.pallas_call(
        functools.partial(one_hot_kernel, len(features)),
        grid=(columns // width,),
        in_specs=[whole(array) for array in (*features, *ids)] + [tile] * len(before),
        out_specs=[tile, tile],
        out_shape=[jax.ShapeDtypeStruct((rows, columns), jnp.bfloat16)] * 2,
        scratch_shapes=[pltpu.VMEM((rows, tokens), jnp.bfloat16)],
        compiler_params=pltpu.CompilerParams(vmem_limit_bytes=24 * 1024 * 1024),
        cost_estimate=pl.CostEstimate(
            flops=4 * rows * tokens * columns,
            bytes_accessed=2 * rows * (tokens + 2 * columns),
            transcendentals=0,
        ),
        name="one_hot_sums",
    )(*features, *ids, *before)


def refresh_kernel(lines, counts, *refs):
    feature_refs, refs = refs[:counts[0]], refs[counts[0]:]
    exp_refs, refs = refs[:counts[1]], refs[counts[1]:]
    stats_refs, refs = refs[:lines], refs[lines:]
    (true_sum, sample_sum, moment_ref, curvature_ref,
     moment_out, curvature_out, update_out, scaled) = refs
    step = pl.program_id(0)
    part = feature_refs[0].shape[1]

    @pl.when(step == 0)
    def _():
        rows = 4 * lines
        peaks = [ref[0:rows] for ref in stats_refs]
        totals = [ref[rows:2 * rows] for ref in stats_refs]
        own_peaks = stats_refs[0][2 * rows:]
        for core in range(2):
            for turn in range(lines):
                for side in range(2):
                    row = (core * lines + turn) * 2 + side
                    away = [
                        (core * lines + (turn + along) % lines) * 2 + side for along in range(lines)
                    ]
                    near = [values[index:index + 1] for values, index in zip(peaks, away)]
                    parts = [values[index:index + 1] for values, index in zip(totals, away)]
                    peak = functools.reduce(jnp.maximum, near)
                    total = sum(t * jnp.exp(p - peak) for p, t in zip(near, parts))
                    factor = jnp.exp(own_peaks[row:row + 1] - peak) / total
                    place = row * 128
                    ref = feature_refs[place // part]
                    inner = place % part
                    values = ref[:, inner:inner + 128].astype(jnp.float32)
                    scaled[:, place:place + 128] = (values * factor).astype(jnp.bfloat16)

    exps = jnp.concatenate([ref[...] for ref in exp_refs], axis=0)
    shared = jnp.dot(scaled[...], exps, preferred_element_type=jnp.float32)
    moment_out[...], curvature_out[...], update_out[...] = refresh(
        shared - true_sum[...].astype(jnp.float32),
        shared - sample_sum[...].astype(jnp.float32),
        moment_ref[...],
        curvature_ref[...],
    )


def refresh_states(lines, features, exps, stats, sums, moment, curvature):
    rows, columns = moment.shape
    tokens = sum(array.shape[1] for array in features)
    width = min(256, columns)
    whole = lambda array: pl.BlockSpec(array.shape, lambda step: (0, 0))
    tile = pl.BlockSpec((rows, width), lambda step: (0, step))
    return pl.pallas_call(
        functools.partial(refresh_kernel, lines, (len(features), len(exps))),
        grid=(columns // width,),
        in_specs=[whole(array) for array in features]
        + [pl.BlockSpec((array.shape[0], width), lambda step: (0, step)) for array in exps]
        + [whole(array) for array in stats]
        + [tile] * 4,
        out_specs=[tile] * 3,
        out_shape=[jax.ShapeDtypeStruct((rows, columns), jnp.bfloat16)] * 3,
        scratch_shapes=[pltpu.VMEM((rows, tokens), jnp.bfloat16)],
        compiler_params=pltpu.CompilerParams(vmem_limit_bytes=32 * 1024 * 1024),
        cost_estimate=pl.CostEstimate(
            flops=2 * rows * columns * tokens,
            bytes_accessed=2 * (rows * tokens + tokens * columns + 7 * rows * columns),
            transcendentals=0,
        ),
        name="refresh_states",
    )(*features, *exps, *stats, *sums, moment, curvature)


def merge_kernel(own_ref, across_ref, core_ref, both_ref, merged_ref):
    rows = own_ref.shape[0] // 2
    for core, (near, far) in enumerate(((own_ref, across_ref), (core_ref, both_ref))):
        for row in range(rows):
            place = core * rows + row
            other = row ^ 1
            first, second = near[row:row + 1], far[other:other + 1]
            peak = jnp.maximum(first, second)
            total = near[rows + row:rows + row + 1] * jnp.exp(first - peak)
            total += far[rows + other:rows + other + 1] * jnp.exp(second - peak)
            merged_ref[place:place + 1] = peak
            merged_ref[2 * rows + place:2 * rows + place + 1] = total
            merged_ref[4 * rows + place:4 * rows + place + 1] = first


def merged_stats(own, across, core, both):
    rows, lanes = own.shape
    return pl.pallas_call(
        merge_kernel,
        out_shape=jax.ShapeDtypeStruct((3 * rows, lanes), jnp.float32),
        name="merged_stats",
    )(own, across, core, both)


def after(value, *others):
    return lax.optimization_barrier((value, *others))[0]


def all_tokens(reps, shards, hidden, norm_gain, input_ids, sampled_ids, head_weight, moment, curvature):
    lines = shards // 2
    length = hidden.shape[0]
    half = length // 2
    rows, columns = moment.shape
    rep = lax.axis_index("rep")
    shard = lax.axis_index("shard")
    first_col = shard * columns
    group_len = length * shards

    def to_x(values):
        return lax.ppermute(values, "rep", swap_pairs(reps, 2))

    def to_core(values):
        return lax.ppermute(values, "rep", swap_pairs(reps, 1))

    def to_y(values):
        return lax.ppermute(values, "shard", swap_pairs(shards, 1))

    def to_y_core(values):
        pairs = [
            (rep_at * shards + at, (rep_at ^ 1) * shards + (at ^ 1))
            for rep_at in range(reps) for at in range(shards)
        ]
        return lax.ppermute(values, ("rep", "shard"), pairs)

    normed = normalize(hidden, norm_gain)

    core, turn, side, across = np.meshgrid(
        np.arange(2), np.arange(lines), np.arange(2), np.arange(2), indexing="ij"
    )
    holder = (rep ^ (2 * across + core)).reshape(-1)
    place = (2 * ((shard // 2 - turn) % lines) + ((shard % 2) ^ side)).reshape(-1)
    order = holder * shards + place
    last = jnp.arange(input_ids.shape[0]) % group_len == group_len - 1
    targets = jnp.where(last, -1, jnp.roll(input_ids, -1) - first_col)
    ids = jnp.stack([targets, sampled_ids - first_col]).reshape(2, reps * shards, length)
    ids = jnp.take(ids, order, axis=1).reshape(2, 2, lines, 4 * length)
    split = lines // 2
    early_ids = ids[:, :, :split].reshape(2, 1, -1)
    late_ids = ids[:, :, split:].reshape(2, 1, -1)

    rep_scalar = rep.astype(jnp.int32).reshape(1)
    stats = jnp.zeros((4 * lines, 128), jnp.float32)
    block, waiting, start = normed, [], 0
    quads, exps, other_exps, early, sums = [], [], [], None, None
    for turn in range(lines):
        final = turn + 1 == lines
        if turn > 1:
            block = after(block, exps[turn - 2])
        from_x = to_x(block)
        from_y = to_y(block)
        following = None
        if not final:
            following = lax.ppermute(block, "shard", shift_pairs(lines, 1, 0))
        if exps:
            from_x, from_y = lax.optimization_barrier((from_x, from_y, exps[-1], *waiting))[:2]
        first = to_x(from_y[:half])
        second = to_y(from_x[half:])
        quads.append([block, from_x, from_y, first, second])
        blocks = waiting + [block, from_x, from_y]
        gates = [following]
        if final:
            blocks = blocks + [first, second]
            gates = [*sums, *other_exps]
        if turn == split:
            turns = sum(quads[:split], [])
            turns[0] = after(turns[0], exps[-1], following)
            early = turned_features(rep_scalar, turns, rows)
            gates.append(early[0])
        blocks[0] = after(blocks[0], *gates)
        exp, stats = round_logits(start, blocks, head_weight, stats)
        exps.append(exp)
        start += exp.shape[0]
        if turn == split:
            early = [early[0], to_core(early[1])]
            early_ids = [after(early_ids[0], exp), early_ids[1]]
            sums = one_hot_sums(early, early_ids, columns)
        if turn + 2 == lines:
            other_exps = [to_core(after(early_exp, exp)) for early_exp in exps[:-1]]
        waiting = [first, second]
        block = following

    across_stats, core_stats, both_stats = to_y(stats), to_core(stats), to_y_core(stats)
    late_blocks = sum(quads[split:], [])
    late_blocks[0] = after(late_blocks[0], stats)
    late = turned_features(rep_scalar, late_blocks, rows)
    merged = merged_stats(stats, across_stats, core_stats, both_stats)
    all_stats = [merged] + [
        lax.ppermute(merged, "shard", shift_pairs(lines, -along, 0)) for along in range(1, lines)
    ]
    late_exps = lax.optimization_barrier((late[1], *exps[-2:], merged))
    other_exps += [to_core(exp) for exp in late_exps[1:3]]
    late = [late[0], to_core(late_exps[0])]
    sums = one_hot_sums(late, late_ids, columns, sums)
    return tuple(refresh_states(
        lines, [early[0], late[0], early[1], late[1]], exps + other_exps,
        all_stats, sums, moment, curvature,
    ))


def solution(mesh):
    in_specs = (
        P(("rep", "shard"), None),
        P(),
        P(),
        P(),
        P(None, "shard"),
        P("rep", "shard"),
        P("rep", "shard"),
    )
    out_specs = (P("rep", "shard"), P("rep", "shard"), P("rep", "shard"))
    reps, shards = mesh.shape["rep"], mesh.shape["shard"]

    def whole(hidden, *others):
        tokens, depth = hidden.shape
        length = tokens // (reps * shards)
        fits = hidden.size * 2 <= GATHER_BYTES and reps == 4 and shards % 2 == 0
        if fits and length == 64 and (depth // reps) % 128 == 0:
            plan = functools.partial(all_tokens, reps, shards)
        else:
            plan = by_groups

        return jax.shard_map(
            plan, mesh=mesh, in_specs=in_specs, out_specs=out_specs, check_vma=False
        )(hidden, *others)

    return whole
```

```python
import functools

import jax
import jax.numpy as jnp
import numpy as np
from jax import lax
from jax.experimental import pallas as pl
from jax.experimental.pallas import tpu as pltpu
from jax.sharding import PartitionSpec as P

EPS_NORM = 1e-05
BETA_ONE = 0.96
BETA_TWO = 0.95
RHO_SCALE = 0.05
GATHER_BYTES = 32 * 1024 * 1024
BANDS = 4
BRIEF = pl.CostEstimate(flops=1024, bytes_accessed=1024, transcendentals=0)


def normalize(hidden, norm_gain):
    values = hidden.astype(jnp.float32)
    row_scale = lax.rsqrt(jnp.mean(values * values, axis=-1, keepdims=True) + EPS_NORM)
    return (values * row_scale * norm_gain).astype(jnp.bfloat16)


def refresh(gradient, sample_grad, moment, curvature):
    moment_new = BETA_ONE * moment.astype(jnp.float32) + (1.0 - BETA_ONE) * gradient
    curvature_new = (
        BETA_TWO * curvature.astype(jnp.float32) + (1.0 - BETA_TWO) * sample_grad * sample_grad
    )
    update_direction = jnp.clip(moment_new / (RHO_SCALE * curvature_new), -1.0, 1.0)
    return (
        moment_new.astype(jnp.bfloat16),
        curvature_new.astype(jnp.bfloat16),
        update_direction.astype(jnp.bfloat16),
    )


def by_groups(hidden, norm_gain, input_ids, sampled_ids, head_weight, moment, curvature):
    normed = normalize(hidden, norm_gain)
    gathered = lax.all_gather(normed, "shard", axis=0, tiled=True)
    group_len = gathered.shape[0]
    columns = head_weight.shape[1]
    first_col = lax.axis_index("shard") * columns
    logits = jnp.dot(gathered, head_weight, preferred_element_type=jnp.float32)
    row_peak = lax.pmax(jnp.max(logits, axis=-1), "shard")
    scaled_exp = jnp.exp(logits - row_peak[:, None])
    row_sum = lax.psum(jnp.sum(scaled_exp, axis=-1), "shard")
    probabilities = (scaled_exp / row_sum[:, None]).astype(jnp.bfloat16)
    group_start = lax.axis_index("rep") * group_len
    token_ids = lax.dynamic_slice_in_dim(input_ids, group_start, group_len, 0)
    sample_ids = lax.dynamic_slice_in_dim(sampled_ids, group_start, group_len, 0)
    position = jnp.arange(group_len)
    shifted = jnp.roll(token_ids, -1) - first_col
    usable = (position < group_len - 1) & (shifted >= 0) & (shifted < columns)
    true_slot = jnp.where(usable, shifted, columns)
    sample_local = sample_ids - first_col
    inside = (sample_local >= 0) & (sample_local < columns)
    sample_slot = jnp.where(inside, sample_local, columns)
    shared = lax.dot_general(
        gathered, probabilities, (((0,), (0,)), ((), ())), preferred_element_type=jnp.float32
    )
    widened = gathered.astype(jnp.float32)
    true_sums = jax.ops.segment_sum(widened, true_slot, num_segments=columns + 1)[:columns]
    sample_sums = jax.ops.segment_sum(widened, sample_slot, num_segments=columns + 1)[:columns]
    true_part = (shared - true_sums.T).astype(jnp.bfloat16)
    sample_part = (shared - sample_sums.T).astype(jnp.bfloat16)
    gradient = lax.psum_scatter(true_part, "rep", scatter_dimension=0, tiled=True)
    sample_grad = lax.psum_scatter(sample_part, "rep", scatter_dimension=0, tiled=True)
    return refresh(
        gradient.astype(jnp.float32), sample_grad.astype(jnp.float32), moment, curvature
    )


def swap_pairs(count, bit):
    return [(index, index ^ bit) for index in range(count)]


def shift_pairs(lines, along, across):
    pairs = []
    for place in range(lines):
        for side in range(2):
            source = 2 * place + side
            pairs.append((source, 2 * ((place + along) % lines) + (side ^ across)))
    return pairs


def logits_kernel(start, sizes, *refs):
    block_refs, refs = refs[:len(sizes)], refs[len(sizes):]
    weight_refs, refs = refs[:BANDS], refs[BANDS:]
    before_ref, exp_ref, stats_ref, tokens, logits, highs, sums = refs
    step = pl.program_id(0)
    count, columns = logits.shape
    depth, width = weight_refs[0].shape
    shift = start % 128
    half = stats_ref.shape[0] // 2

    @pl.when(step == 0)
    def _():
        place = 0
        for size, ref in zip(sizes, block_refs):
            tokens[place:place + size] = ref[...]
            place += size
        highs[...] = jnp.full(highs.shape, -jnp.inf, jnp.float32)

    tile = sum(
        jnp.dot(
            tokens[:, band * depth:(band + 1) * depth], ref[...],
            preferred_element_type=jnp.float32,
        )
        for band, ref in enumerate(weight_refs)
    )
    logits[:, pl.ds(pl.multiple_of(step * width, 128), width)] = tile
    high = functools.reduce(
        jnp.maximum, [tile[:, lane:lane + 128] for lane in range(0, width, 128)]
    )
    highs[shift:shift + count] = jnp.maximum(highs[shift:shift + count], high)

    @pl.when(step == pl.num_programs(0) - 1)
    def _():
        highs[...] = jnp.broadcast_to(jnp.max(highs[...], axis=1, keepdims=True), highs.shape)
        chunk = 16

        def body(index, carry):
            place = pl.ds(pl.multiple_of(index * chunk, chunk), chunk)
            outer = pl.ds(pl.multiple_of(shift + index * chunk, chunk), chunk)
            peak = highs[outer, :]
            total = jnp.zeros((chunk, 128), jnp.float32)
            for lane in range(0, columns, 128):
                scaled = jnp.exp(logits[place, lane:lane + 128] - peak)
                exp_ref[place, lane:lane + 128] = scaled.astype(jnp.bfloat16)
                total += scaled
            sums[outer, :] = total
            return carry

        lax.fori_loop(0, count // chunk, body, 0, unroll=2)
        totals = jnp.broadcast_to(jnp.sum(sums[...], axis=1, keepdims=True), sums.shape)
        stats_ref[...] = before_ref[...]
        for base, rows in ((0, highs[...].T[0:1]), (half, totals.T[0:1])):
            for lane in range(shift, shift + count, 64):
                row = base + (start - shift + lane) // 128
                inner = lane % 128
                stats_ref[row:row + 1, inner:inner + 64] = rows[:, lane:lane + 64]


def round_logits(start, blocks, head_weight, before):
    depth, columns = head_weight.shape
    sizes = [block.shape[0] for block in blocks]
    count = sum(sizes)
    width = min(256, columns)
    spread = -(-(start % 128 + count) // 128) * 128
    whole = lambda array: pl.BlockSpec(array.shape, lambda step: (0, 0))
    return pl.pallas_call(
        functools.partial(logits_kernel, start, sizes),
        grid=(columns // width,),
        in_specs=[whole(block) for block in blocks]
        + [
            pl.BlockSpec((depth // BANDS, width), lambda step, band=band: (band, step))
            for band in range(BANDS)
        ]
        + [whole(before)],
        out_specs=[pl.BlockSpec((count, columns), lambda step: (0, 0)), whole(before)],
        out_shape=[
            jax.ShapeDtypeStruct((count, columns), jnp.bfloat16),
            jax.ShapeDtypeStruct(before.shape, jnp.float32),
        ],
        scratch_shapes=[
            pltpu.VMEM((count, depth), jnp.bfloat16),
            pltpu.VMEM((count, columns), jnp.float32),
            pltpu.VMEM((spread, 128), jnp.float32),
            pltpu.VMEM((spread, 128), jnp.float32),
        ],
        compiler_params=pltpu.CompilerParams(vmem_limit_bytes=26 * 1024 * 1024),
        cost_estimate=BRIEF,
        name="round_logits",
    )(*blocks, *[head_weight] * BANDS, before)


def turn_kernel(sizes, rep_ref, *refs):
    block_refs = refs[:len(sizes)]
    mine_ref, other_ref, tokens = refs[len(sizes):]
    step = pl.program_id(0)
    place = 0
    for size, ref in zip(sizes, block_refs):
        tokens[place:place + size] = ref[...]
        place += size
    turned = tokens[...].T

    @pl.when(step == 0)
    def _():
        mine_ref[...] = turned

    @pl.when(step == 1)
    def _():
        other_ref[...] = turned


def turned_features(rep, blocks, rows):
    sizes = [block.shape[0] for block in blocks]
    count = sum(sizes)
    whole = pl.BlockSpec((rows, count), lambda step, rep_ref: (0, 0))
    return pl.pallas_call(
        functools.partial(turn_kernel, sizes),
        grid_spec=pltpu.PrefetchScalarGridSpec(
            num_scalar_prefetch=1,
            grid=(2,),
            in_specs=[
                pl.BlockSpec((size, rows), lambda step, rep_ref: (0, rep_ref[0] ^ step))
                for size in sizes
            ],
            out_specs=[whole, whole],
            scratch_shapes=[pltpu.VMEM((count, rows), jnp.bfloat16)],
        ),
        out_shape=[jax.ShapeDtypeStruct((rows, count), jnp.bfloat16)] * 2,
        compiler_params=pltpu.CompilerParams(vmem_limit_bytes=24 * 1024 * 1024),
        cost_estimate=BRIEF,
        name="turned_features",
    )(rep, *blocks)


def one_hot_kernel(count, *refs):
    feature_refs, refs = refs[:count], refs[count:]
    (true_ref, sample_ref), refs = refs[:2], refs[2:]
    before_refs, refs = refs[:-3], refs[-3:]
    true_out, sample_out, features = refs
    step = pl.program_id(0)
    width = true_out.shape[1]
    part = feature_refs[0].shape[1]

    @pl.when(step == 0)
    def _():
        for index, ref in enumerate(feature_refs):
            features[:, index * part:(index + 1) * part] = ref[...]

    tokens = part * count
    columns = step * width + lax.broadcasted_iota(jnp.int32, (width, tokens), 0)
    hot = jnp.concatenate([columns == true_ref[...], columns == sample_ref[...]], axis=0)
    totals = lax.dot_general(
        features[...], hot.astype(jnp.float32).astype(jnp.bfloat16),
        (((1,), (1,)), ((), ())), preferred_element_type=jnp.float32,
    )
    for index, out_ref in enumerate((true_out, sample_out)):
        total = totals[:, index * width:(index + 1) * width]
        if before_refs:
            total += before_refs[index][...].astype(jnp.float32)
        out_ref[...] = total.astype(jnp.bfloat16)


def one_hot_sums(features, ids, columns, before=()):
    rows, part = features[0].shape
    tokens = part * len(features)
    width = min(256, columns)
    whole = lambda array: pl.BlockSpec(array.shape, lambda step: (0, 0))
    tile = pl.BlockSpec((rows, width), lambda step: (0, step))
    return pl.pallas_call(
        functools.partial(one_hot_kernel, len(features)),
        grid=(columns // width,),
        in_specs=[whole(array) for array in (*features, *ids)] + [tile] * len(before),
        out_specs=[tile, tile],
        out_shape=[jax.ShapeDtypeStruct((rows, columns), jnp.bfloat16)] * 2,
        scratch_shapes=[pltpu.VMEM((rows, tokens), jnp.bfloat16)],
        compiler_params=pltpu.CompilerParams(vmem_limit_bytes=24 * 1024 * 1024),
        cost_estimate=BRIEF,
        name="one_hot_sums",
    )(*features, *ids, *before)


def refresh_kernel(lines, counts, *refs):
    feature_refs, refs = refs[:counts[0]], refs[counts[0]:]
    exp_refs, refs = refs[:counts[1]], refs[counts[1]:]
    stats_refs, refs = refs[:lines], refs[lines:]
    (true_sum, sample_sum, moment_ref, curvature_ref,
     moment_out, curvature_out, update_out, scaled) = refs
    step = pl.program_id(0)
    part = feature_refs[0].shape[1]

    @pl.when(step == 0)
    def _():
        rows = 4 * lines
        peaks = [ref[0:rows] for ref in stats_refs]
        totals = [ref[rows:2 * rows] for ref in stats_refs]
        own_peaks = stats_refs[0][2 * rows:]
        for core in range(2):
            for turn in range(lines):
                for side in range(2):
                    row = (core * lines + turn) * 2 + side
                    away = [
                        (core * lines + (turn + along) % lines) * 2 + side for along in range(lines)
                    ]
                    near = [values[index:index + 1] for values, index in zip(peaks, away)]
                    parts = [values[index:index + 1] for values, index in zip(totals, away)]
                    peak = functools.reduce(jnp.maximum, near)
                    total = sum(t * jnp.exp(p - peak) for p, t in zip(near, parts))
                    factor = jnp.exp(own_peaks[row:row + 1] - peak) / total
                    place = row * 128
                    ref = feature_refs[place // part]
                    inner = place % part
                    values = ref[:, inner:inner + 128].astype(jnp.float32)
                    scaled[:, place:place + 128] = (values * factor).astype(jnp.bfloat16)

    exps = jnp.concatenate([ref[...] for ref in exp_refs], axis=0)
    shared = jnp.dot(scaled[...], exps, preferred_element_type=jnp.float32)
    moment_out[...], curvature_out[...], update_out[...] = refresh(
        shared - true_sum[...].astype(jnp.float32),
        shared - sample_sum[...].astype(jnp.float32),
        moment_ref[...],
        curvature_ref[...],
    )


def refresh_states(lines, features, exps, stats, sums, moment, curvature):
    rows, columns = moment.shape
    tokens = sum(array.shape[1] for array in features)
    width = min(256, columns)
    whole = lambda array: pl.BlockSpec(array.shape, lambda step: (0, 0))
    tile = pl.BlockSpec((rows, width), lambda step: (0, step))
    return pl.pallas_call(
        functools.partial(refresh_kernel, lines, (len(features), len(exps))),
        grid=(columns // width,),
        in_specs=[whole(array) for array in features]
        + [pl.BlockSpec((array.shape[0], width), lambda step: (0, step)) for array in exps]
        + [whole(array) for array in stats]
        + [tile] * 4,
        out_specs=[tile] * 3,
        out_shape=[jax.ShapeDtypeStruct((rows, columns), jnp.bfloat16)] * 3,
        scratch_shapes=[pltpu.VMEM((rows, tokens), jnp.bfloat16)],
        compiler_params=pltpu.CompilerParams(vmem_limit_bytes=32 * 1024 * 1024),
        cost_estimate=BRIEF,
        name="refresh_states",
    )(*features, *exps, *stats, *sums, moment, curvature)


def merge_kernel(own_ref, across_ref, core_ref, both_ref, merged_ref):
    rows = own_ref.shape[0] // 2
    for core, (near, far) in enumerate(((own_ref, across_ref), (core_ref, both_ref))):
        for row in range(rows):
            place = core * rows + row
            other = row ^ 1
            first, second = near[row:row + 1], far[other:other + 1]
            peak = jnp.maximum(first, second)
            total = near[rows + row:rows + row + 1] * jnp.exp(first - peak)
            total += far[rows + other:rows + other + 1] * jnp.exp(second - peak)
            merged_ref[place:place + 1] = peak
            merged_ref[2 * rows + place:2 * rows + place + 1] = total
            merged_ref[4 * rows + place:4 * rows + place + 1] = first


def merged_stats(own, across, core, both):
    rows, lanes = own.shape
    return pl.pallas_call(
        merge_kernel,
        out_shape=jax.ShapeDtypeStruct((3 * rows, lanes), jnp.float32),
        name="merged_stats",
    )(own, across, core, both)


def after(value, *others):
    return lax.optimization_barrier((value, *others))[0]


def all_tokens(reps, shards, hidden, norm_gain, input_ids, sampled_ids, head_weight, moment, curvature):
    lines = shards // 2
    length = hidden.shape[0]
    half = length // 2
    rows, columns = moment.shape
    rep = lax.axis_index("rep")
    shard = lax.axis_index("shard")
    first_col = shard * columns
    group_len = length * shards

    def to_x(values):
        return lax.ppermute(values, "rep", swap_pairs(reps, 2))

    def to_core(values):
        return lax.ppermute(values, "rep", swap_pairs(reps, 1))

    def to_y(values):
        return lax.ppermute(values, "shard", swap_pairs(shards, 1))

    def to_y_core(values):
        pairs = [
            (rep_at * shards + at, (rep_at ^ 1) * shards + (at ^ 1))
            for rep_at in range(reps) for at in range(shards)
        ]
        return lax.ppermute(values, ("rep", "shard"), pairs)

    normed = normalize(hidden, norm_gain)

    core, turn, side, across = np.meshgrid(
        np.arange(2), np.arange(lines), np.arange(2), np.arange(2), indexing="ij"
    )
    holder = (rep ^ (2 * across + core)).reshape(-1)
    place = (2 * ((shard // 2 - turn) % lines) + ((shard % 2) ^ side)).reshape(-1)
    order = holder * shards + place
    last = jnp.arange(input_ids.shape[0]) % group_len == group_len - 1
    targets = jnp.where(last, -1, jnp.roll(input_ids, -1) - first_col)
    ids = jnp.stack([targets, sampled_ids - first_col]).reshape(2, reps * shards, length)
    ids = jnp.take(ids, order, axis=1).reshape(2, 2, lines, 4 * length)
    split = lines // 2
    early_ids = ids[:, :, :split].reshape(2, 1, -1)
    late_ids = ids[:, :, split:].reshape(2, 1, -1)

    rep_scalar = rep.astype(jnp.int32).reshape(1)
    head_weight = pltpu.with_memory_space_constraint(head_weight, pltpu.HBM)
    stats = jnp.zeros((4 * lines, 128), jnp.float32)
    block, start = normed, 0
    quads, waiting, exps, done = [], [], [], []
    for turn in range(lines):
        final = turn + 1 == lines
        from_x = to_x(block)
        from_y = to_y(block)
        following = None
        if not final:
            following = lax.ppermute(block, "shard", shift_pairs(lines, 1, 0))
        if turn > 0:
            gates = (*done, *exps[-1:])
            from_x, from_y = lax.optimization_barrier((from_x, from_y, *gates))[:2]
        first = to_x(from_y[:half])
        second = to_y(from_x[half:])
        done = [first, second]
        quads.append([block, from_x, from_y, first, second])
        waiting = waiting + [block, from_x, from_y]
        block = following
        if turn + 1 < split:
            waiting = waiting + done
            continue
        gates = [] if final else [following]
        if final:
            waiting = waiting + done
            turns = sum(quads[split:], [])
            turns[0] = after(turns[0], *sums)
            late = turned_features(rep_scalar, turns, rows)
            gates = [late[1]]
            held = lax.optimization_barrier((*exps, late[0]))
            other_exps = [to_core(exp) for exp in held[:-1]]
            late = [late[0], to_core(late[1])]
        if turn == split:
            early = turned_features(rep_scalar, sum(quads[:split], []), rows)
            gates.append(early[1])
        waiting[0] = after(waiting[0], *gates)
        exp, stats = round_logits(start, waiting, head_weight, stats)
        exps.append(exp)
        start += exp.shape[0]
        if turn == split:
            early = [early[0], to_core(early[1])]
            early_ids = [after(early_ids[0], exp), early_ids[1]]
            sums = one_hot_sums(early, early_ids, columns)
        waiting = done

    stats = after(stats, late[1], *other_exps)
    across_stats, core_stats, both_stats = to_y(stats), to_core(stats), to_y_core(stats)
    merged = merged_stats(stats, across_stats, core_stats, both_stats)
    all_stats = [merged] + [
        lax.ppermute(merged, "shard", shift_pairs(lines, -along, 0)) for along in range(1, lines)
    ]
    held = lax.optimization_barrier((late_ids[0], exps[-1], merged))
    other_exps.append(to_core(held[1]))
    sums = one_hot_sums(late, [held[0], late_ids[1]], columns, sums)
    return tuple(refresh_states(
        lines, [early[0], late[0], early[1], late[1]], exps + other_exps,
        all_stats, sums, moment, curvature,
    ))


def solution(mesh):
    in_specs = (
        P(("rep", "shard"), None),
        P(),
        P(),
        P(),
        P(None, "shard"),
        P("rep", "shard"),
        P("rep", "shard"),
    )
    out_specs = (P("rep", "shard"), P("rep", "shard"), P("rep", "shard"))
    reps, shards = mesh.shape["rep"], mesh.shape["shard"]

    def whole(hidden, *others):
        tokens, depth = hidden.shape
        length = tokens // (reps * shards)
        fits = hidden.size * 2 <= GATHER_BYTES and reps == 4 and shards % 2 == 0
        if fits and length == 64 and (depth // reps) % 128 == 0:
            plan = functools.partial(all_tokens, reps, shards)
        else:
            plan = by_groups

        return jax.shard_map(
            plan, mesh=mesh, in_specs=in_specs, out_specs=out_specs, check_vma=False
        )(hidden, *others)

    return whole
```

```python
import functools

import jax
import jax.numpy as jnp
import numpy as np
from jax import lax
from jax.experimental import pallas as pl
from jax.experimental.pallas import tpu as pltpu
from jax.sharding import PartitionSpec as P

EPS_NORM = 1e-05
BETA_ONE = 0.96
BETA_TWO = 0.95
RHO_SCALE = 0.05
GATHER_BYTES = 32 * 1024 * 1024
BRIEF = pl.CostEstimate(flops=1024, bytes_accessed=1024, transcendentals=0)


def normalize(hidden, norm_gain):
    values = hidden.astype(jnp.float32)
    row_scale = lax.rsqrt(jnp.mean(values * values, axis=-1, keepdims=True) + EPS_NORM)
    return (values * row_scale * norm_gain).astype(jnp.bfloat16)


def refresh(gradient, sample_grad, moment, curvature):
    moment_new = BETA_ONE * moment.astype(jnp.float32) + (1.0 - BETA_ONE) * gradient
    curvature_new = (
        BETA_TWO * curvature.astype(jnp.float32) + (1.0 - BETA_TWO) * sample_grad * sample_grad
    )
    update_direction = jnp.clip(moment_new / (RHO_SCALE * curvature_new), -1.0, 1.0)
    return (
        moment_new.astype(jnp.bfloat16),
        curvature_new.astype(jnp.bfloat16),
        update_direction.astype(jnp.bfloat16),
    )


def by_groups(hidden, norm_gain, input_ids, sampled_ids, head_weight, moment, curvature):
    normed = normalize(hidden, norm_gain)
    gathered = lax.all_gather(normed, "shard", axis=0, tiled=True)
    group_len = gathered.shape[0]
    columns = head_weight.shape[1]
    first_col = lax.axis_index("shard") * columns
    logits = jnp.dot(gathered, head_weight, preferred_element_type=jnp.float32)
    row_peak = lax.pmax(jnp.max(logits, axis=-1), "shard")
    scaled_exp = jnp.exp(logits - row_peak[:, None])
    row_sum = lax.psum(jnp.sum(scaled_exp, axis=-1), "shard")
    probabilities = (scaled_exp / row_sum[:, None]).astype(jnp.bfloat16)
    group_start = lax.axis_index("rep") * group_len
    token_ids = lax.dynamic_slice_in_dim(input_ids, group_start, group_len, 0)
    sample_ids = lax.dynamic_slice_in_dim(sampled_ids, group_start, group_len, 0)
    position = jnp.arange(group_len)
    shifted = jnp.roll(token_ids, -1) - first_col
    usable = (position < group_len - 1) & (shifted >= 0) & (shifted < columns)
    true_slot = jnp.where(usable, shifted, columns)
    sample_local = sample_ids - first_col
    inside = (sample_local >= 0) & (sample_local < columns)
    sample_slot = jnp.where(inside, sample_local, columns)
    shared = lax.dot_general(
        gathered, probabilities, (((0,), (0,)), ((), ())), preferred_element_type=jnp.float32
    )
    widened = gathered.astype(jnp.float32)
    true_sums = jax.ops.segment_sum(widened, true_slot, num_segments=columns + 1)[:columns]
    sample_sums = jax.ops.segment_sum(widened, sample_slot, num_segments=columns + 1)[:columns]
    true_part = (shared - true_sums.T).astype(jnp.bfloat16)
    sample_part = (shared - sample_sums.T).astype(jnp.bfloat16)
    gradient = lax.psum_scatter(true_part, "rep", scatter_dimension=0, tiled=True)
    sample_grad = lax.psum_scatter(sample_part, "rep", scatter_dimension=0, tiled=True)
    return refresh(
        gradient.astype(jnp.float32), sample_grad.astype(jnp.float32), moment, curvature
    )


def swap_pairs(count, bit):
    return [(index, index ^ bit) for index in range(count)]


def shift_pairs(lines, along, across):
    pairs = []
    for place in range(lines):
        for side in range(2):
            source = 2 * place + side
            pairs.append((source, 2 * ((place + along) % lines) + (side ^ across)))
    return pairs


def logits_kernel(stat_rows, *refs):
    count = len(stat_rows)
    block_refs, refs = refs[:count], refs[count:]
    weight_ref, before_ref, exp_ref, stats_ref, logits, highs, sums = refs
    step = pl.program_id(0)
    tokens, columns = logits.shape
    length = tokens // count
    half = stats_ref.shape[0] // 2
    rows = jnp.concatenate([ref[...] for ref in block_refs], axis=0)
    width = min(512, columns)
    for lane in range(0, columns, width):
        part = jnp.dot(
            rows, weight_ref[:, lane:lane + width], preferred_element_type=jnp.float32
        )
        held = logits[:, lane:lane + width]
        logits[:, lane:lane + width] = jnp.where(step == 0, 0.0, held) + part

    @pl.when(step == pl.num_programs(0) - 1)
    def _():
        chunk = 16

        def peaks(index, carry):
            place = pl.ds(pl.multiple_of(index * chunk, chunk), chunk)
            highs[place, :] = functools.reduce(
                jnp.maximum, [logits[place, lane:lane + 128] for lane in range(0, columns, 128)]
            )
            return carry

        lax.fori_loop(0, tokens // chunk, peaks, 0, unroll=2)
        highs[...] = jnp.broadcast_to(jnp.max(highs[...], axis=1, keepdims=True), highs.shape)

        def scale(index, carry):
            place = pl.ds(pl.multiple_of(index * chunk, chunk), chunk)
            peak = highs[place, :]
            total = jnp.zeros((chunk, 128), jnp.float32)
            for lane in range(0, columns, 128):
                scaled = jnp.exp(logits[place, lane:lane + 128] - peak)
                exp_ref[place, lane:lane + 128] = scaled.astype(jnp.bfloat16)
                total += scaled
            sums[place, :] = total
            return carry

        lax.fori_loop(0, tokens // chunk, scale, 0, unroll=2)
        totals = jnp.broadcast_to(jnp.sum(sums[...], axis=1, keepdims=True), sums.shape)
        stats_ref[...] = before_ref[...]
        for base, values in ((0, highs[...].T[0:1]), (half, totals.T[0:1])):
            for index, row in enumerate(stat_rows):
                stats_ref[base + row:base + row + 1, :length] = (
                    values[:, index * length:(index + 1) * length]
                )


def round_logits(blocks, stat_rows, head_weight, before):
    depth, columns = head_weight.shape
    length = blocks[0].shape[0]
    tokens = length * len(blocks)
    band = 512
    whole = lambda shape: pl.BlockSpec(shape, lambda step: (0, 0))
    return pl.pallas_call(
        functools.partial(logits_kernel, stat_rows),
        grid=(depth // band,),
        in_specs=[pl.BlockSpec((length, band), lambda step: (0, step))] * len(blocks)
        + [pl.BlockSpec((band, columns), lambda step: (step, 0)), whole(before.shape)],
        out_specs=[whole((tokens, columns)), whole(before.shape)],
        out_shape=[
            jax.ShapeDtypeStruct((tokens, columns), jnp.bfloat16),
            jax.ShapeDtypeStruct(before.shape, jnp.float32),
        ],
        scratch_shapes=[
            pltpu.VMEM((tokens, columns), jnp.float32),
            pltpu.VMEM((tokens, 128), jnp.float32),
            pltpu.VMEM((tokens, 128), jnp.float32),
        ],
        compiler_params=pltpu.CompilerParams(vmem_limit_bytes=24 * 1024 * 1024),
        cost_estimate=BRIEF,
        name="round_logits",
    )(*blocks, head_weight, before)


def turn_kernel(count, rep_ref, *refs):
    mine_ref, other_ref = refs[count:]
    step = pl.program_id(0)
    turned = jnp.concatenate([ref[...] for ref in refs[:count]], axis=0).T

    @pl.when(step == 0)
    def _():
        mine_ref[...] = turned

    @pl.when(step == 1)
    def _():
        other_ref[...] = turned


def turned_features(rep, blocks, rows):
    length = blocks[0].shape[0]
    tokens = length * len(blocks)
    whole = pl.BlockSpec((rows, tokens), lambda step, rep_ref: (0, 0))
    block = pl.BlockSpec((length, rows), lambda step, rep_ref: (0, rep_ref[0] ^ step))
    return pl.pallas_call(
        functools.partial(turn_kernel, len(blocks)),
        grid_spec=pltpu.PrefetchScalarGridSpec(
            num_scalar_prefetch=1,
            grid=(2,),
            in_specs=[block] * len(blocks),
            out_specs=[whole, whole],
        ),
        out_shape=[jax.ShapeDtypeStruct((rows, tokens), jnp.bfloat16)] * 2,
        compiler_params=pltpu.CompilerParams(vmem_limit_bytes=20 * 1024 * 1024),
        cost_estimate=BRIEF,
        name="turned_features",
    )(rep, *blocks)


def one_hot_kernel(count, *refs):
    feature_refs, refs = refs[:count], refs[count:]
    true_ref, sample_ref, true_out, sample_out = refs
    width = true_out.shape[1]
    features = jnp.concatenate([ref[...] for ref in feature_refs], axis=1)
    columns = pl.program_id(0) * width + lax.broadcasted_iota(
        jnp.int32, (width, features.shape[1]), 0
    )
    hot = jnp.concatenate([columns == true_ref[...], columns == sample_ref[...]], axis=0)
    totals = lax.dot_general(
        features, hot.astype(jnp.float32).astype(jnp.bfloat16),
        (((1,), (1,)), ((), ())), preferred_element_type=jnp.float32,
    )
    true_out[...] = totals[:, :width].astype(jnp.bfloat16)
    sample_out[...] = totals[:, width:].astype(jnp.bfloat16)


def one_hot_sums(features, ids, columns):
    rows = features[0].shape[0]
    width = min(256, columns)
    whole = lambda array: pl.BlockSpec(array.shape, lambda step: (0, 0))
    tile = pl.BlockSpec((rows, width), lambda step: (0, step))
    return pl.pallas_call(
        functools.partial(one_hot_kernel, len(features)),
        grid=(columns // width,),
        in_specs=[whole(array) for array in (*features, *ids)],
        out_specs=[tile, tile],
        out_shape=[jax.ShapeDtypeStruct((rows, columns), jnp.bfloat16)] * 2,
        compiler_params=pltpu.CompilerParams(vmem_limit_bytes=24 * 1024 * 1024),
        cost_estimate=BRIEF,
        name="one_hot_sums",
    )(*features, *ids)


def merge_kernel(own_ref, across_ref, core_ref, both_ref, merged_ref, first_ref):
    rows = own_ref.shape[0] // 2
    side = rows // 2
    for core, (near, far) in enumerate(((own_ref, across_ref), (core_ref, both_ref))):
        place = core * rows
        first, total = near[:rows], near[rows:]
        second = jnp.concatenate([far[side:rows], far[:side]], axis=0)
        other = jnp.concatenate([far[rows + side:], far[rows:rows + side]], axis=0)
        peak = jnp.maximum(first, second)
        merged_ref[place:place + rows] = peak
        merged_ref[2 * rows + place:3 * rows + place] = (
            total * jnp.exp(first - peak) + other * jnp.exp(second - peak)
        )
        first_ref[place:place + rows] = first


def merged_stats(own, across, core, both):
    rows, lanes = own.shape
    return pl.pallas_call(
        merge_kernel,
        out_shape=[
            jax.ShapeDtypeStruct((2 * rows, lanes), jnp.float32),
            jax.ShapeDtypeStruct((rows, lanes), jnp.float32),
        ],
        compiler_params=pltpu.CompilerParams(vmem_limit_bytes=4 * 1024 * 1024),
        cost_estimate=BRIEF,
        name="merged_stats",
    )(own, across, core, both)


def refresh_kernel(lines, length, early_rows, late_rows, *refs):
    early_refs, late_refs, refs = refs[:2], refs[2:4], refs[4:]
    exp_refs, refs = refs[:6], refs[6:]
    stats_refs, refs = refs[:lines], refs[lines:]
    (first_ref, true_ids, sample_ids, true_sum, sample_sum, moment_ref, curvature_ref,
     moment_out, curvature_out, update_out, scaled, factors, true_at, sample_at) = refs
    step = pl.program_id(0)
    width = moment_out.shape[1]
    early = len(early_rows) * length
    late = len(late_rows) * length

    @pl.when(step == 0)
    def _():
        rows = first_ref.shape[0]

        def turned(values, along):
            return jnp.concatenate([
                values[group + (turn + along) % lines:group + (turn + along) % lines + 1]
                for group in range(0, rows, lines) for turn in range(lines)
            ], axis=0) if along else values

        peaks = [turned(ref[:rows], along) for along, ref in enumerate(stats_refs)]
        totals = [turned(ref[rows:], along) for along, ref in enumerate(stats_refs)]
        peak = functools.reduce(jnp.maximum, peaks)
        total = sum(t * jnp.exp(p - peak) for p, t in zip(peaks, totals))
        factor = jnp.exp(first_ref[...] - peak) / total
        per_core = rows // 2
        for core in range(2):
            for index in range(0, len(early_rows), 2):
                pair = jnp.concatenate([
                    factor[core * per_core + row:core * per_core + row + 1, :length]
                    for row in early_rows[index:index + 2]
                ], axis=1)
                place = index * length
                values = early_refs[core][:, place:place + 2 * length].astype(jnp.float32)
                place += core * early
                scaled[:, place:place + 2 * length] = (values * pair).astype(jnp.bfloat16)
        full = jnp.concatenate([factor, jnp.zeros((128 - rows, 128), jnp.float32)], axis=0).T
        for core in range(2):
            for index, row in enumerate(late_rows):
                place = core * late + index * length
                at = core * per_core + row
                factors[place:place + length] = jnp.broadcast_to(
                    full[:length, at:at + 1], (length, 128)
                )
        lanes = lax.broadcasted_iota(jnp.int32, true_at.shape, 1)
        true_at[...] = true_ids[...] - lanes
        sample_at[...] = sample_ids[...] - lanes

    shared = jnp.dot(
        scaled[...], jnp.concatenate([exp_refs[0][...], exp_refs[3][...]], axis=0),
        preferred_element_type=jnp.float32,
    )
    gradient = shared - true_sum[...].astype(jnp.float32)
    sample_grad = shared - sample_sum[...].astype(jnp.float32)
    for core in range(2):
        place = slice(core * late, (core + 1) * late)
        exps = jnp.concatenate([ref[...] for ref in exp_refs[3 * core + 1:3 * core + 3]], axis=0)
        true_parts, sample_parts = [], []
        for lane in range(0, width, 128):
            probs = exps[:, lane:lane + 128].astype(jnp.float32) * factors[place]
            at = step * width + lane
            true_parts.append(
                (probs - jnp.where(true_at[place] == at, 1.0, 0.0)).astype(jnp.bfloat16)
            )
            sample_parts.append(
                (probs - jnp.where(sample_at[place] == at, 1.0, 0.0)).astype(jnp.bfloat16)
            )
        features = late_refs[core][...]
        gradient += jnp.dot(
            features, jnp.concatenate(true_parts, axis=1), preferred_element_type=jnp.float32
        )
        sample_grad += jnp.dot(
            features, jnp.concatenate(sample_parts, axis=1), preferred_element_type=jnp.float32
        )
    moment_out[...], curvature_out[...], update_out[...] = refresh(
        gradient, sample_grad, moment_ref[...], curvature_ref[...]
    )


def refresh_states(lines, length, early_rows, late_rows, early, late, exps, stats, first,
                   late_ids, sums, moment, curvature):
    rows, columns = moment.shape
    width = min(256, columns)
    late_tokens = 2 * late[0].shape[1]
    whole = lambda array: pl.BlockSpec(array.shape, lambda step: (0, 0))
    tile = pl.BlockSpec((rows, width), lambda step: (0, step))
    return pl.pallas_call(
        functools.partial(refresh_kernel, lines, length, early_rows, late_rows),
        grid=(columns // width,),
        in_specs=[whole(array) for array in (*early, *late)]
        + [pl.BlockSpec((array.shape[0], width), lambda step: (0, step)) for array in exps]
        + [whole(array) for array in (*stats, first, *late_ids)]
        + [tile] * 4,
        out_specs=[tile] * 3,
        out_shape=[jax.ShapeDtypeStruct((rows, columns), jnp.bfloat16)] * 3,
        scratch_shapes=[
            pltpu.VMEM((rows, 2 * early[0].shape[1]), jnp.bfloat16),
            pltpu.VMEM((late_tokens, 128), jnp.float32),
            pltpu.VMEM((late_tokens, 128), jnp.int32),
            pltpu.VMEM((late_tokens, 128), jnp.int32),
        ],
        compiler_params=pltpu.CompilerParams(vmem_limit_bytes=36 * 1024 * 1024),
        cost_estimate=BRIEF,
        name="refresh_states",
    )(*early, *late, *exps, *stats, first, *late_ids, *sums, moment, curvature)


def after(value, *others):
    return lax.optimization_barrier((value, *others))[0]


def all_tokens(reps, shards, hidden, norm_gain, input_ids, sampled_ids, head_weight, moment, curvature):
    lines = shards // 2
    length = hidden.shape[0]
    rows, columns = moment.shape
    rep = lax.axis_index("rep")
    shard = lax.axis_index("shard")
    first_col = shard * columns
    group_len = length * shards

    def to_x(values):
        return lax.ppermute(values, "rep", swap_pairs(reps, 2))

    def to_core(values):
        return lax.ppermute(values, "rep", swap_pairs(reps, 1))

    def to_y(values):
        return lax.ppermute(values, "shard", swap_pairs(shards, 1))

    def to_y_core(values):
        pairs = [
            (rep_at * shards + at, (rep_at ^ 1) * shards + (at ^ 1))
            for rep_at in range(reps) for at in range(shards)
        ]
        return lax.ppermute(values, ("rep", "shard"), pairs)

    def to_z(values, along):
        return lax.ppermute(values, "shard", shift_pairs(lines, along, 0))

    split = lines // 2
    plain = [(0, 0), (0, 1), (1, 0)]
    early_blocks = [(*kind, turn) for turn in range(split) for kind in plain]
    middle_blocks = [(*kind, turn) for turn in range(split, lines) for kind in plain]
    middle_blocks += [(1, 1, turn) for turn in range(split)]
    last_blocks = [(1, 1, turn) for turn in range(split, lines)]
    groups = [early_blocks, middle_blocks, last_blocks]

    def stat_row(block):
        return (2 * block[0] + block[1]) * lines + block[2]

    normed = normalize(hidden, norm_gain)

    last = jnp.arange(input_ids.shape[0]) % group_len == group_len - 1
    targets = jnp.where(last, -1, jnp.roll(input_ids, -1) - first_col)
    ids = jnp.stack([targets, sampled_ids - first_col]).reshape(2, reps * shards, length)
    side, across, turn = (np.array(values) for values in zip(*sum(groups, [])))
    holder = (rep ^ (2 * across[None] + np.arange(2)[:, None])).reshape(-1)
    place = 2 * ((shard // 2 - turn) % lines) + ((shard % 2) ^ side)
    ids = jnp.take(ids, holder * shards + jnp.tile(place, 2), axis=1)
    ids = ids.reshape(2, 2, len(side), length)
    early_ids = ids[:, :, :len(early_blocks)].reshape(2, 1, -1)
    late_ids = ids[:, :, len(early_blocks):].reshape(2, -1, 1)
    early_ids, late_ids = [early_ids[0], early_ids[1]], [late_ids[0], late_ids[1]]
    rep_scalar = rep.astype(jnp.int32).reshape(1)
    head_weight = pltpu.with_memory_space_constraint(head_weight, pltpu.HBM)
    stats = jnp.zeros((8 * lines, 128), jnp.float32)

    held = {(0, 0, 0): normed}
    exps = []

    def logits(group, stats, *gates):
        blocks = [held[block] for block in group]
        blocks[0] = after(blocks[0], *gates)
        exp, stats = round_logits(blocks, [stat_row(block) for block in group], head_weight, stats)
        exps.append(exp)
        return stats

    def diagonal(turn, *gates):
        if turn % 2 == 0:
            return to_x(after(held[1, 0, turn], *gates) if gates else held[1, 0, turn])
        return to_y(after(held[0, 1, turn], *gates) if gates else held[0, 1, turn])

    for turn in range(lines):
        block = held[0, 0, turn]
        held[0, 1, turn] = to_x(block)
        held[1, 0, turn] = to_y(block)
        if turn + 1 < lines:
            arrived = [to_z(block, 1), held[0, 1, turn], held[1, 0, turn]]
            if turn == 0:
                arrived += [*early_ids, *late_ids, rep_scalar, stats]
            arrived = lax.optimization_barrier((*arrived, *exps[-1:]))
            held[0, 0, turn + 1], held[0, 1, turn], held[1, 0, turn] = arrived[:3]
            if turn == 0:
                early_ids, late_ids = list(arrived[3:5]), list(arrived[5:7])
                rep_scalar, stats = arrived[7:]
            if turn + 1 == split:
                stats = logits(early_blocks, stats, held[0, 0, split])
        if turn < split:
            held[1, 1, turn] = diagonal(turn)

    early = [held[block] for block in early_blocks]
    early[0] = after(early[0], held[0, 0, lines - 1], held[1, 1, 0])
    early = turned_features(rep_scalar, early, rows)
    early = [early[0], to_core(early[1])]
    early_ids[0] = after(early_ids[0], held[0, 0, lines - 1])
    sums = one_hot_sums(early, early_ids, columns)
    for turn in range(split, lines):
        held[1, 1, turn] = diagonal(turn, early[0] if turn % 2 == 0 else sums[0])
    other_exps = [to_core(after(exps[0], early[0]))]
    stats = logits(middle_blocks, stats, *sums, other_exps[0])
    stats = logits(last_blocks, stats)
    other_exps.append(to_core(after(exps[1], stats)))
    across_stats, core_stats, both_stats = to_y(stats), to_core(stats), to_y_core(stats)
    late_held = [held[block] for block in middle_blocks + last_blocks]
    late_held[0] = after(late_held[0], stats)
    late = turned_features(rep_scalar, late_held, rows)
    merged, first = merged_stats(
        after(stats, *other_exps), across_stats, core_stats, both_stats
    )
    all_stats = [merged] + [to_z(merged, -along) for along in range(1, lines)]
    other_exps.append(to_core(after(exps[-1], merged)))
    late = [late[0], to_core(late[1])]
    return tuple(refresh_states(
        lines, length, [stat_row(block) for block in early_blocks],
        [stat_row(block) for block in middle_blocks + last_blocks], early, late,
        exps + other_exps, all_stats, first, late_ids, sums, moment, curvature,
    ))


def solution(mesh):
    in_specs = (
        P(("rep", "shard"), None),
        P(),
        P(),
        P(),
        P(None, "shard"),
        P("rep", "shard"),
        P("rep", "shard"),
    )
    out_specs = (P("rep", "shard"), P("rep", "shard"), P("rep", "shard"))
    reps, shards = mesh.shape["rep"], mesh.shape["shard"]

    def whole(hidden, *others):
        tokens, depth = hidden.shape
        length = tokens // (reps * shards)
        fits = hidden.size * 2 <= GATHER_BYTES and reps == 4 and shards % 2 == 0
        if fits and length == 64 and (depth // reps) % 128 == 0:
            plan = functools.partial(all_tokens, reps, shards)
        else:
            plan = by_groups

        return jax.shard_map(
            plan, mesh=mesh, in_specs=in_specs, out_specs=out_specs, check_vma=False
        )(hidden, *others)

    return whole
```

```python
import functools

import jax
import jax.numpy as jnp
import numpy as np
from jax import lax
from jax.experimental import pallas as pl
from jax.experimental.pallas import tpu as pltpu
from jax.sharding import PartitionSpec as P

EPS_NORM = 1e-05
BETA_ONE = 0.96
BETA_TWO = 0.95
RHO_SCALE = 0.05
GATHER_BYTES = 32 * 1024 * 1024
LOGITS_VMEM = 20 * 1024 * 1024
BRIEF = pl.CostEstimate(flops=1024, bytes_accessed=1024, transcendentals=0)


def normalize(hidden, norm_gain):
    values = hidden.astype(jnp.float32)
    row_scale = lax.rsqrt(jnp.mean(values * values, axis=-1, keepdims=True) + EPS_NORM)
    return (values * row_scale * norm_gain).astype(jnp.bfloat16)


def refresh(gradient, sample_grad, moment, curvature):
    moment_new = BETA_ONE * moment.astype(jnp.float32) + (1.0 - BETA_ONE) * gradient
    curvature_new = (
        BETA_TWO * curvature.astype(jnp.float32) + (1.0 - BETA_TWO) * sample_grad * sample_grad
    )
    update_direction = jnp.clip(moment_new / (RHO_SCALE * curvature_new), -1.0, 1.0)
    return (
        moment_new.astype(jnp.bfloat16),
        curvature_new.astype(jnp.bfloat16),
        update_direction.astype(jnp.bfloat16),
    )


def by_groups(hidden, norm_gain, input_ids, sampled_ids, head_weight, moment, curvature):
    normed = normalize(hidden, norm_gain)
    gathered = lax.all_gather(normed, "shard", axis=0, tiled=True)
    group_len = gathered.shape[0]
    columns = head_weight.shape[1]
    first_col = lax.axis_index("shard") * columns
    logits = jnp.dot(gathered, head_weight, preferred_element_type=jnp.float32)
    row_peak = lax.pmax(jnp.max(logits, axis=-1), "shard")
    scaled_exp = jnp.exp(logits - row_peak[:, None])
    row_sum = lax.psum(jnp.sum(scaled_exp, axis=-1), "shard")
    probabilities = (scaled_exp / row_sum[:, None]).astype(jnp.bfloat16)
    group_start = lax.axis_index("rep") * group_len
    token_ids = lax.dynamic_slice_in_dim(input_ids, group_start, group_len, 0)
    sample_ids = lax.dynamic_slice_in_dim(sampled_ids, group_start, group_len, 0)
    position = jnp.arange(group_len)
    shifted = jnp.roll(token_ids, -1) - first_col
    usable = (position < group_len - 1) & (shifted >= 0) & (shifted < columns)
    true_slot = jnp.where(usable, shifted, columns)
    sample_local = sample_ids - first_col
    inside = (sample_local >= 0) & (sample_local < columns)
    sample_slot = jnp.where(inside, sample_local, columns)
    shared = lax.dot_general(
        gathered, probabilities, (((0,), (0,)), ((), ())), preferred_element_type=jnp.float32
    )
    widened = gathered.astype(jnp.float32)
    true_sums = jax.ops.segment_sum(widened, true_slot, num_segments=columns + 1)[:columns]
    sample_sums = jax.ops.segment_sum(widened, sample_slot, num_segments=columns + 1)[:columns]
    true_part = (shared - true_sums.T).astype(jnp.bfloat16)
    sample_part = (shared - sample_sums.T).astype(jnp.bfloat16)
    gradient = lax.psum_scatter(true_part, "rep", scatter_dimension=0, tiled=True)
    sample_grad = lax.psum_scatter(sample_part, "rep", scatter_dimension=0, tiled=True)
    return refresh(
        gradient.astype(jnp.float32), sample_grad.astype(jnp.float32), moment, curvature
    )


def swap_pairs(count, bit):
    return [(index, index ^ bit) for index in range(count)]


def shift_pairs(lines, along, across):
    pairs = []
    for place in range(lines):
        for side in range(2):
            source = 2 * place + side
            pairs.append((source, 2 * ((place + along) % lines) + (side ^ across)))
    return pairs


def prepare_kernel(weight_ref, true_ids, sample_ids, *refs):
    held_ref, true_at, sample_at, arrived = refs[-4:]
    count = arrived.shape[0]
    band = weight_ref.shape[0] // count
    copies = [
        pltpu.make_async_copy(
            weight_ref.at[pl.ds(index * band, band)], held_ref.at[pl.ds(index * band, band)],
            arrived.at[index],
        )
        for index in range(count)
    ]
    for copy in copies:
        copy.start()
    lanes = lax.broadcasted_iota(jnp.int32, (128, 128), 1)
    for ids_ref, out_ref in ((true_ids, true_at), (sample_ids, sample_at)):
        for place in range(0, out_ref.shape[0], 128):
            ids = jnp.broadcast_to(ids_ref[:, place:place + 128], (128, 128)).T
            out_ref[place:place + 128] = ids - lanes
    for copy in copies:
        copy.wait()


def prepared(weight, true_ids, sample_ids, *earlier):
    near = pl.BlockSpec(memory_space=pltpu.VMEM)
    late = jax.ShapeDtypeStruct((true_ids.shape[1], 128), jnp.int32)
    return pl.pallas_call(
        prepare_kernel,
        in_specs=[pl.BlockSpec(memory_space=pltpu.HBM)] + [near] * (2 + len(earlier)),
        out_specs=[near] * 3,
        out_shape=[pltpu.VMEM(weight.shape, weight.dtype), late, late],
        scratch_shapes=[pltpu.SemaphoreType.DMA((4,))],
        compiler_params=pltpu.CompilerParams(vmem_limit_bytes=8 * 1024 * 1024),
        cost_estimate=BRIEF,
        name="prepared",
    )(pltpu.with_memory_space_constraint(weight, pltpu.HBM), true_ids, sample_ids, *earlier)


def logits_kernel(stat_rows, *refs):
    count = len(stat_rows)
    block_refs, refs = refs[:count], refs[count:]
    weight_ref, before_ref, exp_ref, stats_ref, rows, logits, scaled_exp, highs, sums, sent = refs
    tokens, columns = logits.shape
    length = tokens // count
    half = stats_ref.shape[0] // 2
    for index, ref in enumerate(block_refs):
        rows[index * length:(index + 1) * length] = ref[...]
    highs[...] = jnp.full(highs.shape, -jnp.inf, jnp.float32)
    width = min(256, columns)

    def multiply(index, carry):
        place = pl.ds(pl.multiple_of(index * width, width), width)
        part = jnp.dot(rows[...], weight_ref[:, place], preferred_element_type=jnp.float32)
        logits[:, place] = part
        high = functools.reduce(
            jnp.maximum, [part[:, lane:lane + 128] for lane in range(0, width, 128)]
        )
        highs[...] = jnp.maximum(highs[...], high)
        return carry

    lax.fori_loop(0, columns // width, multiply, 0)
    highs[...] = jnp.broadcast_to(jnp.max(highs[...], axis=1, keepdims=True), highs.shape)
    chunk = 16
    copies = []
    for block in range(count):

        def scale(index, carry, block=block):
            place = pl.ds(pl.multiple_of(block * length + index * chunk, chunk), chunk)
            peak = highs[place, :]
            total = jnp.zeros((chunk, 128), jnp.float32)
            for lane in range(0, columns, 128):
                scaled = jnp.exp(logits[place, lane:lane + 128] - peak)
                scaled_exp[place, lane:lane + 128] = scaled.astype(jnp.bfloat16)
                total += scaled
            sums[place, :] = total
            return carry

        lax.fori_loop(0, length // chunk, scale, 0, unroll=2)
        place = pl.ds(block * length, length)
        copies.append(
            pltpu.make_async_copy(scaled_exp.at[place], exp_ref.at[place], sent.at[block])
        )
        copies[-1].start()
    totals = jnp.broadcast_to(jnp.sum(sums[...], axis=1, keepdims=True), sums.shape)
    stats_ref[...] = before_ref[...]
    for base, values in ((0, highs[...].T[0:1]), (half, totals.T[0:1])):
        for index, row in enumerate(stat_rows):
            stats_ref[base + row:base + row + 1, :length] = (
                values[:, index * length:(index + 1) * length]
            )
    for copy in copies:
        copy.wait()


def round_logits(blocks, stat_rows, held_weight, before):
    depth, columns = held_weight.shape
    length = blocks[0].shape[0]
    tokens = length * len(blocks)
    near = pl.BlockSpec(memory_space=pltpu.VMEM)
    held_weight = pltpu.with_memory_space_constraint(held_weight, pltpu.VMEM)
    return pl.pallas_call(
        functools.partial(logits_kernel, stat_rows),
        in_specs=[near] * (len(blocks) + 2),
        out_specs=[pl.BlockSpec(memory_space=pltpu.HBM), near],
        out_shape=[
            pltpu.HBM((tokens, columns), jnp.bfloat16),
            jax.ShapeDtypeStruct(before.shape, jnp.float32),
        ],
        scratch_shapes=[
            pltpu.VMEM((tokens, depth), jnp.bfloat16),
            pltpu.VMEM((tokens, columns), jnp.float32),
            pltpu.VMEM((tokens, columns), jnp.bfloat16),
            pltpu.VMEM((tokens, 128), jnp.float32),
            pltpu.VMEM((tokens, 128), jnp.float32),
            pltpu.SemaphoreType.DMA((len(blocks),)),
        ],
        compiler_params=pltpu.CompilerParams(vmem_limit_bytes=LOGITS_VMEM),
        cost_estimate=BRIEF,
        name="round_logits",
    )(*blocks, held_weight, before)


def turn_kernel(count, rep_ref, *refs):
    mine_ref, other_ref = refs[count:]
    step = pl.program_id(0)
    turned = jnp.concatenate([ref[...] for ref in refs[:count]], axis=0).T

    @pl.when(step == 0)
    def _():
        mine_ref[...] = turned

    @pl.when(step == 1)
    def _():
        other_ref[...] = turned


def turned_features(rep, blocks, rows):
    length = blocks[0].shape[0]
    tokens = length * len(blocks)
    whole = pl.BlockSpec((rows, tokens), lambda step, rep_ref: (0, 0))
    block = pl.BlockSpec((length, rows), lambda step, rep_ref: (0, rep_ref[0] ^ step))
    return pl.pallas_call(
        functools.partial(turn_kernel, len(blocks)),
        grid_spec=pltpu.PrefetchScalarGridSpec(
            num_scalar_prefetch=1,
            grid=(2,),
            in_specs=[block] * len(blocks),
            out_specs=[whole, whole],
        ),
        out_shape=[jax.ShapeDtypeStruct((rows, tokens), jnp.bfloat16)] * 2,
        compiler_params=pltpu.CompilerParams(vmem_limit_bytes=20 * 1024 * 1024),
        cost_estimate=BRIEF,
        name="turned_features",
    )(rep, *blocks)


def one_hot_kernel(count, *refs):
    feature_refs, refs = refs[:count], refs[count:]
    true_ref, sample_ref, true_out, sample_out = refs
    width = true_out.shape[1]
    features = jnp.concatenate([ref[...] for ref in feature_refs], axis=1)
    columns = pl.program_id(0) * width + lax.broadcasted_iota(
        jnp.int32, (width, features.shape[1]), 0
    )
    hot = jnp.concatenate([columns == true_ref[...], columns == sample_ref[...]], axis=0)
    totals = lax.dot_general(
        features, hot.astype(jnp.float32).astype(jnp.bfloat16),
        (((1,), (1,)), ((), ())), preferred_element_type=jnp.float32,
    )
    true_out[...] = totals[:, :width].astype(jnp.bfloat16)
    sample_out[...] = totals[:, width:].astype(jnp.bfloat16)


def one_hot_sums(features, ids, columns):
    rows = features[0].shape[0]
    width = min(256, columns)
    whole = lambda array: pl.BlockSpec(array.shape, lambda step: (0, 0))
    tile = pl.BlockSpec((rows, width), lambda step: (0, step))
    return pl.pallas_call(
        functools.partial(one_hot_kernel, len(features)),
        grid=(columns // width,),
        in_specs=[whole(array) for array in (*features, *ids)],
        out_specs=[tile, tile],
        out_shape=[pltpu.HBM((rows, columns), jnp.bfloat16)] * 2,
        compiler_params=pltpu.CompilerParams(vmem_limit_bytes=24 * 1024 * 1024),
        cost_estimate=BRIEF,
        name="one_hot_sums",
    )(*features, *ids)


def merge_kernel(own_ref, across_ref, core_ref, both_ref, merged_ref, first_ref):
    rows = own_ref.shape[0] // 2
    side = rows // 2
    for core, (near, far) in enumerate(((own_ref, across_ref), (core_ref, both_ref))):
        place = core * rows
        first, total = near[:rows], near[rows:]
        second = jnp.concatenate([far[side:rows], far[:side]], axis=0)
        other = jnp.concatenate([far[rows + side:], far[rows:rows + side]], axis=0)
        peak = jnp.maximum(first, second)
        merged_ref[place:place + rows] = peak
        merged_ref[2 * rows + place:3 * rows + place] = (
            total * jnp.exp(first - peak) + other * jnp.exp(second - peak)
        )
        first_ref[place:place + rows] = first


def merged_stats(own, across, core, both):
    rows, lanes = own.shape
    return pl.pallas_call(
        merge_kernel,
        out_shape=[
            jax.ShapeDtypeStruct((2 * rows, lanes), jnp.float32),
            jax.ShapeDtypeStruct((rows, lanes), jnp.float32),
        ],
        compiler_params=pltpu.CompilerParams(vmem_limit_bytes=4 * 1024 * 1024),
        cost_estimate=BRIEF,
        name="merged_stats",
    )(own, across, core, both)


def refresh_kernel(lines, length, early_rows, late_rows, *refs):
    early_refs, late_refs, refs = refs[:2], refs[2:4], refs[4:]
    exp_refs, refs = refs[:6], refs[6:]
    stats_refs, refs = refs[:lines], refs[lines:]
    (first_ref, true_at, sample_at, true_sum, sample_sum, moment_ref, curvature_ref,
     moment_out, curvature_out, update_out, scaled, factors) = refs
    step = pl.program_id(0)
    width = moment_out.shape[1]
    early = len(early_rows) * length
    late = len(late_rows) * length

    @pl.when(step == 0)
    def _():
        rows = first_ref.shape[0]

        def turned(values, along):
            return jnp.concatenate([
                values[group + (turn + along) % lines:group + (turn + along) % lines + 1]
                for group in range(0, rows, lines) for turn in range(lines)
            ], axis=0) if along else values

        peaks = [turned(ref[:rows], along) for along, ref in enumerate(stats_refs)]
        totals = [turned(ref[rows:], along) for along, ref in enumerate(stats_refs)]
        peak = functools.reduce(jnp.maximum, peaks)
        total = sum(t * jnp.exp(p - peak) for p, t in zip(peaks, totals))
        factor = jnp.exp(first_ref[...] - peak) / total
        per_core = rows // 2
        for core in range(2):
            for index in range(0, len(early_rows), 2):
                pair = jnp.concatenate([
                    factor[core * per_core + row:core * per_core + row + 1, :length]
                    for row in early_rows[index:index + 2]
                ], axis=1)
                place = index * length
                values = early_refs[core][:, place:place + 2 * length].astype(jnp.float32)
                place += core * early
                scaled[:, place:place + 2 * length] = (values * pair).astype(jnp.bfloat16)
        full = jnp.concatenate([factor, jnp.zeros((128 - rows, 128), jnp.float32)], axis=0).T
        for core in range(2):
            for index, row in enumerate(late_rows):
                place = core * late + index * length
                at = core * per_core + row
                factors[place:place + length] = jnp.broadcast_to(
                    full[:length, at:at + 1], (length, 128)
                )

    shared = jnp.dot(
        scaled[...], jnp.concatenate([exp_refs[0][...], exp_refs[3][...]], axis=0),
        preferred_element_type=jnp.float32,
    )
    gradient = shared - true_sum[...].astype(jnp.float32)
    sample_grad = shared - sample_sum[...].astype(jnp.float32)
    for core in range(2):
        place = slice(core * late, (core + 1) * late)
        exps = jnp.concatenate([ref[...] for ref in exp_refs[3 * core + 1:3 * core + 3]], axis=0)
        true_parts, sample_parts = [], []
        for lane in range(0, width, 128):
            probs = exps[:, lane:lane + 128].astype(jnp.float32) * factors[place]
            at = step * width + lane
            true_parts.append(
                (probs - jnp.where(true_at[place] == at, 1.0, 0.0)).astype(jnp.bfloat16)
            )
            sample_parts.append(
                (probs - jnp.where(sample_at[place] == at, 1.0, 0.0)).astype(jnp.bfloat16)
            )
        features = late_refs[core][...]
        gradient += jnp.dot(
            features, jnp.concatenate(true_parts, axis=1), preferred_element_type=jnp.float32
        )
        sample_grad += jnp.dot(
            features, jnp.concatenate(sample_parts, axis=1), preferred_element_type=jnp.float32
        )
    moment_out[...], curvature_out[...], update_out[...] = refresh(
        gradient, sample_grad, moment_ref[...], curvature_ref[...]
    )


def refresh_states(lines, length, early_rows, late_rows, early, late, exps, stats, first,
                   late_ids, sums, moment, curvature):
    rows, columns = moment.shape
    width = min(256, columns)
    late_tokens = 2 * late[0].shape[1]
    whole = lambda array: pl.BlockSpec(array.shape, lambda step: (0, 0))
    tile = pl.BlockSpec((rows, width), lambda step: (0, step))
    return pl.pallas_call(
        functools.partial(refresh_kernel, lines, length, early_rows, late_rows),
        grid=(columns // width,),
        in_specs=[whole(array) for array in (*early, *late)]
        + [pl.BlockSpec((array.shape[0], width), lambda step: (0, step)) for array in exps]
        + [whole(array) for array in (*stats, first, *late_ids)]
        + [tile] * 4,
        out_specs=[tile] * 3,
        out_shape=[jax.ShapeDtypeStruct((rows, columns), jnp.bfloat16)] * 3,
        scratch_shapes=[
            pltpu.VMEM((rows, 2 * early[0].shape[1]), jnp.bfloat16),
            pltpu.VMEM((late_tokens, 128), jnp.float32),
        ],
        compiler_params=pltpu.CompilerParams(vmem_limit_bytes=36 * 1024 * 1024),
        cost_estimate=BRIEF,
        name="refresh_states",
    )(
        *early, *late, *in_hbm(exps[:3]), *exps[3:], *stats, first, *late_ids,
        *in_hbm(sums, [moment, curvature])
    )


def in_hbm(*lists):
    return [pltpu.with_memory_space_constraint(array, pltpu.HBM) for array in sum(map(list, lists), [])]


def after(value, *others):
    return lax.optimization_barrier((value, *others))[0]


def all_tokens(reps, shards, hidden, norm_gain, input_ids, sampled_ids, head_weight, moment, curvature):
    lines = shards // 2
    length = hidden.shape[0]
    rows, columns = moment.shape
    rep = lax.axis_index("rep")
    shard = lax.axis_index("shard")
    first_col = shard * columns
    group_len = length * shards

    def to_x(values):
        return lax.ppermute(values, "rep", swap_pairs(reps, 2))

    def to_core(values):
        return lax.ppermute(values, "rep", swap_pairs(reps, 1))

    def to_y(values):
        return lax.ppermute(values, "shard", swap_pairs(shards, 1))

    def to_y_core(values):
        pairs = [
            (rep_at * shards + at, (rep_at ^ 1) * shards + (at ^ 1))
            for rep_at in range(reps) for at in range(shards)
        ]
        return lax.ppermute(values, ("rep", "shard"), pairs)

    def to_z(values, along):
        return lax.ppermute(values, "shard", shift_pairs(lines, along, 0))

    split = lines // 2
    plain = [(0, 0), (0, 1), (1, 0)]
    early_blocks = [(*kind, turn) for turn in range(split) for kind in plain]
    middle_blocks = [(*kind, turn) for turn in range(split, lines) for kind in plain]
    middle_blocks += [(1, 1, turn) for turn in range(split)]
    last_blocks = [(1, 1, turn) for turn in range(split, lines)]
    groups = [early_blocks, middle_blocks, last_blocks]

    def stat_row(block):
        return (2 * block[0] + block[1]) * lines + block[2]

    normed = normalize(hidden, norm_gain)

    last = jnp.arange(input_ids.shape[0]) % group_len == group_len - 1
    targets = jnp.where(last, -1, jnp.roll(input_ids, -1) - first_col)
    ids = jnp.stack([targets, sampled_ids - first_col]).reshape(2, reps * shards, length)
    side, across, turn = (np.array(values) for values in zip(*sum(groups, [])))
    holder = (rep ^ (2 * across[None] + np.arange(2)[:, None])).reshape(-1)
    place = 2 * ((shard // 2 - turn) % lines) + ((shard % 2) ^ side)
    ids = jnp.take(ids, holder * shards + jnp.tile(place, 2), axis=1)
    ids = ids.reshape(2, 2, len(side), length)
    early_ids = ids[:, :, :len(early_blocks)].reshape(2, 1, -1)
    late_ids = ids[:, :, len(early_blocks):].reshape(2, 1, -1)
    early_ids, late_ids = [early_ids[0], early_ids[1]], [late_ids[0], late_ids[1]]
    rep_scalar = rep.astype(jnp.int32).reshape(1)
    stats = jnp.zeros((8 * lines, 128), jnp.float32)

    held = {(0, 0, 0): normed}
    exps = []

    def logits(group, stats, *gates):
        blocks = [held[block] for block in group]
        blocks[0] = after(blocks[0], *gates)
        exp, stats = round_logits(blocks, [stat_row(block) for block in group], head_weight, stats)
        exps.append(exp)
        return stats

    def diagonal(turn, *gates):
        if turn % 2 == 0:
            return to_x(after(held[1, 0, turn], *gates) if gates else held[1, 0, turn])
        return to_y(after(held[0, 1, turn], *gates) if gates else held[0, 1, turn])

    for turn in range(lines):
        block = held[0, 0, turn]
        held[0, 1, turn] = to_x(block)
        held[1, 0, turn] = to_y(block)
        if turn + 1 < lines:
            arrived = [to_z(block, 1), held[0, 1, turn], held[1, 0, turn]]
            if turn == 0:
                head_weight, *late_ids = prepared(head_weight, *late_ids, *early_ids, stats)
                arrived += [*early_ids, *late_ids, rep_scalar, stats, head_weight]
            arrived = lax.optimization_barrier((*arrived, *exps[-1:]))
            held[0, 0, turn + 1], held[0, 1, turn], held[1, 0, turn] = arrived[:3]
            if turn == 0:
                early_ids, late_ids = list(arrived[3:5]), list(arrived[5:7])
                rep_scalar, stats, head_weight = arrived[7:]
            if turn + 1 == split:
                stats = logits(early_blocks, stats, held[0, 0, split])
        if turn < split:
            held[1, 1, turn] = diagonal(turn)

    early = [held[block] for block in early_blocks]
    early[0] = after(early[0], held[0, 0, lines - 1], held[1, 1, 0])
    early = turned_features(rep_scalar, early, rows)
    early = [early[0], to_core(early[1])]
    early_ids[0] = after(early_ids[0], held[0, 0, lines - 1])
    sums = one_hot_sums(early, early_ids, columns)
    for turn in range(split, lines):
        held[1, 1, turn] = diagonal(turn, early[0] if turn % 2 == 0 else sums[0])
    other_exps = [to_core(after(exps[0], early[0]))]
    stats = logits(middle_blocks, stats, *sums, other_exps[0])
    stats = logits(last_blocks, stats)
    other_exps.append(to_core(after(exps[1], stats)))
    across_stats, core_stats, both_stats = to_y(stats), to_core(stats), to_y_core(stats)
    late_held = [held[block] for block in middle_blocks + last_blocks]
    late_held[0] = after(late_held[0], stats)
    late = turned_features(rep_scalar, late_held, rows)
    merged, first = merged_stats(
        after(stats, *other_exps), across_stats, core_stats, both_stats
    )
    all_stats = [merged] + [to_z(merged, -along) for along in range(1, lines)]
    other_exps.append(to_core(after(exps[-1], merged)))
    late = [late[0], to_core(late[1])]
    return tuple(refresh_states(
        lines, length, [stat_row(block) for block in early_blocks],
        [stat_row(block) for block in middle_blocks + last_blocks], early, late,
        exps + other_exps, all_stats, first, late_ids, sums, moment, curvature,
    ))


def solution(mesh):
    in_specs = (
        P(("rep", "shard"), None),
        P(),
        P(),
        P(),
        P(None, "shard"),
        P("rep", "shard"),
        P("rep", "shard"),
    )
    out_specs = (P("rep", "shard"), P("rep", "shard"), P("rep", "shard"))
    reps, shards = mesh.shape["rep"], mesh.shape["shard"]

    def whole(hidden, *others):
        tokens, depth = hidden.shape
        length = tokens // (reps * shards)
        fits = hidden.size * 2 <= GATHER_BYTES and reps == 4 and shards % 2 == 0
        if fits and length == 64 and (depth // reps) % 128 == 0:
            plan = functools.partial(all_tokens, reps, shards)
        else:
            plan = by_groups

        return jax.shard_map(
            plan, mesh=mesh, in_specs=in_specs, out_specs=out_specs, check_vma=False
        )(hidden, *others)

    return whole
```

```python
import functools

import jax
import jax.numpy as jnp
import numpy as np
from jax import lax
from jax.experimental import pallas as pl
from jax.experimental.pallas import tpu as pltpu
from jax.sharding import PartitionSpec as P

EPS_NORM = 1e-05
BETA_ONE = 0.96
BETA_TWO = 0.95
RHO_SCALE = 0.05
GATHER_BYTES = 32 * 1024 * 1024
LOGITS_VMEM = 20 * 1024 * 1024
BRIEF = pl.CostEstimate(flops=1024, bytes_accessed=1024, transcendentals=0)


def normalize(hidden, norm_gain):
    values = hidden.astype(jnp.float32)
    row_scale = lax.rsqrt(jnp.mean(values * values, axis=-1, keepdims=True) + EPS_NORM)
    return (values * row_scale * norm_gain).astype(jnp.bfloat16)


def refresh(gradient, sample_grad, moment, curvature):
    moment_new = BETA_ONE * moment.astype(jnp.float32) + (1.0 - BETA_ONE) * gradient
    curvature_new = (
        BETA_TWO * curvature.astype(jnp.float32) + (1.0 - BETA_TWO) * sample_grad * sample_grad
    )
    update_direction = jnp.clip(moment_new / (RHO_SCALE * curvature_new), -1.0, 1.0)
    return (
        moment_new.astype(jnp.bfloat16),
        curvature_new.astype(jnp.bfloat16),
        update_direction.astype(jnp.bfloat16),
    )


def by_groups(hidden, norm_gain, input_ids, sampled_ids, head_weight, moment, curvature):
    normed = normalize(hidden, norm_gain)
    gathered = lax.all_gather(normed, "shard", axis=0, tiled=True)
    group_len = gathered.shape[0]
    columns = head_weight.shape[1]
    first_col = lax.axis_index("shard") * columns
    logits = jnp.dot(gathered, head_weight, preferred_element_type=jnp.float32)
    row_peak = lax.pmax(jnp.max(logits, axis=-1), "shard")
    scaled_exp = jnp.exp(logits - row_peak[:, None])
    row_sum = lax.psum(jnp.sum(scaled_exp, axis=-1), "shard")
    probabilities = (scaled_exp / row_sum[:, None]).astype(jnp.bfloat16)
    group_start = lax.axis_index("rep") * group_len
    token_ids = lax.dynamic_slice_in_dim(input_ids, group_start, group_len, 0)
    sample_ids = lax.dynamic_slice_in_dim(sampled_ids, group_start, group_len, 0)
    position = jnp.arange(group_len)
    shifted = jnp.roll(token_ids, -1) - first_col
    usable = (position < group_len - 1) & (shifted >= 0) & (shifted < columns)
    true_slot = jnp.where(usable, shifted, columns)
    sample_local = sample_ids - first_col
    inside = (sample_local >= 0) & (sample_local < columns)
    sample_slot = jnp.where(inside, sample_local, columns)
    shared = lax.dot_general(
        gathered, probabilities, (((0,), (0,)), ((), ())), preferred_element_type=jnp.float32
    )
    widened = gathered.astype(jnp.float32)
    true_sums = jax.ops.segment_sum(widened, true_slot, num_segments=columns + 1)[:columns]
    sample_sums = jax.ops.segment_sum(widened, sample_slot, num_segments=columns + 1)[:columns]
    true_part = (shared - true_sums.T).astype(jnp.bfloat16)
    sample_part = (shared - sample_sums.T).astype(jnp.bfloat16)
    gradient = lax.psum_scatter(true_part, "rep", scatter_dimension=0, tiled=True)
    sample_grad = lax.psum_scatter(sample_part, "rep", scatter_dimension=0, tiled=True)
    return refresh(
        gradient.astype(jnp.float32), sample_grad.astype(jnp.float32), moment, curvature
    )


def swap_pairs(count, bit):
    return [(index, index ^ bit) for index in range(count)]


def shift_pairs(lines, along, across):
    pairs = []
    for place in range(lines):
        for side in range(2):
            source = 2 * place + side
            pairs.append((source, 2 * ((place + along) % lines) + (side ^ across)))
    return pairs


def prepare_kernel(weight_ref, true_ids, sample_ids, *refs):
    held_ref, true_at, sample_at, arrived = refs[-4:]
    count = arrived.shape[0]
    band = weight_ref.shape[0] // count
    copies = [
        pltpu.make_async_copy(
            weight_ref.at[pl.ds(index * band, band)], held_ref.at[pl.ds(index * band, band)],
            arrived.at[index],
        )
        for index in range(count)
    ]
    for copy in copies:
        copy.start()
    lanes = lax.broadcasted_iota(jnp.int32, (128, 128), 1)
    for ids_ref, out_ref in ((true_ids, true_at), (sample_ids, sample_at)):
        for place in range(0, out_ref.shape[0], 128):
            ids = jnp.broadcast_to(ids_ref[:, place:place + 128], (128, 128)).T
            out_ref[place:place + 128] = ids - lanes
    for copy in copies:
        copy.wait()


def prepared(weight, true_ids, sample_ids, *earlier):
    near = pl.BlockSpec(memory_space=pltpu.VMEM)
    late = jax.ShapeDtypeStruct((true_ids.shape[1], 128), jnp.int32)
    return pl.pallas_call(
        prepare_kernel,
        in_specs=[pl.BlockSpec(memory_space=pltpu.HBM)] + [near] * (2 + len(earlier)),
        out_specs=[near] * 3,
        out_shape=[pltpu.VMEM(weight.shape, weight.dtype), late, late],
        scratch_shapes=[pltpu.SemaphoreType.DMA((4,))],
        compiler_params=pltpu.CompilerParams(vmem_limit_bytes=8 * 1024 * 1024),
        cost_estimate=BRIEF,
        name="prepared",
    )(pltpu.with_memory_space_constraint(weight, pltpu.HBM), true_ids, sample_ids, *earlier)


def logits_kernel(stat_rows, *refs):
    count = len(stat_rows)
    block_refs, refs = refs[:count], refs[count:]
    weight_ref, before_ref, exp_ref, stats_ref, rows, logits, scaled_exp, highs, sums, sent = refs
    tokens, columns = logits.shape
    length = tokens // count
    half = stats_ref.shape[0] // 2
    for index, ref in enumerate(block_refs):
        rows[index * length:(index + 1) * length] = ref[...]
    highs[...] = jnp.full(highs.shape, -jnp.inf, jnp.float32)
    width = min(256, columns)

    def multiply(index, carry):
        place = pl.ds(pl.multiple_of(index * width, width), width)
        part = jnp.dot(rows[...], weight_ref[:, place], preferred_element_type=jnp.float32)
        logits[:, place] = part
        high = functools.reduce(
            jnp.maximum, [part[:, lane:lane + 128] for lane in range(0, width, 128)]
        )
        highs[...] = jnp.maximum(highs[...], high)
        return carry

    lax.fori_loop(0, columns // width, multiply, 0)
    highs[...] = jnp.broadcast_to(jnp.max(highs[...], axis=1, keepdims=True), highs.shape)
    chunk = 16
    copies = []
    for block in range(count):

        def scale(index, carry, block=block):
            place = pl.ds(pl.multiple_of(block * length + index * chunk, chunk), chunk)
            peak = highs[place, :]
            total = jnp.zeros((chunk, 128), jnp.float32)
            for lane in range(0, columns, 128):
                scaled = jnp.exp(logits[place, lane:lane + 128] - peak)
                scaled_exp[place, lane:lane + 128] = scaled.astype(jnp.bfloat16)
                total += scaled
            sums[place, :] = total
            return carry

        lax.fori_loop(0, length // chunk, scale, 0, unroll=2)
        place = pl.ds(block * length, length)
        copies.append(
            pltpu.make_async_copy(scaled_exp.at[place], exp_ref.at[place], sent.at[block])
        )
        copies[-1].start()
    totals = jnp.broadcast_to(jnp.sum(sums[...], axis=1, keepdims=True), sums.shape)
    stats_ref[...] = before_ref[...]
    for base, values in ((0, highs[...].T[0:1]), (half, totals.T[0:1])):
        for index, row in enumerate(stat_rows):
            stats_ref[base + row:base + row + 1, :length] = (
                values[:, index * length:(index + 1) * length]
            )
    for copy in copies:
        copy.wait()


def round_logits(blocks, stat_rows, held_weight, before):
    depth, columns = held_weight.shape
    length = blocks[0].shape[0]
    tokens = length * len(blocks)
    near = pl.BlockSpec(memory_space=pltpu.VMEM)
    held_weight = pltpu.with_memory_space_constraint(held_weight, pltpu.VMEM)
    return pl.pallas_call(
        functools.partial(logits_kernel, stat_rows),
        in_specs=[near] * (len(blocks) + 2),
        out_specs=[pl.BlockSpec(memory_space=pltpu.HBM), near],
        out_shape=[
            pltpu.HBM((tokens, columns), jnp.bfloat16),
            jax.ShapeDtypeStruct(before.shape, jnp.float32),
        ],
        scratch_shapes=[
            pltpu.VMEM((tokens, depth), jnp.bfloat16),
            pltpu.VMEM((tokens, columns), jnp.float32),
            pltpu.VMEM((tokens, columns), jnp.bfloat16),
            pltpu.VMEM((tokens, 128), jnp.float32),
            pltpu.VMEM((tokens, 128), jnp.float32),
            pltpu.SemaphoreType.DMA((len(blocks),)),
        ],
        compiler_params=pltpu.CompilerParams(vmem_limit_bytes=LOGITS_VMEM),
        cost_estimate=BRIEF,
        name="round_logits",
    )(*blocks, held_weight, before)


def turn_kernel(count, rep_ref, *refs):
    mine_ref, other_ref = refs[count:]
    step = pl.program_id(0)
    turned = jnp.concatenate([ref[...] for ref in refs[:count]], axis=0).T

    @pl.when(step == 0)
    def _():
        mine_ref[...] = turned

    @pl.when(step == 1)
    def _():
        other_ref[...] = turned


def turned_features(rep, blocks, rows):
    length = blocks[0].shape[0]
    tokens = length * len(blocks)
    whole = pl.BlockSpec((rows, tokens), lambda step, rep_ref: (0, 0))
    block = pl.BlockSpec((length, rows), lambda step, rep_ref: (0, rep_ref[0] ^ step))
    return pl.pallas_call(
        functools.partial(turn_kernel, len(blocks)),
        grid_spec=pltpu.PrefetchScalarGridSpec(
            num_scalar_prefetch=1,
            grid=(2,),
            in_specs=[block] * len(blocks),
            out_specs=[whole, whole],
        ),
        out_shape=[jax.ShapeDtypeStruct((rows, tokens), jnp.bfloat16)] * 2,
        compiler_params=pltpu.CompilerParams(vmem_limit_bytes=20 * 1024 * 1024),
        cost_estimate=BRIEF,
        name="turned_features",
    )(rep, *blocks)


def one_hot_kernel(count, *refs):
    feature_refs, refs = refs[:count], refs[count:]
    true_ref, sample_ref, true_out, sample_out = refs
    width = true_out.shape[1]
    features = jnp.concatenate([ref[...] for ref in feature_refs], axis=1)
    columns = pl.program_id(0) * width + lax.broadcasted_iota(
        jnp.int32, (width, features.shape[1]), 0
    )
    hot = jnp.concatenate([columns == true_ref[...], columns == sample_ref[...]], axis=0)
    totals = lax.dot_general(
        features, hot.astype(jnp.float32).astype(jnp.bfloat16),
        (((1,), (1,)), ((), ())), preferred_element_type=jnp.float32,
    )
    true_out[...] = totals[:, :width].astype(jnp.bfloat16)
    sample_out[...] = totals[:, width:].astype(jnp.bfloat16)


def one_hot_sums(features, ids, columns):
    rows = features[0].shape[0]
    width = min(256, columns)
    whole = lambda array: pl.BlockSpec(array.shape, lambda step: (0, 0))
    tile = pl.BlockSpec((rows, width), lambda step: (0, step))
    return pl.pallas_call(
        functools.partial(one_hot_kernel, len(features)),
        grid=(columns // width,),
        in_specs=[whole(array) for array in (*features, *ids)],
        out_specs=[tile, tile],
        out_shape=[pltpu.HBM((rows, columns), jnp.bfloat16)] * 2,
        compiler_params=pltpu.CompilerParams(vmem_limit_bytes=24 * 1024 * 1024),
        cost_estimate=BRIEF,
        name="one_hot_sums",
    )(*features, *ids)


def merge_kernel(own_ref, across_ref, core_ref, both_ref, merged_ref, first_ref):
    rows = own_ref.shape[0] // 2
    side = rows // 2
    for core, (near, far) in enumerate(((own_ref, across_ref), (core_ref, both_ref))):
        place = core * rows
        first, total = near[:rows], near[rows:]
        second = jnp.concatenate([far[side:rows], far[:side]], axis=0)
        other = jnp.concatenate([far[rows + side:], far[rows:rows + side]], axis=0)
        peak = jnp.maximum(first, second)
        merged_ref[place:place + rows] = peak
        merged_ref[2 * rows + place:3 * rows + place] = (
            total * jnp.exp(first - peak) + other * jnp.exp(second - peak)
        )
        first_ref[place:place + rows] = first


def merged_stats(own, across, core, both):
    rows, lanes = own.shape
    return pl.pallas_call(
        merge_kernel,
        out_shape=[
            jax.ShapeDtypeStruct((2 * rows, lanes), jnp.float32),
            jax.ShapeDtypeStruct((rows, lanes), jnp.float32),
        ],
        compiler_params=pltpu.CompilerParams(vmem_limit_bytes=4 * 1024 * 1024),
        cost_estimate=BRIEF,
        name="merged_stats",
    )(own, across, core, both)


def refresh_kernel(lines, length, early_rows, late_rows, *refs):
    early_refs, late_refs, refs = refs[:2], refs[2:4], refs[4:]
    exp_refs, refs = refs[:8], refs[8:]
    stats_refs, refs = refs[:lines], refs[lines:]
    (first_ref, true_at, sample_at, true_sum, sample_sum, moment_ref, curvature_ref,
     moment_out, curvature_out, update_out, scaled, factors) = refs
    step = pl.program_id(0)
    width = moment_out.shape[1]
    early = len(early_rows) * length
    late = len(late_rows) * length

    @pl.when(step == 0)
    def _():
        rows = first_ref.shape[0]

        def turned(values, along):
            return jnp.concatenate([
                values[group + (turn + along) % lines:group + (turn + along) % lines + 1]
                for group in range(0, rows, lines) for turn in range(lines)
            ], axis=0) if along else values

        peaks = [turned(ref[:rows], along) for along, ref in enumerate(stats_refs)]
        totals = [turned(ref[rows:], along) for along, ref in enumerate(stats_refs)]
        peak = functools.reduce(jnp.maximum, peaks)
        total = sum(t * jnp.exp(p - peak) for p, t in zip(peaks, totals))
        factor = jnp.exp(first_ref[...] - peak) / total
        per_core = rows // 2
        for core in range(2):
            for index in range(0, len(early_rows), 2):
                pair = jnp.concatenate([
                    factor[core * per_core + row:core * per_core + row + 1, :length]
                    for row in early_rows[index:index + 2]
                ], axis=1)
                place = index * length
                values = early_refs[core][:, place:place + 2 * length].astype(jnp.float32)
                place += core * early
                scaled[:, place:place + 2 * length] = (values * pair).astype(jnp.bfloat16)
        full = jnp.concatenate([factor, jnp.zeros((128 - rows, 128), jnp.float32)], axis=0).T
        for core in range(2):
            for index, row in enumerate(late_rows):
                place = core * late + index * length
                at = core * per_core + row
                factors[place:place + length] = jnp.broadcast_to(
                    full[:length, at:at + 1], (length, 128)
                )

    shared = jnp.dot(
        scaled[...],
        jnp.concatenate([ref[...] for ref in exp_refs[:2] + exp_refs[4:6]], axis=0),
        preferred_element_type=jnp.float32,
    )
    gradient = shared - true_sum[...].astype(jnp.float32)
    sample_grad = shared - sample_sum[...].astype(jnp.float32)
    for core in range(2):
        place = slice(core * late, (core + 1) * late)
        exps = jnp.concatenate([ref[...] for ref in exp_refs[4 * core + 2:4 * core + 4]], axis=0)
        true_parts, sample_parts = [], []
        for lane in range(0, width, 128):
            probs = exps[:, lane:lane + 128].astype(jnp.float32) * factors[place]
            at = step * width + lane
            true_parts.append(
                (probs - jnp.where(true_at[place] == at, 1.0, 0.0)).astype(jnp.bfloat16)
            )
            sample_parts.append(
                (probs - jnp.where(sample_at[place] == at, 1.0, 0.0)).astype(jnp.bfloat16)
            )
        features = late_refs[core][...]
        gradient += jnp.dot(
            features, jnp.concatenate(true_parts, axis=1), preferred_element_type=jnp.float32
        )
        sample_grad += jnp.dot(
            features, jnp.concatenate(sample_parts, axis=1), preferred_element_type=jnp.float32
        )
    moment_out[...], curvature_out[...], update_out[...] = refresh(
        gradient, sample_grad, moment_ref[...], curvature_ref[...]
    )


def refresh_states(lines, length, early_rows, late_rows, early, late, exps, stats, first,
                   late_ids, sums, moment, curvature):
    rows, columns = moment.shape
    width = min(256, columns)
    late_tokens = 2 * late[0].shape[1]
    whole = lambda array: pl.BlockSpec(array.shape, lambda step: (0, 0))
    tile = pl.BlockSpec((rows, width), lambda step: (0, step))
    return pl.pallas_call(
        functools.partial(refresh_kernel, lines, length, early_rows, late_rows),
        grid=(columns // width,),
        in_specs=[whole(array) for array in (*early, *late)]
        + [pl.BlockSpec((array.shape[0], width), lambda step: (0, step)) for array in exps]
        + [whole(array) for array in (*stats, first, *late_ids)]
        + [tile] * 4,
        out_specs=[tile] * 3,
        out_shape=[jax.ShapeDtypeStruct((rows, columns), jnp.bfloat16)] * 3,
        scratch_shapes=[
            pltpu.VMEM((rows, 2 * early[0].shape[1]), jnp.bfloat16),
            pltpu.VMEM((late_tokens, 128), jnp.float32),
        ],
        compiler_params=pltpu.CompilerParams(vmem_limit_bytes=36 * 1024 * 1024),
        cost_estimate=BRIEF,
        name="refresh_states",
    )(
        *early, *late, *in_hbm(exps[:4]), *exps[4:], *stats, first, *late_ids,
        *in_hbm(sums, [moment, curvature])
    )


def in_hbm(*lists):
    return [pltpu.with_memory_space_constraint(array, pltpu.HBM) for array in sum(map(list, lists), [])]


def after(value, *others):
    return lax.optimization_barrier((value, *others))[0]


def all_tokens(reps, shards, hidden, norm_gain, input_ids, sampled_ids, head_weight, moment, curvature):
    lines = shards // 2
    length = hidden.shape[0]
    rows, columns = moment.shape
    rep = lax.axis_index("rep")
    shard = lax.axis_index("shard")
    first_col = shard * columns
    group_len = length * shards

    def to_x(values):
        return lax.ppermute(values, "rep", swap_pairs(reps, 2))

    def to_core(values):
        return lax.ppermute(values, "rep", swap_pairs(reps, 1))

    def to_y(values):
        return lax.ppermute(values, "shard", swap_pairs(shards, 1))

    def to_y_core(values):
        pairs = [
            (rep_at * shards + at, (rep_at ^ 1) * shards + (at ^ 1))
            for rep_at in range(reps) for at in range(shards)
        ]
        return lax.ppermute(values, ("rep", "shard"), pairs)

    def to_z(values, along):
        return lax.ppermute(values, "shard", shift_pairs(lines, along, 0))

    split = lines // 2
    plain = [(0, 0), (0, 1), (1, 0)]
    groups = [[(*kind, turn) for kind in plain] for turn in range(split)]
    groups += [[(*kind, turn) for turn in range(split, lines - 1) for kind in plain]]
    groups[-1] += [(0, 0, lines - 1)]
    groups += [[(0, 1, lines - 1), (1, 0, lines - 1)]]
    groups[-1] += [(1, 1, turn) for turn in range(lines)]
    early_blocks, late_blocks = sum(groups[:split], []), sum(groups[split:], [])

    def stat_row(block):
        return (2 * block[0] + block[1]) * lines + block[2]

    normed = normalize(hidden, norm_gain)

    last = jnp.arange(input_ids.shape[0]) % group_len == group_len - 1
    targets = jnp.where(last, -1, jnp.roll(input_ids, -1) - first_col)
    ids = jnp.stack([targets, sampled_ids - first_col]).reshape(2, reps * shards, length)
    side, across, turn = (np.array(values) for values in zip(*(early_blocks + late_blocks)))
    holder = (rep ^ (2 * across[None] + np.arange(2)[:, None])).reshape(-1)
    place = 2 * ((shard // 2 - turn) % lines) + ((shard % 2) ^ side)
    ids = jnp.take(ids, holder * shards + jnp.tile(place, 2), axis=1)
    ids = ids.reshape(2, 2, len(side), length)
    early_ids = ids[:, :, :len(early_blocks)].reshape(2, 1, -1)
    late_ids = ids[:, :, len(early_blocks):].reshape(2, 1, -1)
    early_ids, late_ids = [early_ids[0], early_ids[1]], [late_ids[0], late_ids[1]]
    rep_scalar = rep.astype(jnp.int32).reshape(1)
    stats = jnp.zeros((8 * lines, 128), jnp.float32)

    held = {(0, 0, 0): normed}
    exps = []

    def logits(group, stats, *gates):
        blocks = [held[block] for block in group]
        blocks[0] = after(blocks[0], *gates)
        exp, stats = round_logits(blocks, [stat_row(block) for block in group], head_weight, stats)
        exps.append(exp)
        return stats

    def diagonal(turn):
        if turn % 2 == 0:
            return to_x(held[1, 0, turn])
        return to_y(held[0, 1, turn])

    for turn in range(lines):
        block = held[0, 0, turn]
        held[0, 1, turn] = to_x(block)
        held[1, 0, turn] = to_y(block)
        if turn + 1 < lines:
            arrived = [to_z(block, 1), held[0, 1, turn], held[1, 0, turn]]
            if turn == 0:
                arrived += [*early_ids, *late_ids, rep_scalar, stats]
            else:
                arrived += exps
            arrived = lax.optimization_barrier(tuple(arrived))
            held[0, 0, turn + 1], held[0, 1, turn], held[1, 0, turn] = arrived[:3]
            if turn == 0:
                early_ids, late_ids = list(arrived[3:5]), list(arrived[5:7])
                rep_scalar, stats = arrived[7:]
                head_weight, *late_ids = prepared(head_weight, *late_ids, stats)
            early_exps = arrived[3:]
        if turn + 1 < lines:
            held[1, 1, turn] = diagonal(turn)
        if turn < split:
            stats = logits(groups[turn], stats, held[0, 0, turn + 1])

    early = [held[block] for block in early_blocks]
    early[0] = after(early[0], held[0, 0, split])
    early = turned_features(rep_scalar, early, rows)
    early = [early[0], to_core(early[1])]
    stats = logits(groups[split], stats, held[0, 0, lines - 1], early[1])
    held[0, 1, lines - 1] = after(held[0, 1, lines - 1], exps[split])
    held[1, 1, lines - 1] = diagonal(lines - 1)
    early_exps = lax.optimization_barrier((*early_exps, early[1]))[:split]
    other_exps = [to_core(exp) for exp in early_exps]
    early_ids[0] = after(early_ids[0], exps[split], held[0, 1, lines - 1], *other_exps)
    sums = one_hot_sums(early, early_ids, columns)
    stats = logits(groups[-1], stats, *sums)
    stats = after(stats, *other_exps)
    other_exps.append(to_core(after(exps[split], stats)))
    across_stats, core_stats, both_stats = to_y(stats), to_core(stats), to_y_core(stats)
    late = [held[block] for block in late_blocks]
    late[0] = after(late[0], stats)
    late = turned_features(rep_scalar, late, rows)
    merged, first = merged_stats(
        after(stats, *other_exps), across_stats, core_stats, both_stats
    )
    all_stats = [merged] + [to_z(merged, -along) for along in range(1, lines)]
    other_exps.append(to_core(after(exps[-1], merged)))
    late = [late[0], to_core(late[1])]
    return tuple(refresh_states(
        lines, length, [stat_row(block) for block in early_blocks],
        [stat_row(block) for block in late_blocks], early, late,
        exps + other_exps, all_stats, first, late_ids, sums, moment, curvature,
    ))


def solution(mesh):
    in_specs = (
        P(("rep", "shard"), None),
        P(),
        P(),
        P(),
        P(None, "shard"),
        P("rep", "shard"),
        P("rep", "shard"),
    )
    out_specs = (P("rep", "shard"), P("rep", "shard"), P("rep", "shard"))
    reps, shards = mesh.shape["rep"], mesh.shape["shard"]

    def whole(hidden, *others):
        tokens, depth = hidden.shape
        length = tokens // (reps * shards)
        fits = hidden.size * 2 <= GATHER_BYTES and reps == 4 and shards == 8
        if fits and length == 64 and (depth // reps) % 128 == 0:
            plan = functools.partial(all_tokens, reps, shards)
        else:
            plan = by_groups

        return jax.shard_map(
            plan, mesh=mesh, in_specs=in_specs, out_specs=out_specs, check_vma=False
        )(hidden, *others)

    return whole
```

```python
import functools

import jax
import jax.numpy as jnp
import numpy as np
from jax import lax
from jax.experimental import pallas as pl
from jax.experimental.pallas import tpu as pltpu
from jax.sharding import PartitionSpec as P

EPS_NORM = 1e-05
BETA_ONE = 0.96
BETA_TWO = 0.95
RHO_SCALE = 0.05
GATHER_BYTES = 32 * 1024 * 1024
LOGITS_VMEM = 20 * 1024 * 1024
BRIEF = pl.CostEstimate(flops=1024, bytes_accessed=1024, transcendentals=0)


def normalize(hidden, norm_gain):
    values = hidden.astype(jnp.float32)
    row_scale = lax.rsqrt(jnp.mean(values * values, axis=-1, keepdims=True) + EPS_NORM)
    return (values * row_scale * norm_gain).astype(jnp.bfloat16)


def refresh(gradient, sample_grad, moment, curvature):
    moment_new = BETA_ONE * moment.astype(jnp.float32) + (1.0 - BETA_ONE) * gradient
    curvature_new = (
        BETA_TWO * curvature.astype(jnp.float32) + (1.0 - BETA_TWO) * sample_grad * sample_grad
    )
    update_direction = jnp.clip(moment_new / (RHO_SCALE * curvature_new), -1.0, 1.0)
    return (
        moment_new.astype(jnp.bfloat16),
        curvature_new.astype(jnp.bfloat16),
        update_direction.astype(jnp.bfloat16),
    )


def by_groups(hidden, norm_gain, input_ids, sampled_ids, head_weight, moment, curvature):
    normed = normalize(hidden, norm_gain)
    gathered = lax.all_gather(normed, "shard", axis=0, tiled=True)
    group_len = gathered.shape[0]
    columns = head_weight.shape[1]
    first_col = lax.axis_index("shard") * columns
    logits = jnp.dot(gathered, head_weight, preferred_element_type=jnp.float32)
    row_peak = lax.pmax(jnp.max(logits, axis=-1), "shard")
    scaled_exp = jnp.exp(logits - row_peak[:, None])
    row_sum = lax.psum(jnp.sum(scaled_exp, axis=-1), "shard")
    probabilities = (scaled_exp / row_sum[:, None]).astype(jnp.bfloat16)
    group_start = lax.axis_index("rep") * group_len
    token_ids = lax.dynamic_slice_in_dim(input_ids, group_start, group_len, 0)
    sample_ids = lax.dynamic_slice_in_dim(sampled_ids, group_start, group_len, 0)
    position = jnp.arange(group_len)
    shifted = jnp.roll(token_ids, -1) - first_col
    usable = (position < group_len - 1) & (shifted >= 0) & (shifted < columns)
    true_slot = jnp.where(usable, shifted, columns)
    sample_local = sample_ids - first_col
    inside = (sample_local >= 0) & (sample_local < columns)
    sample_slot = jnp.where(inside, sample_local, columns)
    shared = lax.dot_general(
        gathered, probabilities, (((0,), (0,)), ((), ())), preferred_element_type=jnp.float32
    )
    widened = gathered.astype(jnp.float32)
    true_sums = jax.ops.segment_sum(widened, true_slot, num_segments=columns + 1)[:columns]
    sample_sums = jax.ops.segment_sum(widened, sample_slot, num_segments=columns + 1)[:columns]
    true_part = (shared - true_sums.T).astype(jnp.bfloat16)
    sample_part = (shared - sample_sums.T).astype(jnp.bfloat16)
    gradient = lax.psum_scatter(true_part, "rep", scatter_dimension=0, tiled=True)
    sample_grad = lax.psum_scatter(sample_part, "rep", scatter_dimension=0, tiled=True)
    return refresh(
        gradient.astype(jnp.float32), sample_grad.astype(jnp.float32), moment, curvature
    )


def swap_pairs(count, bit):
    return [(index, index ^ bit) for index in range(count)]


def shift_pairs(lines, along, across):
    pairs = []
    for place in range(lines):
        for side in range(2):
            source = 2 * place + side
            pairs.append((source, 2 * ((place + along) % lines) + (side ^ across)))
    return pairs


def prepare_kernel(weight_ref, true_ids, sample_ids, *refs):
    held_ref, true_at, sample_at, arrived = refs[-4:]
    count = arrived.shape[0]
    band = weight_ref.shape[0] // count
    copies = [
        pltpu.make_async_copy(
            weight_ref.at[pl.ds(index * band, band)], held_ref.at[pl.ds(index * band, band)],
            arrived.at[index],
        )
        for index in range(count)
    ]
    for copy in copies:
        copy.start()
    lanes = lax.broadcasted_iota(jnp.int32, (128, 128), 1)
    for ids_ref, out_ref in ((true_ids, true_at), (sample_ids, sample_at)):
        for place in range(0, out_ref.shape[0], 128):
            ids = jnp.broadcast_to(ids_ref[:, place:place + 128], (128, 128)).T
            out_ref[place:place + 128] = ids - lanes
    for copy in copies:
        copy.wait()


def prepared(weight, true_ids, sample_ids, *earlier):
    near = pl.BlockSpec(memory_space=pltpu.VMEM)
    late = jax.ShapeDtypeStruct((true_ids.shape[1], 128), jnp.int32)
    return pl.pallas_call(
        prepare_kernel,
        in_specs=[pl.BlockSpec(memory_space=pltpu.HBM)] + [near] * (2 + len(earlier)),
        out_specs=[near] * 3,
        out_shape=[pltpu.VMEM(weight.shape, weight.dtype), late, late],
        scratch_shapes=[pltpu.SemaphoreType.DMA((4,))],
        compiler_params=pltpu.CompilerParams(vmem_limit_bytes=8 * 1024 * 1024),
        cost_estimate=BRIEF,
        name="prepared",
    )(pltpu.with_memory_space_constraint(weight, pltpu.HBM), true_ids, sample_ids, *earlier)


def logits_kernel(stat_rows, first_row, joins, *refs):
    count = len(stat_rows)
    block_refs, refs = refs[:count], refs[count:]
    if joins:
        refs = refs[:2] + refs[3:]
    weight_ref, before_ref, exp_ref, stats_ref, rows, logits, scaled_exp, highs, sums, sent = refs
    tokens, columns = logits.shape
    length = tokens // count
    half = stats_ref.shape[0] // 2
    for index, ref in enumerate(block_refs):
        rows[index * length:(index + 1) * length] = ref[...]
    highs[...] = jnp.full(highs.shape, -jnp.inf, jnp.float32)
    width = min(256, columns)

    def multiply(index, carry):
        place = pl.ds(pl.multiple_of(index * width, width), width)
        part = jnp.dot(rows[...], weight_ref[:, place], preferred_element_type=jnp.float32)
        logits[:, place] = part
        high = functools.reduce(
            jnp.maximum, [part[:, lane:lane + 128] for lane in range(0, width, 128)]
        )
        highs[...] = jnp.maximum(highs[...], high)
        return carry

    lax.fori_loop(0, columns // width, multiply, 0)
    highs[...] = jnp.broadcast_to(jnp.max(highs[...], axis=1, keepdims=True), highs.shape)
    chunk = 16
    copies = []
    for block in range(count):

        def scale(index, carry, block=block):
            place = pl.ds(pl.multiple_of(block * length + index * chunk, chunk), chunk)
            peak = highs[place, :]
            total = jnp.zeros((chunk, 128), jnp.float32)
            for lane in range(0, columns, 128):
                scaled = jnp.exp(logits[place, lane:lane + 128] - peak)
                scaled_exp[place, lane:lane + 128] = scaled.astype(jnp.bfloat16)
                total += scaled
            sums[place, :] = total
            return carry

        lax.fori_loop(0, length // chunk, scale, 0, unroll=2)
        place = pl.ds(block * length, length)
        target = pl.ds(first_row + block * length, length)
        copies.append(
            pltpu.make_async_copy(scaled_exp.at[place], exp_ref.at[target], sent.at[block])
        )
        copies[-1].start()
    totals = jnp.broadcast_to(jnp.sum(sums[...], axis=1, keepdims=True), sums.shape)
    stats_ref[...] = before_ref[...]
    for base, values in ((0, highs[...].T[0:1]), (half, totals.T[0:1])):
        for index, row in enumerate(stat_rows):
            stats_ref[base + row:base + row + 1, :length] = (
                values[:, index * length:(index + 1) * length]
            )
    for copy in copies:
        copy.wait()


def round_logits(blocks, stat_rows, held_weight, before, first_row, exp_rows, into):
    depth, columns = held_weight.shape
    length = blocks[0].shape[0]
    tokens = length * len(blocks)
    near = pl.BlockSpec(memory_space=pltpu.VMEM)
    held_weight = pltpu.with_memory_space_constraint(held_weight, pltpu.VMEM)
    far = pl.BlockSpec(memory_space=pltpu.HBM)
    joins = [] if into is None else [pltpu.with_memory_space_constraint(into, pltpu.HBM)]
    return pl.pallas_call(
        functools.partial(logits_kernel, stat_rows, first_row, len(joins)),
        in_specs=[near] * (len(blocks) + 2) + [far] * len(joins),
        input_output_aliases={len(blocks) + 2: 0} if joins else {},
        out_specs=[far, near],
        out_shape=[
            pltpu.HBM((exp_rows, columns), jnp.bfloat16),
            jax.ShapeDtypeStruct(before.shape, jnp.float32),
        ],
        scratch_shapes=[
            pltpu.VMEM((tokens, depth), jnp.bfloat16),
            pltpu.VMEM((tokens, columns), jnp.float32),
            pltpu.VMEM((tokens, columns), jnp.bfloat16),
            pltpu.VMEM((tokens, 128), jnp.float32),
            pltpu.VMEM((tokens, 128), jnp.float32),
            pltpu.SemaphoreType.DMA((len(blocks),)),
        ],
        compiler_params=pltpu.CompilerParams(vmem_limit_bytes=LOGITS_VMEM),
        cost_estimate=BRIEF,
        name="round_logits",
    )(*blocks, held_weight, before, *joins)


def turn_kernel(count, rep_ref, *refs):
    mine_ref, other_ref = refs[count:]
    step = pl.program_id(0)
    turned = jnp.concatenate([ref[...] for ref in refs[:count]], axis=0).T

    @pl.when(step == 0)
    def _():
        mine_ref[...] = turned

    @pl.when(step == 1)
    def _():
        other_ref[...] = turned


def turned_features(rep, blocks, rows):
    length = blocks[0].shape[0]
    tokens = length * len(blocks)
    whole = pl.BlockSpec((rows, tokens), lambda step, rep_ref: (0, 0))
    block = pl.BlockSpec((length, rows), lambda step, rep_ref: (0, rep_ref[0] ^ step))
    return pl.pallas_call(
        functools.partial(turn_kernel, len(blocks)),
        grid_spec=pltpu.PrefetchScalarGridSpec(
            num_scalar_prefetch=1,
            grid=(2,),
            in_specs=[block] * len(blocks),
            out_specs=[whole, whole],
        ),
        out_shape=[jax.ShapeDtypeStruct((rows, tokens), jnp.bfloat16)] * 2,
        compiler_params=pltpu.CompilerParams(vmem_limit_bytes=20 * 1024 * 1024),
        cost_estimate=BRIEF,
        name="turned_features",
    )(rep, *blocks)


def one_hot_kernel(count, *refs):
    feature_refs, refs = refs[:count], refs[count:]
    true_ref, sample_ref, true_out, sample_out = refs
    width = true_out.shape[1]
    features = jnp.concatenate([ref[...] for ref in feature_refs], axis=1)
    columns = pl.program_id(0) * width + lax.broadcasted_iota(
        jnp.int32, (width, features.shape[1]), 0
    )
    hot = jnp.concatenate([columns == true_ref[...], columns == sample_ref[...]], axis=0)
    totals = lax.dot_general(
        features, hot.astype(jnp.float32).astype(jnp.bfloat16),
        (((1,), (1,)), ((), ())), preferred_element_type=jnp.float32,
    )
    true_out[...] = totals[:, :width].astype(jnp.bfloat16)
    sample_out[...] = totals[:, width:].astype(jnp.bfloat16)


def one_hot_sums(features, ids, columns):
    rows = features[0].shape[0]
    width = min(256, columns)
    whole = lambda array: pl.BlockSpec(array.shape, lambda step: (0, 0))
    tile = pl.BlockSpec((rows, width), lambda step: (0, step))
    return pl.pallas_call(
        functools.partial(one_hot_kernel, len(features)),
        grid=(columns // width,),
        in_specs=[whole(array) for array in (*features, *ids)],
        out_specs=[tile, tile],
        out_shape=[pltpu.HBM((rows, columns), jnp.bfloat16)] * 2,
        compiler_params=pltpu.CompilerParams(vmem_limit_bytes=24 * 1024 * 1024),
        cost_estimate=BRIEF,
        name="one_hot_sums",
    )(*features, *ids)


def merge_kernel(own_ref, across_ref, core_ref, both_ref, merged_ref, first_ref):
    rows = own_ref.shape[0] // 2
    side = rows // 2
    for core, (near, far) in enumerate(((own_ref, across_ref), (core_ref, both_ref))):
        place = core * rows
        first, total = near[:rows], near[rows:]
        second = jnp.concatenate([far[side:rows], far[:side]], axis=0)
        other = jnp.concatenate([far[rows + side:], far[rows:rows + side]], axis=0)
        peak = jnp.maximum(first, second)
        merged_ref[place:place + rows] = peak
        merged_ref[2 * rows + place:3 * rows + place] = (
            total * jnp.exp(first - peak) + other * jnp.exp(second - peak)
        )
        first_ref[place:place + rows] = first


def merged_stats(own, across, core, both):
    rows, lanes = own.shape
    return pl.pallas_call(
        merge_kernel,
        out_shape=[
            jax.ShapeDtypeStruct((2 * rows, lanes), jnp.float32),
            jax.ShapeDtypeStruct((rows, lanes), jnp.float32),
        ],
        compiler_params=pltpu.CompilerParams(vmem_limit_bytes=4 * 1024 * 1024),
        cost_estimate=BRIEF,
        name="merged_stats",
    )(own, across, core, both)


def refresh_kernel(lines, length, early_rows, late_rows, *refs):
    early_refs, late_refs, refs = refs[:2], refs[2:4], refs[4:]
    exp_refs, refs = refs[:6], refs[6:]
    stats_refs, refs = refs[:lines], refs[lines:]
    (first_ref, true_at, sample_at, true_sum, sample_sum, moment_ref, curvature_ref,
     moment_out, curvature_out, update_out, scaled, factors) = refs
    step = pl.program_id(0)
    width = moment_out.shape[1]
    early = len(early_rows) * length
    late = len(late_rows) * length

    @pl.when(step == 0)
    def _():
        rows = first_ref.shape[0]

        def turned(values, along):
            return jnp.concatenate([
                values[group + (turn + along) % lines:group + (turn + along) % lines + 1]
                for group in range(0, rows, lines) for turn in range(lines)
            ], axis=0) if along else values

        peaks = [turned(ref[:rows], along) for along, ref in enumerate(stats_refs)]
        totals = [turned(ref[rows:], along) for along, ref in enumerate(stats_refs)]
        peak = functools.reduce(jnp.maximum, peaks)
        total = sum(t * jnp.exp(p - peak) for p, t in zip(peaks, totals))
        factor = jnp.exp(first_ref[...] - peak) / total
        per_core = rows // 2
        for core in range(2):
            for index in range(0, len(early_rows), 2):
                pair = jnp.concatenate([
                    factor[core * per_core + row:core * per_core + row + 1, :length]
                    for row in early_rows[index:index + 2]
                ], axis=1)
                place = index * length
                values = early_refs[core][:, place:place + 2 * length].astype(jnp.float32)
                place += core * early
                scaled[:, place:place + 2 * length] = (values * pair).astype(jnp.bfloat16)
        full = jnp.concatenate([factor, jnp.zeros((128 - rows, 128), jnp.float32)], axis=0).T
        for core in range(2):
            for index, row in enumerate(late_rows):
                place = core * late + index * length
                at = core * per_core + row
                factors[place:place + length] = jnp.broadcast_to(
                    full[:length, at:at + 1], (length, 128)
                )

    shared = jnp.dot(
        scaled[...],
        jnp.concatenate([exp_refs[0][...], exp_refs[3][...]], axis=0),
        preferred_element_type=jnp.float32,
    )
    gradient = shared - true_sum[...].astype(jnp.float32)
    sample_grad = shared - sample_sum[...].astype(jnp.float32)
    for core in range(2):
        place = slice(core * late, (core + 1) * late)
        exps = jnp.concatenate([ref[...] for ref in exp_refs[3 * core + 1:3 * core + 3]], axis=0)
        true_parts, sample_parts = [], []
        for lane in range(0, width, 128):
            probs = exps[:, lane:lane + 128].astype(jnp.float32) * factors[place]
            at = step * width + lane
            true_parts.append(
                (probs - jnp.where(true_at[place] == at, 1.0, 0.0)).astype(jnp.bfloat16)
            )
            sample_parts.append(
                (probs - jnp.where(sample_at[place] == at, 1.0, 0.0)).astype(jnp.bfloat16)
            )
        features = late_refs[core][...]
        gradient += jnp.dot(
            features, jnp.concatenate(true_parts, axis=1), preferred_element_type=jnp.float32
        )
        sample_grad += jnp.dot(
            features, jnp.concatenate(sample_parts, axis=1), preferred_element_type=jnp.float32
        )
    moment_out[...], curvature_out[...], update_out[...] = refresh(
        gradient, sample_grad, moment_ref[...], curvature_ref[...]
    )


def refresh_states(lines, length, early_rows, late_rows, early, late, exps, stats, first,
                   late_ids, sums, moment, curvature):
    rows, columns = moment.shape
    width = min(256, columns)
    late_tokens = 2 * late[0].shape[1]
    whole = lambda array: pl.BlockSpec(array.shape, lambda step: (0, 0))
    tile = pl.BlockSpec((rows, width), lambda step: (0, step))
    return pl.pallas_call(
        functools.partial(refresh_kernel, lines, length, early_rows, late_rows),
        grid=(columns // width,),
        in_specs=[whole(array) for array in (*early, *late)]
        + [pl.BlockSpec((array.shape[0], width), lambda step: (0, step)) for array in exps]
        + [whole(array) for array in (*stats, first, *late_ids)]
        + [tile] * 4,
        out_specs=[tile] * 3,
        out_shape=[jax.ShapeDtypeStruct((rows, columns), jnp.bfloat16)] * 3,
        scratch_shapes=[
            pltpu.VMEM((rows, 2 * early[0].shape[1]), jnp.bfloat16),
            pltpu.VMEM((late_tokens, 128), jnp.float32),
        ],
        compiler_params=pltpu.CompilerParams(vmem_limit_bytes=36 * 1024 * 1024),
        cost_estimate=BRIEF,
        name="refresh_states",
    )(
        *early, *late, *in_hbm(exps[:3]), *exps[3:], *stats, first, *late_ids,
        *in_hbm(sums, [moment, curvature])
    )


def in_hbm(*lists):
    return [pltpu.with_memory_space_constraint(array, pltpu.HBM) for array in sum(map(list, lists), [])]


def after(value, *others):
    return lax.optimization_barrier((value, *others))[0]


def all_tokens(reps, shards, hidden, norm_gain, input_ids, sampled_ids, head_weight, moment, curvature):
    lines = shards // 2
    length = hidden.shape[0]
    rows, columns = moment.shape
    rep = lax.axis_index("rep")
    shard = lax.axis_index("shard")
    first_col = shard * columns
    group_len = length * shards

    def to_x(values):
        return lax.ppermute(values, "rep", swap_pairs(reps, 2))

    def to_core(values):
        return lax.ppermute(values, "rep", swap_pairs(reps, 1))

    def to_y(values):
        return lax.ppermute(values, "shard", swap_pairs(shards, 1))

    def to_y_core(values):
        pairs = [
            (rep_at * shards + at, (rep_at ^ 1) * shards + (at ^ 1))
            for rep_at in range(reps) for at in range(shards)
        ]
        return lax.ppermute(values, ("rep", "shard"), pairs)

    def to_z(values, along):
        return lax.ppermute(values, "shard", shift_pairs(lines, along, 0))

    split = lines // 2
    plain = [(0, 0), (0, 1), (1, 0)]
    groups = [[(*kind, turn) for kind in plain] for turn in range(split)]
    groups += [[(*kind, turn) for turn in range(split, lines - 1) for kind in plain]]
    groups[-1] += [(0, 0, lines - 1)] + [(1, 1, turn) for turn in range(split)]
    groups += [[(0, 1, lines - 1), (1, 0, lines - 1)]]
    groups[-1] += [(1, 1, turn) for turn in range(split, lines)]
    early_blocks, late_blocks = sum(groups[:split], []), sum(groups[split:], [])

    def stat_row(block):
        return (2 * block[0] + block[1]) * lines + block[2]

    normed = normalize(hidden, norm_gain)

    last = jnp.arange(input_ids.shape[0]) % group_len == group_len - 1
    targets = jnp.where(last, -1, jnp.roll(input_ids, -1) - first_col)
    ids = jnp.stack([targets, sampled_ids - first_col]).reshape(2, reps * shards, length)
    side, across, turn = (np.array(values) for values in zip(*(early_blocks + late_blocks)))
    holder = (rep ^ (2 * across[None] + np.arange(2)[:, None])).reshape(-1)
    place = 2 * ((shard // 2 - turn) % lines) + ((shard % 2) ^ side)
    ids = jnp.take(ids, holder * shards + jnp.tile(place, 2), axis=1)
    ids = ids.reshape(2, 2, len(side), length)
    early_ids = ids[:, :, :len(early_blocks)].reshape(2, 1, -1)
    late_ids = ids[:, :, len(early_blocks):].reshape(2, 1, -1)
    early_ids, late_ids = [early_ids[0], early_ids[1]], [late_ids[0], late_ids[1]]
    rep_scalar = rep.astype(jnp.int32).reshape(1)
    stats = jnp.zeros((8 * lines, 128), jnp.float32)

    held = {(0, 0, 0): normed}
    early_exp = None

    def logits(group, stats, *gates, first_row=0, exp_rows=None, into=None):
        blocks = [held[block] for block in group]
        blocks[0] = after(blocks[0], *gates)
        rows = [stat_row(block) for block in group]
        exp_rows = exp_rows or len(group) * length
        return round_logits(blocks, rows, head_weight, stats, first_row, exp_rows, into)

    def diagonal(turn):
        if turn % 2 == 0:
            return to_x(held[1, 0, turn])
        return to_y(held[0, 1, turn])

    for turn in range(lines):
        block = held[0, 0, turn]
        held[0, 1, turn] = to_x(block)
        held[1, 0, turn] = to_y(block)
        if turn + 1 < lines:
            arrived = [to_z(block, 1), held[0, 1, turn], held[1, 0, turn]]
            if turn == 0:
                arrived += [*early_ids, *late_ids, rep_scalar, stats]
            elif turn < split:
                arrived += [early_exp]
            else:
                arrived += [early_exp] + [held[1, 1, past] for past in range(split)]
            arrived = lax.optimization_barrier(tuple(arrived))
            held[0, 0, turn + 1], held[0, 1, turn], held[1, 0, turn] = arrived[:3]
            if turn == 0:
                early_ids, late_ids = list(arrived[3:5]), list(arrived[5:7])
                rep_scalar, stats = arrived[7:]
                head_weight, *late_ids = prepared(head_weight, *late_ids, stats)
            else:
                early_exp = arrived[3]
                held.update({(1, 1, past): got for past, got in enumerate(arrived[4:])})
            held[1, 1, turn] = diagonal(turn)
        if turn < split:
            size = len(groups[turn]) * length
            early_exp, stats = logits(
                groups[turn], stats, held[0, 0, turn + 1],
                first_row=turn * size, exp_rows=split * size, into=early_exp,
            )

    early = [held[block] for block in early_blocks]
    early[0] = after(early[0], held[0, 0, lines - 1])
    early = turned_features(rep_scalar, early, rows)
    early = [early[0], to_core(early[1])]
    other_exps = [to_core(early_exp)]
    middle_exp, stats = logits(groups[split], stats, held[0, 0, lines - 1])
    held[0, 1, lines - 1] = after(held[0, 1, lines - 1], middle_exp)
    held[1, 1, lines - 1] = diagonal(lines - 1)
    early_ids[0] = after(early_ids[0], middle_exp, held[0, 1, lines - 1], *other_exps)
    sums = one_hot_sums(early, early_ids, columns)
    last_exp, stats = logits(groups[-1], stats, *sums)
    exps = [early_exp, middle_exp, last_exp]
    stats = after(stats, *other_exps)
    other_exps.append(to_core(after(middle_exp, stats)))
    across_stats, core_stats, both_stats = to_y(stats), to_core(stats), to_y_core(stats)
    late = [held[block] for block in late_blocks]
    late[0] = after(late[0], stats)
    late = turned_features(rep_scalar, late, rows)
    merged, first = merged_stats(
        after(stats, *other_exps), across_stats, core_stats, both_stats
    )
    all_stats = [merged] + [to_z(merged, -along) for along in range(1, lines)]
    other_exps.append(to_core(after(last_exp, merged)))
    late = [late[0], to_core(late[1])]
    return tuple(refresh_states(
        lines, length, [stat_row(block) for block in early_blocks],
        [stat_row(block) for block in late_blocks], early, late,
        exps + other_exps, all_stats, first, late_ids, sums, moment, curvature,
    ))


def solution(mesh):
    in_specs = (
        P(("rep", "shard"), None),
        P(),
        P(),
        P(),
        P(None, "shard"),
        P("rep", "shard"),
        P("rep", "shard"),
    )
    out_specs = (P("rep", "shard"), P("rep", "shard"), P("rep", "shard"))
    reps, shards = mesh.shape["rep"], mesh.shape["shard"]

    def whole(hidden, *others):
        tokens, depth = hidden.shape
        length = tokens // (reps * shards)
        fits = hidden.size * 2 <= GATHER_BYTES and reps == 4 and shards == 8
        if fits and length == 64 and (depth // reps) % 128 == 0:
            plan = functools.partial(all_tokens, reps, shards)
        else:
            plan = by_groups

        return jax.shard_map(
            plan, mesh=mesh, in_specs=in_specs, out_specs=out_specs, check_vma=False
        )(hidden, *others)

    return whole
```

```python
import functools

import jax
import jax.numpy as jnp
import numpy as np
from jax import lax
from jax.experimental import pallas as pl
from jax.experimental.pallas import tpu as pltpu
from jax.sharding import PartitionSpec as P

EPS_NORM = 1e-05
BETA_ONE = 0.96
BETA_TWO = 0.95
RHO_SCALE = 0.05
GATHER_BYTES = 32 * 1024 * 1024
LOGITS_VMEM = 20 * 1024 * 1024
BRIEF = pl.CostEstimate(flops=1024, bytes_accessed=1024, transcendentals=0)


def normalize(hidden, norm_gain):
    values = hidden.astype(jnp.float32)
    row_scale = lax.rsqrt(jnp.mean(values * values, axis=-1, keepdims=True) + EPS_NORM)
    return (values * row_scale * norm_gain).astype(jnp.bfloat16)


def refresh(gradient, sample_grad, moment, curvature):
    moment_new = BETA_ONE * moment.astype(jnp.float32) + (1.0 - BETA_ONE) * gradient
    curvature_new = (
        BETA_TWO * curvature.astype(jnp.float32) + (1.0 - BETA_TWO) * sample_grad * sample_grad
    )
    update_direction = jnp.clip(moment_new / (RHO_SCALE * curvature_new), -1.0, 1.0)
    return (
        moment_new.astype(jnp.bfloat16),
        curvature_new.astype(jnp.bfloat16),
        update_direction.astype(jnp.bfloat16),
    )


def by_groups(hidden, norm_gain, input_ids, sampled_ids, head_weight, moment, curvature):
    normed = normalize(hidden, norm_gain)
    gathered = lax.all_gather(normed, "shard", axis=0, tiled=True)
    group_len = gathered.shape[0]
    columns = head_weight.shape[1]
    first_col = lax.axis_index("shard") * columns
    logits = jnp.dot(gathered, head_weight, preferred_element_type=jnp.float32)
    row_peak = lax.pmax(jnp.max(logits, axis=-1), "shard")
    scaled_exp = jnp.exp(logits - row_peak[:, None])
    row_sum = lax.psum(jnp.sum(scaled_exp, axis=-1), "shard")
    probabilities = (scaled_exp / row_sum[:, None]).astype(jnp.bfloat16)
    group_start = lax.axis_index("rep") * group_len
    token_ids = lax.dynamic_slice_in_dim(input_ids, group_start, group_len, 0)
    sample_ids = lax.dynamic_slice_in_dim(sampled_ids, group_start, group_len, 0)
    position = jnp.arange(group_len)
    shifted = jnp.roll(token_ids, -1) - first_col
    usable = (position < group_len - 1) & (shifted >= 0) & (shifted < columns)
    true_slot = jnp.where(usable, shifted, columns)
    sample_local = sample_ids - first_col
    inside = (sample_local >= 0) & (sample_local < columns)
    sample_slot = jnp.where(inside, sample_local, columns)
    shared = lax.dot_general(
        gathered, probabilities, (((0,), (0,)), ((), ())), preferred_element_type=jnp.float32
    )
    widened = gathered.astype(jnp.float32)
    true_sums = jax.ops.segment_sum(widened, true_slot, num_segments=columns + 1)[:columns]
    sample_sums = jax.ops.segment_sum(widened, sample_slot, num_segments=columns + 1)[:columns]
    true_part = (shared - true_sums.T).astype(jnp.bfloat16)
    sample_part = (shared - sample_sums.T).astype(jnp.bfloat16)
    gradient = lax.psum_scatter(true_part, "rep", scatter_dimension=0, tiled=True)
    sample_grad = lax.psum_scatter(sample_part, "rep", scatter_dimension=0, tiled=True)
    return refresh(
        gradient.astype(jnp.float32), sample_grad.astype(jnp.float32), moment, curvature
    )


def swap_pairs(count, bit):
    return [(index, index ^ bit) for index in range(count)]


def shift_pairs(lines, along, across):
    pairs = []
    for place in range(lines):
        for side in range(2):
            source = 2 * place + side
            pairs.append((source, 2 * ((place + along) % lines) + (side ^ across)))
    return pairs


def prepare_kernel(weight_ref, true_ids, sample_ids, *refs):
    held_ref, true_at, sample_at, arrived = refs[-4:]
    count = arrived.shape[0]
    band = weight_ref.shape[0] // count
    copies = [
        pltpu.make_async_copy(
            weight_ref.at[pl.ds(index * band, band)], held_ref.at[pl.ds(index * band, band)],
            arrived.at[index],
        )
        for index in range(count)
    ]
    for copy in copies:
        copy.start()
    lanes = lax.broadcasted_iota(jnp.int32, (128, 128), 1)
    for ids_ref, out_ref in ((true_ids, true_at), (sample_ids, sample_at)):
        for place in range(0, out_ref.shape[0], 128):
            ids = jnp.broadcast_to(ids_ref[:, place:place + 128], (128, 128)).T
            out_ref[place:place + 128] = ids - lanes
    for copy in copies:
        copy.wait()


def prepared(weight, true_ids, sample_ids, *earlier):
    near = pl.BlockSpec(memory_space=pltpu.VMEM)
    late = jax.ShapeDtypeStruct((true_ids.shape[1], 128), jnp.int32)
    return pl.pallas_call(
        prepare_kernel,
        in_specs=[pl.BlockSpec(memory_space=pltpu.HBM)] + [near] * (2 + len(earlier)),
        out_specs=[near] * 3,
        out_shape=[pltpu.VMEM(weight.shape, weight.dtype), late, late],
        scratch_shapes=[pltpu.SemaphoreType.DMA((4,))],
        compiler_params=pltpu.CompilerParams(vmem_limit_bytes=8 * 1024 * 1024),
        cost_estimate=BRIEF,
        name="prepared",
    )(pltpu.with_memory_space_constraint(weight, pltpu.HBM), true_ids, sample_ids, *earlier)


def logits_kernel(stat_rows, first_row, joins, *refs):
    count = len(stat_rows)
    block_refs, refs = refs[:count], refs[count:]
    if joins:
        refs = refs[:2] + refs[3:]
    weight_ref, before_ref, exp_ref, stats_ref, rows, logits, scaled_exp, highs, sums, sent = refs
    tokens, columns = logits.shape
    length = tokens // count
    half = stats_ref.shape[0] // 2
    for index, ref in enumerate(block_refs):
        rows[index * length:(index + 1) * length] = ref[...]
    highs[...] = jnp.full(highs.shape, -jnp.inf, jnp.float32)
    width = min(256, columns)

    def multiply(index, carry):
        place = pl.ds(pl.multiple_of(index * width, width), width)
        part = jnp.dot(rows[...], weight_ref[:, place], preferred_element_type=jnp.float32)
        logits[:, place] = part
        high = functools.reduce(
            jnp.maximum, [part[:, lane:lane + 128] for lane in range(0, width, 128)]
        )
        highs[...] = jnp.maximum(highs[...], high)
        return carry

    lax.fori_loop(0, columns // width, multiply, 0)
    highs[...] = jnp.broadcast_to(jnp.max(highs[...], axis=1, keepdims=True), highs.shape)
    chunk = 16
    copies = []
    for block in range(count):

        def scale(index, carry, block=block):
            place = pl.ds(pl.multiple_of(block * length + index * chunk, chunk), chunk)
            peak = highs[place, :]
            total = jnp.zeros((chunk, 128), jnp.float32)
            for lane in range(0, columns, 128):
                scaled = jnp.exp(logits[place, lane:lane + 128] - peak)
                scaled_exp[place, lane:lane + 128] = scaled.astype(jnp.bfloat16)
                total += scaled
            sums[place, :] = total
            return carry

        lax.fori_loop(0, length // chunk, scale, 0, unroll=2)
        place = pl.ds(block * length, length)
        target = pl.ds(first_row + block * length, length)
        copies.append(
            pltpu.make_async_copy(scaled_exp.at[place], exp_ref.at[target], sent.at[block])
        )
        copies[-1].start()
    totals = jnp.broadcast_to(jnp.sum(sums[...], axis=1, keepdims=True), sums.shape)
    stats_ref[...] = before_ref[...]
    for base, values in ((0, highs[...].T[0:1]), (half, totals.T[0:1])):
        for index, row in enumerate(stat_rows):
            stats_ref[base + row:base + row + 1, :length] = (
                values[:, index * length:(index + 1) * length]
            )
    for copy in copies:
        copy.wait()


def round_logits(blocks, stat_rows, held_weight, before, first_row, exp_rows, into):
    depth, columns = held_weight.shape
    length = blocks[0].shape[0]
    tokens = length * len(blocks)
    near = pl.BlockSpec(memory_space=pltpu.VMEM)
    held_weight = pltpu.with_memory_space_constraint(held_weight, pltpu.VMEM)
    far = pl.BlockSpec(memory_space=pltpu.HBM)
    joins = [] if into is None else [pltpu.with_memory_space_constraint(into, pltpu.HBM)]
    return pl.pallas_call(
        functools.partial(logits_kernel, stat_rows, first_row, len(joins)),
        in_specs=[near] * (len(blocks) + 2) + [far] * len(joins),
        input_output_aliases={len(blocks) + 2: 0} if joins else {},
        out_specs=[far, near],
        out_shape=[
            pltpu.HBM((exp_rows, columns), jnp.bfloat16),
            jax.ShapeDtypeStruct(before.shape, jnp.float32),
        ],
        scratch_shapes=[
            pltpu.VMEM((tokens, depth), jnp.bfloat16),
            pltpu.VMEM((tokens, columns), jnp.float32),
            pltpu.VMEM((tokens, columns), jnp.bfloat16),
            pltpu.VMEM((tokens, 128), jnp.float32),
            pltpu.VMEM((tokens, 128), jnp.float32),
            pltpu.SemaphoreType.DMA((len(blocks),)),
        ],
        compiler_params=pltpu.CompilerParams(vmem_limit_bytes=LOGITS_VMEM),
        cost_estimate=BRIEF,
        name="round_logits",
    )(*blocks, held_weight, before, *joins)


def turn_kernel(count, rep_ref, *refs):
    mine_ref, other_ref = refs[count:]
    step = pl.program_id(0)
    turned = jnp.concatenate([ref[...] for ref in refs[:count]], axis=0).T

    @pl.when(step == 0)
    def _():
        mine_ref[...] = turned

    @pl.when(step == 1)
    def _():
        other_ref[...] = turned


def turned_features(rep, blocks, rows):
    length = blocks[0].shape[0]
    tokens = length * len(blocks)
    whole = pl.BlockSpec((rows, tokens), lambda step, rep_ref: (0, 0))
    block = pl.BlockSpec((length, rows), lambda step, rep_ref: (0, rep_ref[0] ^ step))
    return pl.pallas_call(
        functools.partial(turn_kernel, len(blocks)),
        grid_spec=pltpu.PrefetchScalarGridSpec(
            num_scalar_prefetch=1,
            grid=(2,),
            in_specs=[block] * len(blocks),
            out_specs=[whole, whole],
        ),
        out_shape=[jax.ShapeDtypeStruct((rows, tokens), jnp.bfloat16)] * 2,
        compiler_params=pltpu.CompilerParams(vmem_limit_bytes=20 * 1024 * 1024),
        cost_estimate=BRIEF,
        name="turned_features",
    )(rep, *blocks)


def one_hot_kernel(count, *refs):
    feature_refs, refs = refs[:count], refs[count:]
    true_ref, sample_ref, true_out, sample_out = refs
    width = true_out.shape[1]
    features = jnp.concatenate([ref[...] for ref in feature_refs], axis=1)
    columns = pl.program_id(0) * width + lax.broadcasted_iota(
        jnp.int32, (width, features.shape[1]), 0
    )
    hot = jnp.concatenate([columns == true_ref[...], columns == sample_ref[...]], axis=0)
    totals = lax.dot_general(
        features, hot.astype(jnp.float32).astype(jnp.bfloat16),
        (((1,), (1,)), ((), ())), preferred_element_type=jnp.float32,
    )
    true_out[...] = totals[:, :width].astype(jnp.bfloat16)
    sample_out[...] = totals[:, width:].astype(jnp.bfloat16)


def one_hot_sums(features, ids, columns):
    rows = features[0].shape[0]
    width = min(256, columns)
    whole = lambda array: pl.BlockSpec(array.shape, lambda step: (0, 0))
    tile = pl.BlockSpec((rows, width), lambda step: (0, step))
    return pl.pallas_call(
        functools.partial(one_hot_kernel, len(features)),
        grid=(columns // width,),
        in_specs=[whole(array) for array in (*features, *ids)],
        out_specs=[tile, tile],
        out_shape=[pltpu.HBM((rows, columns), jnp.bfloat16)] * 2,
        compiler_params=pltpu.CompilerParams(vmem_limit_bytes=24 * 1024 * 1024),
        cost_estimate=BRIEF,
        name="one_hot_sums",
    )(*features, *ids)


def merge_kernel(own_ref, across_ref, core_ref, both_ref, merged_ref, first_ref):
    rows = own_ref.shape[0] // 2
    side = rows // 2
    for core, (near, far) in enumerate(((own_ref, across_ref), (core_ref, both_ref))):
        place = core * rows
        first, total = near[:rows], near[rows:]
        second = jnp.concatenate([far[side:rows], far[:side]], axis=0)
        other = jnp.concatenate([far[rows + side:], far[rows:rows + side]], axis=0)
        peak = jnp.maximum(first, second)
        merged_ref[place:place + rows] = peak
        merged_ref[2 * rows + place:3 * rows + place] = (
            total * jnp.exp(first - peak) + other * jnp.exp(second - peak)
        )
        first_ref[place:place + rows] = first


def merged_stats(own, across, core, both):
    rows, lanes = own.shape
    return pl.pallas_call(
        merge_kernel,
        out_shape=[
            jax.ShapeDtypeStruct((2 * rows, lanes), jnp.float32),
            jax.ShapeDtypeStruct((rows, lanes), jnp.float32),
        ],
        compiler_params=pltpu.CompilerParams(vmem_limit_bytes=4 * 1024 * 1024),
        cost_estimate=BRIEF,
        name="merged_stats",
    )(own, across, core, both)


def refresh_kernel(lines, length, block_rows, *refs):
    early_refs, late_refs, refs = refs[:2], refs[2:4], refs[4:]
    exp_refs, refs = refs[:6], refs[6:]
    stats_refs, refs = refs[:lines], refs[lines:]
    (first_ref, true_at, sample_at, true_sum, sample_sum, moment_ref, curvature_ref,
     moment_out, curvature_out, update_out, factors) = refs
    step = pl.program_id(0)
    width = moment_out.shape[1]
    early = early_refs[0].shape[1]
    late = late_refs[0].shape[1]

    @pl.when(step == 0)
    def _():
        rows = first_ref.shape[0]

        def turned(values, along):
            return jnp.concatenate([
                values[group + (turn + along) % lines:group + (turn + along) % lines + 1]
                for group in range(0, rows, lines) for turn in range(lines)
            ], axis=0) if along else values

        peaks = [turned(ref[:rows], along) for along, ref in enumerate(stats_refs)]
        totals = [turned(ref[rows:], along) for along, ref in enumerate(stats_refs)]
        peak = functools.reduce(jnp.maximum, peaks)
        total = sum(t * jnp.exp(p - peak) for p, t in zip(peaks, totals))
        factor = jnp.exp(first_ref[...] - peak) / total
        per_core = rows // 2
        full = jnp.concatenate([factor, jnp.zeros((128 - rows, 128), jnp.float32)], axis=0).T
        for core in range(2):
            for index, row in enumerate(block_rows):
                place = (core * len(block_rows) + index) * length
                at = core * per_core + row
                factors[place:place + length] = jnp.broadcast_to(
                    full[:length, at:at + 1], (length, 128)
                )

    def probs(ref, place, lane):
        scale = factors[place:place + ref.shape[0]]
        return ref[:, lane:lane + 128].astype(jnp.float32) * scale

    early_sides, true_sides, sample_sides = [], [], []
    for core in range(2):
        first_exp, *late_exps = exp_refs[3 * core:3 * core + 3]
        place = core * (early + late)
        early_sides.append(jnp.concatenate([
            probs(first_exp, place, lane).astype(jnp.bfloat16) for lane in range(0, width, 128)
        ], axis=1))
        place += early
        at = core * late
        for ref in late_exps:
            rows = slice(at, at + ref.shape[0])
            true_parts, sample_parts = [], []
            for lane in range(0, width, 128):
                prob = probs(ref, place, lane)
                column = step * width + lane
                true_hot = jnp.where(true_at[rows] == column, 1.0, 0.0)
                sample_hot = jnp.where(sample_at[rows] == column, 1.0, 0.0)
                true_parts.append((prob - true_hot).astype(jnp.bfloat16))
                sample_parts.append((prob - sample_hot).astype(jnp.bfloat16))
            true_sides.append(jnp.concatenate(true_parts, axis=1))
            sample_sides.append(jnp.concatenate(sample_parts, axis=1))
            place += ref.shape[0]
            at += ref.shape[0]
    early_features = jnp.concatenate([ref[...] for ref in early_refs], axis=1)
    late_features = jnp.concatenate([ref[...] for ref in late_refs], axis=1)

    def product(features, sides):
        return jnp.dot(
            features, jnp.concatenate(sides, axis=0), preferred_element_type=jnp.float32
        )

    shared = product(early_features, early_sides)
    gradient = product(late_features, true_sides) + (shared - true_sum[...].astype(jnp.float32))
    sample_grad = product(late_features, sample_sides) + (
        shared - sample_sum[...].astype(jnp.float32)
    )
    moment_out[...], curvature_out[...], update_out[...] = refresh(
        gradient, sample_grad, moment_ref[...], curvature_ref[...]
    )


def refresh_states(lines, length, block_rows, early, late, exps, stats, first,
                   late_ids, sums, moment, curvature):
    rows, columns = moment.shape
    width = min(256, columns)
    whole = lambda array: pl.BlockSpec(array.shape, lambda step: (0, 0))
    tile = pl.BlockSpec((rows, width), lambda step: (0, step))
    return pl.pallas_call(
        functools.partial(refresh_kernel, lines, length, block_rows),
        grid=(columns // width,),
        in_specs=[whole(array) for array in (*early, *late)]
        + [pl.BlockSpec((array.shape[0], width), lambda step: (0, step)) for array in exps]
        + [whole(array) for array in (*stats, first, *late_ids)]
        + [tile] * 4,
        out_specs=[tile] * 3,
        out_shape=[jax.ShapeDtypeStruct((rows, columns), jnp.bfloat16)] * 3,
        scratch_shapes=[pltpu.VMEM((2 * length * len(block_rows), 128), jnp.float32)],
        compiler_params=pltpu.CompilerParams(vmem_limit_bytes=36 * 1024 * 1024),
        cost_estimate=BRIEF,
        name="refresh_states",
    )(
        *early, *late, *in_hbm(exps[:3]), *exps[3:], *stats, first, *late_ids,
        *in_hbm(sums, [moment, curvature])
    )


def in_hbm(*lists):
    return [pltpu.with_memory_space_constraint(array, pltpu.HBM) for array in sum(map(list, lists), [])]


def after(value, *others):
    return lax.optimization_barrier((value, *others))[0]


def all_tokens(reps, shards, hidden, norm_gain, input_ids, sampled_ids, head_weight, moment, curvature):
    lines = shards // 2
    length = hidden.shape[0]
    rows, columns = moment.shape
    rep = lax.axis_index("rep")
    shard = lax.axis_index("shard")
    first_col = shard * columns
    group_len = length * shards

    def to_x(values):
        return lax.ppermute(values, "rep", swap_pairs(reps, 2))

    def to_core(values):
        return lax.ppermute(values, "rep", swap_pairs(reps, 1))

    def to_y(values):
        return lax.ppermute(values, "shard", swap_pairs(shards, 1))

    def to_y_core(values):
        pairs = [
            (rep_at * shards + at, (rep_at ^ 1) * shards + (at ^ 1))
            for rep_at in range(reps) for at in range(shards)
        ]
        return lax.ppermute(values, ("rep", "shard"), pairs)

    def to_z(values, along):
        return lax.ppermute(values, "shard", shift_pairs(lines, along, 0))

    split = lines // 2
    plain = [(0, 0), (0, 1), (1, 0)]
    groups = [[(*kind, turn) for kind in plain] for turn in range(split)]
    groups += [
        [(0, 0, split), (0, 1, split), (0, 0, split + 1), (1, 1, 0)],
        [(1, 0, split), (1, 1, 1)],
        [(0, 1, split + 1), (1, 0, split + 1), (1, 1, split), (1, 1, split + 1)],
    ]
    early_blocks, late_blocks = sum(groups[:split], []), sum(groups[split:], [])

    def stat_row(block):
        return (2 * block[0] + block[1]) * lines + block[2]

    normed = normalize(hidden, norm_gain)

    last = jnp.arange(input_ids.shape[0]) % group_len == group_len - 1
    targets = jnp.where(last, -1, jnp.roll(input_ids, -1) - first_col)
    ids = jnp.stack([targets, sampled_ids - first_col]).reshape(2, reps * shards, length)
    side, across, turn = (np.array(values) for values in zip(*(early_blocks + late_blocks)))
    holder = (rep ^ (2 * across[None] + np.arange(2)[:, None])).reshape(-1)
    place = 2 * ((shard // 2 - turn) % lines) + ((shard % 2) ^ side)
    ids = jnp.take(ids, holder * shards + jnp.tile(place, 2), axis=1)
    ids = ids.reshape(2, 2, len(side), length)
    early_ids = ids[:, :, :len(early_blocks)].reshape(2, 1, -1)
    late_ids = ids[:, :, len(early_blocks):].reshape(2, 1, -1)
    early_ids, late_ids = [early_ids[0], early_ids[1]], [late_ids[0], late_ids[1]]
    rep_scalar = rep.astype(jnp.int32).reshape(1)
    stats = jnp.zeros((8 * lines, 128), jnp.float32)

    held = {(0, 0, 0): normed}
    early_exp = None

    def logits(group, stats, *gates, first_row=0, exp_rows=None, into=None):
        blocks = [held[block] for block in group]
        blocks[0] = after(blocks[0], *gates)
        rows = [stat_row(block) for block in group]
        exp_rows = exp_rows or len(group) * length
        return round_logits(blocks, rows, head_weight, stats, first_row, exp_rows, into)

    def diagonal(turn):
        if turn % 2 == 0:
            return to_x(held[1, 0, turn])
        return to_y(held[0, 1, turn])

    for turn in range(lines):
        block = held[0, 0, turn]
        held[0, 1, turn] = to_x(block)
        held[1, 0, turn] = to_y(block)
        if turn + 1 < lines:
            arrived = [to_z(block, 1), held[0, 1, turn], held[1, 0, turn]]
            if turn == 0:
                head_weight, *late_ids = prepared(head_weight, *late_ids, *early_ids, stats)
                arrived += [*early_ids, *late_ids, rep_scalar, stats, head_weight]
            elif turn < split:
                arrived += [early_exp]
            else:
                held[0, 0, turn + 1], held[0, 1, turn] = arrived[0], arrived[1]
                middle_exp, stats = logits(
                    groups[split], stats, exp_rows=6 * length
                )
                arrived += [early_exp] + [held[1, 1, past] for past in range(split)]
                arrived += [middle_exp]
            arrived = lax.optimization_barrier(tuple(arrived))
            held[0, 0, turn + 1], held[0, 1, turn], held[1, 0, turn] = arrived[:3]
            if turn == 0:
                early_ids, late_ids = list(arrived[3:5]), list(arrived[5:7])
                rep_scalar, stats, head_weight = arrived[7:]
            else:
                early_exp = arrived[3]
                if turn == split:
                    held[1, 1, 0], held[1, 1, 1], middle_exp = arrived[4:]
            held[1, 1, turn] = diagonal(turn)
        if turn < split:
            size = len(groups[turn]) * length
            early_exp, stats = logits(
                groups[turn], stats, held[0, 0, turn + 1],
                first_row=turn * size, exp_rows=split * size, into=early_exp,
            )

    early = [held[block] for block in early_blocks]
    early[0] = after(early[0], held[0, 0, lines - 1])
    early = turned_features(rep_scalar, early, rows)
    early = [early[0], to_core(early[1])]
    other_exps = [to_core(early_exp)]
    middle_exp, stats = logits(
        groups[split + 1], stats, held[0, 0, lines - 1],
        first_row=4 * length, exp_rows=6 * length, into=middle_exp,
    )
    held[0, 1, lines - 1] = after(held[0, 1, lines - 1], middle_exp)
    held[1, 1, lines - 1] = diagonal(lines - 1)
    early_ids[0] = after(early_ids[0], middle_exp, held[0, 1, lines - 1], *other_exps)
    sums = one_hot_sums(early, early_ids, columns)
    last_exp, stats = logits(groups[-1], stats, *sums)
    exps = [early_exp, middle_exp, last_exp]
    stats = after(stats, *other_exps)
    other_exps.append(to_core(after(middle_exp, stats)))
    across_stats, core_stats, both_stats = to_y(stats), to_core(stats), to_y_core(stats)
    late = [held[block] for block in late_blocks]
    late[0] = after(late[0], stats)
    late = turned_features(rep_scalar, late, rows)
    merged, first = merged_stats(
        after(stats, *other_exps), across_stats, core_stats, both_stats
    )
    all_stats = [merged] + [to_z(merged, -along) for along in range(1, lines)]
    other_exps.append(to_core(after(last_exp, merged)))
    late = [late[0], to_core(late[1])]
    return tuple(refresh_states(
        lines, length, [stat_row(block) for block in early_blocks + late_blocks], early, late,
        exps + other_exps, all_stats, first, late_ids, sums, moment, curvature,
    ))


def solution(mesh):
    in_specs = (
        P(("rep", "shard"), None),
        P(),
        P(),
        P(),
        P(None, "shard"),
        P("rep", "shard"),
        P("rep", "shard"),
    )
    out_specs = (P("rep", "shard"), P("rep", "shard"), P("rep", "shard"))
    reps, shards = mesh.shape["rep"], mesh.shape["shard"]

    def whole(hidden, *others):
        tokens, depth = hidden.shape
        length = tokens // (reps * shards)
        fits = hidden.size * 2 <= GATHER_BYTES and reps == 4 and shards == 8
        if fits and length == 64 and (depth // reps) % 128 == 0:
            plan = functools.partial(all_tokens, reps, shards)
        else:
            plan = by_groups

        return jax.shard_map(
            plan, mesh=mesh, in_specs=in_specs, out_specs=out_specs, check_vma=False
        )(hidden, *others)

    return whole
```

```python
import functools

import jax
import jax.numpy as jnp
import numpy as np
from jax import lax
from jax.experimental import pallas as pl
from jax.experimental.pallas import tpu as pltpu
from jax.sharding import PartitionSpec as P

EPS_NORM = 1e-05
BETA_ONE = 0.96
BETA_TWO = 0.95
RHO_SCALE = 0.05
GATHER_BYTES = 32 * 1024 * 1024
LOGITS_VMEM = 20 * 1024 * 1024
BRIEF = pl.CostEstimate(flops=1024, bytes_accessed=1024, transcendentals=0)


def normalize(hidden, norm_gain):
    values = hidden.astype(jnp.float32)
    row_scale = lax.rsqrt(jnp.mean(values * values, axis=-1, keepdims=True) + EPS_NORM)
    return (values * row_scale * norm_gain).astype(jnp.bfloat16)


def refresh(gradient, sample_grad, moment, curvature):
    moment_new = BETA_ONE * moment.astype(jnp.float32) + (1.0 - BETA_ONE) * gradient
    curvature_new = (
        BETA_TWO * curvature.astype(jnp.float32) + (1.0 - BETA_TWO) * sample_grad * sample_grad
    )
    update_direction = jnp.clip(moment_new / (RHO_SCALE * curvature_new), -1.0, 1.0)
    return (
        moment_new.astype(jnp.bfloat16),
        curvature_new.astype(jnp.bfloat16),
        update_direction.astype(jnp.bfloat16),
    )


def by_groups(hidden, norm_gain, input_ids, sampled_ids, head_weight, moment, curvature):
    normed = normalize(hidden, norm_gain)
    gathered = lax.all_gather(normed, "shard", axis=0, tiled=True)
    group_len = gathered.shape[0]
    columns = head_weight.shape[1]
    first_col = lax.axis_index("shard") * columns
    logits = jnp.dot(gathered, head_weight, preferred_element_type=jnp.float32)
    row_peak = lax.pmax(jnp.max(logits, axis=-1), "shard")
    scaled_exp = jnp.exp(logits - row_peak[:, None])
    row_sum = lax.psum(jnp.sum(scaled_exp, axis=-1), "shard")
    probabilities = (scaled_exp / row_sum[:, None]).astype(jnp.bfloat16)
    group_start = lax.axis_index("rep") * group_len
    token_ids = lax.dynamic_slice_in_dim(input_ids, group_start, group_len, 0)
    sample_ids = lax.dynamic_slice_in_dim(sampled_ids, group_start, group_len, 0)
    position = jnp.arange(group_len)
    shifted = jnp.roll(token_ids, -1) - first_col
    usable = (position < group_len - 1) & (shifted >= 0) & (shifted < columns)
    true_slot = jnp.where(usable, shifted, columns)
    sample_local = sample_ids - first_col
    inside = (sample_local >= 0) & (sample_local < columns)
    sample_slot = jnp.where(inside, sample_local, columns)
    shared = lax.dot_general(
        gathered, probabilities, (((0,), (0,)), ((), ())), preferred_element_type=jnp.float32
    )
    widened = gathered.astype(jnp.float32)
    true_sums = jax.ops.segment_sum(widened, true_slot, num_segments=columns + 1)[:columns]
    sample_sums = jax.ops.segment_sum(widened, sample_slot, num_segments=columns + 1)[:columns]
    true_part = (shared - true_sums.T).astype(jnp.bfloat16)
    sample_part = (shared - sample_sums.T).astype(jnp.bfloat16)
    gradient = lax.psum_scatter(true_part, "rep", scatter_dimension=0, tiled=True)
    sample_grad = lax.psum_scatter(sample_part, "rep", scatter_dimension=0, tiled=True)
    return refresh(
        gradient.astype(jnp.float32), sample_grad.astype(jnp.float32), moment, curvature
    )


def swap_pairs(count, bit):
    return [(index, index ^ bit) for index in range(count)]


def shift_pairs(lines, along, across):
    pairs = []
    for place in range(lines):
        for side in range(2):
            source = 2 * place + side
            pairs.append((source, 2 * ((place + along) % lines) + (side ^ across)))
    return pairs


def prepare_kernel(weight_ref, true_ids, sample_ids, *refs):
    held_ref, true_at, sample_at, arrived = refs[-4:]
    count = arrived.shape[0]
    band = weight_ref.shape[0] // count
    copies = [
        pltpu.make_async_copy(
            weight_ref.at[pl.ds(index * band, band)], held_ref.at[pl.ds(index * band, band)],
            arrived.at[index],
        )
        for index in range(count)
    ]
    for copy in copies:
        copy.start()
    lanes = lax.broadcasted_iota(jnp.int32, (128, 128), 1)
    for ids_ref, out_ref in ((true_ids, true_at), (sample_ids, sample_at)):
        for place in range(0, out_ref.shape[0], 128):
            ids = jnp.broadcast_to(ids_ref[:, place:place + 128], (128, 128)).T
            out_ref[place:place + 128] = ids - lanes
    for copy in copies:
        copy.wait()


def prepared(weight, true_ids, sample_ids, *earlier):
    near = pl.BlockSpec(memory_space=pltpu.VMEM)
    late = jax.ShapeDtypeStruct((true_ids.shape[1], 128), jnp.int32)
    return pl.pallas_call(
        prepare_kernel,
        in_specs=[pl.BlockSpec(memory_space=pltpu.HBM)] + [near] * (2 + len(earlier)),
        out_specs=[near] * 3,
        out_shape=[pltpu.VMEM(weight.shape, weight.dtype), late, late],
        scratch_shapes=[pltpu.SemaphoreType.DMA((4,))],
        compiler_params=pltpu.CompilerParams(vmem_limit_bytes=8 * 1024 * 1024),
        cost_estimate=BRIEF,
        name="prepared",
    )(pltpu.with_memory_space_constraint(weight, pltpu.HBM), true_ids, sample_ids, *earlier)


def logits_kernel(stat_rows, first_row, joins, *refs):
    count = len(stat_rows)
    block_refs, refs = refs[:count], refs[count:]
    if joins:
        refs = refs[:2] + refs[3:]
    weight_ref, before_ref, exp_ref, stats_ref, rows, logits, scaled_exp, highs, sums, sent = refs
    tokens, columns = logits.shape
    length = tokens // count
    half = stats_ref.shape[0] // 2
    for index, ref in enumerate(block_refs):
        rows[index * length:(index + 1) * length] = ref[...]
    highs[...] = jnp.full(highs.shape, -jnp.inf, jnp.float32)
    width = min(256, columns)

    def multiply(index, carry):
        place = pl.ds(pl.multiple_of(index * width, width), width)
        part = jnp.dot(rows[...], weight_ref[:, place], preferred_element_type=jnp.float32)
        logits[:, place] = part
        high = functools.reduce(
            jnp.maximum, [part[:, lane:lane + 128] for lane in range(0, width, 128)]
        )
        highs[...] = jnp.maximum(highs[...], high)
        return carry

    lax.fori_loop(0, columns // width, multiply, 0)
    highs[...] = jnp.broadcast_to(jnp.max(highs[...], axis=1, keepdims=True), highs.shape)
    chunk = 16
    copies = []
    for block in range(count):

        def scale(index, carry, block=block):
            place = pl.ds(pl.multiple_of(block * length + index * chunk, chunk), chunk)
            peak = highs[place, :]
            total = jnp.zeros((chunk, 128), jnp.float32)
            for lane in range(0, columns, 128):
                scaled = jnp.exp(logits[place, lane:lane + 128] - peak)
                scaled_exp[place, lane:lane + 128] = scaled.astype(jnp.bfloat16)
                total += scaled
            sums[place, :] = total
            return carry

        lax.fori_loop(0, length // chunk, scale, 0, unroll=2)
        place = pl.ds(block * length, length)
        target = pl.ds(first_row + block * length, length)
        copies.append(
            pltpu.make_async_copy(scaled_exp.at[place], exp_ref.at[target], sent.at[block])
        )
        copies[-1].start()
    totals = jnp.broadcast_to(jnp.sum(sums[...], axis=1, keepdims=True), sums.shape)
    stats_ref[...] = before_ref[...]
    for base, values in ((0, highs[...].T[0:1]), (half, totals.T[0:1])):
        for index, row in enumerate(stat_rows):
            stats_ref[base + row:base + row + 1, :length] = (
                values[:, index * length:(index + 1) * length]
            )
    for copy in copies:
        copy.wait()


def round_logits(blocks, stat_rows, held_weight, before, first_row, exp_rows, into):
    depth, columns = held_weight.shape
    length = blocks[0].shape[0]
    tokens = length * len(blocks)
    near = pl.BlockSpec(memory_space=pltpu.VMEM)
    held_weight = pltpu.with_memory_space_constraint(held_weight, pltpu.VMEM)
    far = pl.BlockSpec(memory_space=pltpu.HBM)
    joins = [] if into is None else [pltpu.with_memory_space_constraint(into, pltpu.HBM)]
    return pl.pallas_call(
        functools.partial(logits_kernel, stat_rows, first_row, len(joins)),
        in_specs=[near] * (len(blocks) + 2) + [far] * len(joins),
        input_output_aliases={len(blocks) + 2: 0} if joins else {},
        out_specs=[far, near],
        out_shape=[
            pltpu.HBM((exp_rows, columns), jnp.bfloat16),
            jax.ShapeDtypeStruct(before.shape, jnp.float32),
        ],
        scratch_shapes=[
            pltpu.VMEM((tokens, depth), jnp.bfloat16),
            pltpu.VMEM((tokens, columns), jnp.float32),
            pltpu.VMEM((tokens, columns), jnp.bfloat16),
            pltpu.VMEM((tokens, 128), jnp.float32),
            pltpu.VMEM((tokens, 128), jnp.float32),
            pltpu.SemaphoreType.DMA((len(blocks),)),
        ],
        compiler_params=pltpu.CompilerParams(vmem_limit_bytes=LOGITS_VMEM),
        cost_estimate=BRIEF,
        name="round_logits",
    )(*blocks, held_weight, before, *joins)


def turn_kernel(count, rep_ref, *refs):
    mine_ref, other_ref = refs[count:]
    step = pl.program_id(0)
    turned = jnp.concatenate([ref[...] for ref in refs[:count]], axis=0).T

    @pl.when(step == 0)
    def _():
        mine_ref[...] = turned

    @pl.when(step == 1)
    def _():
        other_ref[...] = turned


def turned_features(rep, blocks, rows):
    length = blocks[0].shape[0]
    tokens = length * len(blocks)
    whole = pl.BlockSpec((rows, tokens), lambda step, rep_ref: (0, 0))
    block = pl.BlockSpec((length, rows), lambda step, rep_ref: (0, rep_ref[0] ^ step))
    return pl.pallas_call(
        functools.partial(turn_kernel, len(blocks)),
        grid_spec=pltpu.PrefetchScalarGridSpec(
            num_scalar_prefetch=1,
            grid=(2,),
            in_specs=[block] * len(blocks),
            out_specs=[whole, whole],
        ),
        out_shape=[jax.ShapeDtypeStruct((rows, tokens), jnp.bfloat16)] * 2,
        compiler_params=pltpu.CompilerParams(vmem_limit_bytes=20 * 1024 * 1024),
        cost_estimate=BRIEF,
        name="turned_features",
    )(rep, *blocks)


def one_hot_kernel(count, *refs):
    feature_refs, refs = refs[:count], refs[count:]
    true_ref, sample_ref, true_out, sample_out = refs
    width = true_out.shape[1]
    features = jnp.concatenate([ref[...] for ref in feature_refs], axis=1)
    columns = pl.program_id(0) * width + lax.broadcasted_iota(
        jnp.int32, (width, features.shape[1]), 0
    )
    hot = jnp.concatenate([columns == true_ref[...], columns == sample_ref[...]], axis=0)
    totals = lax.dot_general(
        features, hot.astype(jnp.float32).astype(jnp.bfloat16),
        (((1,), (1,)), ((), ())), preferred_element_type=jnp.float32,
    )
    true_out[...] = totals[:, :width].astype(jnp.bfloat16)
    sample_out[...] = totals[:, width:].astype(jnp.bfloat16)


def one_hot_sums(features, ids, columns):
    rows = features[0].shape[0]
    width = min(256, columns)
    whole = lambda array: pl.BlockSpec(array.shape, lambda step: (0, 0))
    tile = pl.BlockSpec((rows, width), lambda step: (0, step))
    return pl.pallas_call(
        functools.partial(one_hot_kernel, len(features)),
        grid=(columns // width,),
        in_specs=[whole(array) for array in (*features, *ids)],
        out_specs=[tile, tile],
        out_shape=[pltpu.HBM((rows, columns), jnp.bfloat16)] * 2,
        compiler_params=pltpu.CompilerParams(vmem_limit_bytes=24 * 1024 * 1024),
        cost_estimate=BRIEF,
        name="one_hot_sums",
    )(*features, *ids)


def merge_kernel(own_ref, across_ref, core_ref, both_ref, merged_ref, first_ref):
    rows = own_ref.shape[0] // 2
    side = rows // 2
    for core, (near, far) in enumerate(((own_ref, across_ref), (core_ref, both_ref))):
        place = core * rows
        first, total = near[:rows], near[rows:]
        second = jnp.concatenate([far[side:rows], far[:side]], axis=0)
        other = jnp.concatenate([far[rows + side:], far[rows:rows + side]], axis=0)
        peak = jnp.maximum(first, second)
        merged_ref[place:place + rows] = peak
        merged_ref[2 * rows + place:3 * rows + place] = (
            total * jnp.exp(first - peak) + other * jnp.exp(second - peak)
        )
        first_ref[place:place + rows] = first


def merged_stats(own, across, core, both):
    rows, lanes = own.shape
    return pl.pallas_call(
        merge_kernel,
        out_shape=[
            jax.ShapeDtypeStruct((2 * rows, lanes), jnp.float32),
            jax.ShapeDtypeStruct((rows, lanes), jnp.float32),
        ],
        compiler_params=pltpu.CompilerParams(vmem_limit_bytes=4 * 1024 * 1024),
        cost_estimate=BRIEF,
        name="merged_stats",
    )(own, across, core, both)


def refresh_kernel(lines, length, block_rows, *refs):
    early_refs, late_refs, refs = refs[:2], refs[2:4], refs[4:]
    exp_refs, refs = refs[:6], refs[6:]
    stats_refs, refs = refs[:lines], refs[lines:]
    (first_ref, true_at, sample_at, true_sum, sample_sum, moment_ref, curvature_ref,
     moment_out, curvature_out, update_out, factors) = refs
    step = pl.program_id(0)
    width = moment_out.shape[1]
    early = early_refs[0].shape[1]
    late = late_refs[0].shape[1]

    @pl.when(step == 0)
    def _():
        rows = first_ref.shape[0]

        def turned(values, along):
            return jnp.concatenate([
                values[group + (turn + along) % lines:group + (turn + along) % lines + 1]
                for group in range(0, rows, lines) for turn in range(lines)
            ], axis=0) if along else values

        peaks = [turned(ref[:rows], along) for along, ref in enumerate(stats_refs)]
        totals = [turned(ref[rows:], along) for along, ref in enumerate(stats_refs)]
        peak = functools.reduce(jnp.maximum, peaks)
        total = sum(t * jnp.exp(p - peak) for p, t in zip(peaks, totals))
        factor = jnp.exp(first_ref[...] - peak) / total
        per_core = rows // 2
        full = jnp.concatenate([factor, jnp.zeros((128 - rows, 128), jnp.float32)], axis=0).T
        for core in range(2):
            for index, row in enumerate(block_rows):
                place = (core * len(block_rows) + index) * length
                at = core * per_core + row
                factors[place:place + length] = jnp.broadcast_to(
                    full[:length, at:at + 1], (length, 128)
                )

    def probs(ref, place, lane):
        scale = factors[place:place + ref.shape[0]]
        return ref[:, lane:lane + 128].astype(jnp.float32) * scale

    early_sides, true_sides, sample_sides = [], [], []
    for core in range(2):
        first_exp, *late_exps = exp_refs[3 * core:3 * core + 3]
        place = core * (early + late)
        early_sides.append(jnp.concatenate([
            probs(first_exp, place, lane).astype(jnp.bfloat16) for lane in range(0, width, 128)
        ], axis=1))
        place += early
        at = core * late
        for ref in late_exps:
            rows = slice(at, at + ref.shape[0])
            true_parts, sample_parts = [], []
            for lane in range(0, width, 128):
                prob = probs(ref, place, lane)
                column = step * width + lane
                true_hot = jnp.where(true_at[rows] == column, 1.0, 0.0)
                sample_hot = jnp.where(sample_at[rows] == column, 1.0, 0.0)
                true_parts.append((prob - true_hot).astype(jnp.bfloat16))
                sample_parts.append((prob - sample_hot).astype(jnp.bfloat16))
            true_sides.append(jnp.concatenate(true_parts, axis=1))
            sample_sides.append(jnp.concatenate(sample_parts, axis=1))
            place += ref.shape[0]
            at += ref.shape[0]
    early_features = jnp.concatenate([ref[...] for ref in early_refs], axis=1)
    late_features = jnp.concatenate([ref[...] for ref in late_refs], axis=1)

    def product(features, sides):
        return jnp.dot(
            features, jnp.concatenate(sides, axis=0), preferred_element_type=jnp.float32
        )

    shared = product(early_features, early_sides)
    gradient = product(late_features, true_sides) + (shared - true_sum[...].astype(jnp.float32))
    sample_grad = product(late_features, sample_sides) + (
        shared - sample_sum[...].astype(jnp.float32)
    )
    moment_out[...], curvature_out[...], update_out[...] = refresh(
        gradient, sample_grad, moment_ref[...], curvature_ref[...]
    )


def refresh_states(lines, length, block_rows, early, late, exps, stats, first,
                   late_ids, sums, moment, curvature):
    rows, columns = moment.shape
    width = min(256, columns)
    whole = lambda array: pl.BlockSpec(array.shape, lambda step: (0, 0))
    tile = pl.BlockSpec((rows, width), lambda step: (0, step))
    return pl.pallas_call(
        functools.partial(refresh_kernel, lines, length, block_rows),
        grid=(columns // width,),
        in_specs=[whole(array) for array in (*early, *late)]
        + [pl.BlockSpec((array.shape[0], width), lambda step: (0, step)) for array in exps]
        + [whole(array) for array in (*stats, first, *late_ids)]
        + [tile] * 4,
        out_specs=[tile] * 3,
        out_shape=[jax.ShapeDtypeStruct((rows, columns), jnp.bfloat16)] * 3,
        scratch_shapes=[pltpu.VMEM((2 * length * len(block_rows), 128), jnp.float32)],
        compiler_params=pltpu.CompilerParams(vmem_limit_bytes=36 * 1024 * 1024),
        cost_estimate=BRIEF,
        name="refresh_states",
    )(
        *early, *late, *in_hbm(exps[:3]), *exps[3:], *stats, first, *late_ids,
        *in_hbm(sums, [moment, curvature])
    )


def in_hbm(*lists):
    return [pltpu.with_memory_space_constraint(array, pltpu.HBM) for array in sum(map(list, lists), [])]


def after(value, *others):
    return lax.optimization_barrier((value, *others))[0]


def all_tokens(reps, shards, hidden, norm_gain, input_ids, sampled_ids, head_weight, moment, curvature):
    lines = shards // 2
    length = hidden.shape[0]
    rows, columns = moment.shape
    rep = lax.axis_index("rep")
    shard = lax.axis_index("shard")
    first_col = shard * columns
    group_len = length * shards

    def to_x(values):
        return lax.ppermute(values, "rep", swap_pairs(reps, 2))

    def to_core(values):
        return lax.ppermute(values, "rep", swap_pairs(reps, 1))

    def to_y(values):
        return lax.ppermute(values, "shard", swap_pairs(shards, 1))

    def to_y_core(values):
        pairs = [
            (rep_at * shards + at, (rep_at ^ 1) * shards + (at ^ 1))
            for rep_at in range(reps) for at in range(shards)
        ]
        return lax.ppermute(values, ("rep", "shard"), pairs)

    def to_z(values, along):
        return lax.ppermute(values, "shard", shift_pairs(lines, along, 0))

    split = lines // 2
    plain = [(0, 0), (0, 1), (1, 0)]
    groups = [[(*kind, turn) for kind in plain] for turn in range(split)]
    groups += [
        [(0, 0, split), (1, 1, 0)],
        [(0, 1, split), (1, 0, split), (0, 0, split + 1), (1, 1, 1)],
        [(0, 1, split + 1), (1, 0, split + 1), (1, 1, split), (1, 1, split + 1)],
    ]
    early_blocks, late_blocks = sum(groups[:split], []), sum(groups[split:], [])

    def stat_row(block):
        return (2 * block[0] + block[1]) * lines + block[2]

    normed = normalize(hidden, norm_gain)

    last = jnp.arange(input_ids.shape[0]) % group_len == group_len - 1
    targets = jnp.where(last, -1, jnp.roll(input_ids, -1) - first_col)
    ids = jnp.stack([targets, sampled_ids - first_col]).reshape(2, reps * shards, length)
    side, across, turn = (np.array(values) for values in zip(*(early_blocks + late_blocks)))
    holder = (rep ^ (2 * across[None] + np.arange(2)[:, None])).reshape(-1)
    place = 2 * ((shard // 2 - turn) % lines) + ((shard % 2) ^ side)
    ids = jnp.take(ids, holder * shards + jnp.tile(place, 2), axis=1)
    ids = ids.reshape(2, 2, len(side), length)
    early_ids = ids[:, :, :len(early_blocks)].reshape(2, 1, -1)
    late_ids = ids[:, :, len(early_blocks):].reshape(2, 1, -1)
    early_ids, late_ids = [early_ids[0], early_ids[1]], [late_ids[0], late_ids[1]]
    rep_scalar = rep.astype(jnp.int32).reshape(1)
    stats = jnp.zeros((8 * lines, 128), jnp.float32)

    held = {(0, 0, 0): normed}
    early_exp = None

    def logits(group, stats, *gates, first_row=0, exp_rows=None, into=None):
        blocks = [held[block] for block in group]
        blocks[0] = after(blocks[0], *gates)
        rows = [stat_row(block) for block in group]
        exp_rows = exp_rows or len(group) * length
        return round_logits(blocks, rows, head_weight, stats, first_row, exp_rows, into)

    def diagonal(turn):
        if turn % 2 == 0:
            return to_x(held[1, 0, turn])
        return to_y(held[0, 1, turn])

    for turn in range(lines):
        block = held[0, 0, turn]
        held[0, 1, turn] = to_x(block)
        held[1, 0, turn] = to_y(block)
        if turn + 1 < lines:
            arrived = [to_z(block, 1), held[0, 1, turn], held[1, 0, turn]]
            if turn == 0:
                head_weight, *late_ids = prepared(head_weight, *late_ids, *early_ids, stats)
                arrived += [*early_ids, *late_ids, rep_scalar, stats, head_weight]
            elif turn < split:
                arrived += [early_exp]
            else:
                middle_exp, stats = logits(
                    groups[split], stats, exp_rows=6 * length
                )
                arrived += [early_exp] + [held[1, 1, past] for past in range(split)]
                arrived += [middle_exp]
            arrived = lax.optimization_barrier(tuple(arrived))
            held[0, 0, turn + 1], held[0, 1, turn], held[1, 0, turn] = arrived[:3]
            if turn == 0:
                early_ids, late_ids = list(arrived[3:5]), list(arrived[5:7])
                rep_scalar, stats, head_weight = arrived[7:]
            else:
                early_exp = arrived[3]
                if turn == split:
                    held[1, 1, 0], held[1, 1, 1], middle_exp = arrived[4:]
            held[1, 1, turn] = diagonal(turn)
        if turn < split:
            size = len(groups[turn]) * length
            early_exp, stats = logits(
                groups[turn], stats, held[0, 0, turn + 1],
                first_row=turn * size, exp_rows=split * size, into=early_exp,
            )

    early = [held[block] for block in early_blocks]
    early[0] = after(early[0], held[0, 0, lines - 1])
    early = turned_features(rep_scalar, early, rows)
    early = [early[0], to_core(early[1])]
    other_exps = [to_core(early_exp)]
    middle_exp, stats = logits(
        groups[split + 1], stats, held[0, 0, lines - 1], early[0],
        first_row=2 * length, exp_rows=6 * length, into=middle_exp,
    )
    held[0, 1, lines - 1] = after(held[0, 1, lines - 1], middle_exp)
    held[1, 1, lines - 1] = diagonal(lines - 1)
    early_ids[0] = after(early_ids[0], middle_exp, held[0, 1, lines - 1], *other_exps)
    sums = one_hot_sums(early, early_ids, columns)
    late = [held[block] for block in late_blocks]
    late[0] = after(late[0], *sums)
    late = turned_features(rep_scalar, late, rows)
    late = [late[0], to_core(late[1])]
    other_exps.append(to_core(after(middle_exp, late[0])))
    last_exp, stats = logits(groups[-1], stats, late[0], *sums)
    exps = [early_exp, middle_exp, last_exp]
    across_stats, core_stats, both_stats = to_y(stats), to_core(stats), to_y_core(stats)
    merged, first = merged_stats(
        after(stats, late[1], *other_exps), across_stats, core_stats, both_stats
    )
    all_stats = [merged] + [to_z(merged, -along) for along in range(1, lines)]
    other_exps.append(to_core(after(last_exp, merged)))
    return tuple(refresh_states(
        lines, length, [stat_row(block) for block in early_blocks + late_blocks], early, late,
        exps + other_exps, all_stats, first, late_ids, sums, moment, curvature,
    ))


def solution(mesh):
    in_specs = (
        P(("rep", "shard"), None),
        P(),
        P(),
        P(),
        P(None, "shard"),
        P("rep", "shard"),
        P("rep", "shard"),
    )
    out_specs = (P("rep", "shard"), P("rep", "shard"), P("rep", "shard"))
    reps, shards = mesh.shape["rep"], mesh.shape["shard"]

    def whole(hidden, *others):
        tokens, depth = hidden.shape
        length = tokens // (reps * shards)
        fits = hidden.size * 2 <= GATHER_BYTES and reps == 4 and shards == 8
        if fits and length == 64 and (depth // reps) % 128 == 0:
            plan = functools.partial(all_tokens, reps, shards)
        else:
            plan = by_groups

        return jax.shard_map(
            plan, mesh=mesh, in_specs=in_specs, out_specs=out_specs, check_vma=False
        )(hidden, *others)

    return whole
```

```python
import functools

import jax
import jax.numpy as jnp
import numpy as np
from jax import lax
from jax.experimental import pallas as pl
from jax.experimental.pallas import tpu as pltpu
from jax.sharding import PartitionSpec as P

EPS_NORM = 1e-05
BETA_ONE = 0.96
BETA_TWO = 0.95
RHO_SCALE = 0.05
GATHER_BYTES = 32 * 1024 * 1024
LOGITS_VMEM = 20 * 1024 * 1024
BRIEF = pl.CostEstimate(flops=1024, bytes_accessed=1024, transcendentals=0)


def normalize(hidden, norm_gain):
    values = hidden.astype(jnp.float32)
    row_scale = lax.rsqrt(jnp.mean(values * values, axis=-1, keepdims=True) + EPS_NORM)
    return (values * row_scale * norm_gain).astype(jnp.bfloat16)


def refresh(gradient, sample_grad, moment, curvature):
    moment_new = BETA_ONE * moment.astype(jnp.float32) + (1.0 - BETA_ONE) * gradient
    curvature_new = (
        BETA_TWO * curvature.astype(jnp.float32) + (1.0 - BETA_TWO) * sample_grad * sample_grad
    )
    update_direction = jnp.clip(moment_new / (RHO_SCALE * curvature_new), -1.0, 1.0)
    return (
        moment_new.astype(jnp.bfloat16),
        curvature_new.astype(jnp.bfloat16),
        update_direction.astype(jnp.bfloat16),
    )


def by_groups(hidden, norm_gain, input_ids, sampled_ids, head_weight, moment, curvature):
    normed = normalize(hidden, norm_gain)
    gathered = lax.all_gather(normed, "shard", axis=0, tiled=True)
    group_len = gathered.shape[0]
    columns = head_weight.shape[1]
    first_col = lax.axis_index("shard") * columns
    logits = jnp.dot(gathered, head_weight, preferred_element_type=jnp.float32)
    row_peak = lax.pmax(jnp.max(logits, axis=-1), "shard")
    scaled_exp = jnp.exp(logits - row_peak[:, None])
    row_sum = lax.psum(jnp.sum(scaled_exp, axis=-1), "shard")
    probabilities = (scaled_exp / row_sum[:, None]).astype(jnp.bfloat16)
    group_start = lax.axis_index("rep") * group_len
    token_ids = lax.dynamic_slice_in_dim(input_ids, group_start, group_len, 0)
    sample_ids = lax.dynamic_slice_in_dim(sampled_ids, group_start, group_len, 0)
    position = jnp.arange(group_len)
    shifted = jnp.roll(token_ids, -1) - first_col
    usable = (position < group_len - 1) & (shifted >= 0) & (shifted < columns)
    true_slot = jnp.where(usable, shifted, columns)
    sample_local = sample_ids - first_col
    inside = (sample_local >= 0) & (sample_local < columns)
    sample_slot = jnp.where(inside, sample_local, columns)
    shared = lax.dot_general(
        gathered, probabilities, (((0,), (0,)), ((), ())), preferred_element_type=jnp.float32
    )
    widened = gathered.astype(jnp.float32)
    true_sums = jax.ops.segment_sum(widened, true_slot, num_segments=columns + 1)[:columns]
    sample_sums = jax.ops.segment_sum(widened, sample_slot, num_segments=columns + 1)[:columns]
    true_part = (shared - true_sums.T).astype(jnp.bfloat16)
    sample_part = (shared - sample_sums.T).astype(jnp.bfloat16)
    gradient = lax.psum_scatter(true_part, "rep", scatter_dimension=0, tiled=True)
    sample_grad = lax.psum_scatter(sample_part, "rep", scatter_dimension=0, tiled=True)
    return refresh(
        gradient.astype(jnp.float32), sample_grad.astype(jnp.float32), moment, curvature
    )


def swap_pairs(count, bit):
    return [(index, index ^ bit) for index in range(count)]


def shift_pairs(lines, along, across):
    pairs = []
    for place in range(lines):
        for side in range(2):
            source = 2 * place + side
            pairs.append((source, 2 * ((place + along) % lines) + (side ^ across)))
    return pairs


def normalize_kernel(hidden_ref, gain_ref, normed_ref):
    normed_ref[...] = normalize(hidden_ref[...], gain_ref[...])


def normalized(hidden, norm_gain):
    return pl.pallas_call(
        normalize_kernel,
        out_shape=jax.ShapeDtypeStruct(hidden.shape, jnp.bfloat16),
        compiler_params=pltpu.CompilerParams(vmem_limit_bytes=8 * 1024 * 1024),
        cost_estimate=BRIEF,
        name="normalized",
    )(*in_hbm([hidden]), norm_gain.reshape(1, -1))


def prepare_kernel(weight_ref, true_ids, sample_ids, *refs):
    held_ref, true_at, sample_at, arrived = refs[-4:]
    count = arrived.shape[0]
    band = weight_ref.shape[0] // count
    copies = [
        pltpu.make_async_copy(
            weight_ref.at[pl.ds(index * band, band)], held_ref.at[pl.ds(index * band, band)],
            arrived.at[index],
        )
        for index in range(count)
    ]
    for copy in copies:
        copy.start()
    lanes = lax.broadcasted_iota(jnp.int32, (128, 128), 1)
    for ids_ref, out_ref in ((true_ids, true_at), (sample_ids, sample_at)):
        for place in range(0, out_ref.shape[0], 128):
            ids = jnp.broadcast_to(ids_ref[:, place:place + 128], (128, 128)).T
            out_ref[place:place + 128] = ids - lanes
    for copy in copies:
        copy.wait()


def prepared(weight, true_ids, sample_ids, *earlier):
    near = pl.BlockSpec(memory_space=pltpu.VMEM)
    late = jax.ShapeDtypeStruct((true_ids.shape[1], 128), jnp.int32)
    return pl.pallas_call(
        prepare_kernel,
        in_specs=[pl.BlockSpec(memory_space=pltpu.HBM)] + [near] * (2 + len(earlier)),
        out_specs=[near] * 3,
        out_shape=[pltpu.VMEM(weight.shape, weight.dtype), late, late],
        scratch_shapes=[pltpu.SemaphoreType.DMA((4,))],
        compiler_params=pltpu.CompilerParams(vmem_limit_bytes=8 * 1024 * 1024),
        cost_estimate=BRIEF,
        name="prepared",
    )(pltpu.with_memory_space_constraint(weight, pltpu.HBM), true_ids, sample_ids, *earlier)


def logits_kernel(stat_rows, first_row, joins, *refs):
    count = len(stat_rows)
    block_refs, refs = refs[:count], refs[count:]
    if joins:
        refs = refs[:2] + refs[3:]
    weight_ref, before_ref, exp_ref, stats_ref, rows, logits, scaled_exp, highs, sums, sent = refs
    tokens, columns = logits.shape
    length = tokens // count
    half = stats_ref.shape[0] // 2
    for index, ref in enumerate(block_refs):
        rows[index * length:(index + 1) * length] = ref[...]
    highs[...] = jnp.full(highs.shape, -jnp.inf, jnp.float32)
    width = min(256, columns)

    def multiply(index, carry):
        place = pl.ds(pl.multiple_of(index * width, width), width)
        part = jnp.dot(rows[...], weight_ref[:, place], preferred_element_type=jnp.float32)
        logits[:, place] = part
        high = functools.reduce(
            jnp.maximum, [part[:, lane:lane + 128] for lane in range(0, width, 128)]
        )
        highs[...] = jnp.maximum(highs[...], high)
        return carry

    lax.fori_loop(0, columns // width, multiply, 0)
    highs[...] = jnp.broadcast_to(jnp.max(highs[...], axis=1, keepdims=True), highs.shape)
    chunk = 16
    copies = []
    for block in range(count):

        def scale(index, carry, block=block):
            place = pl.ds(pl.multiple_of(block * length + index * chunk, chunk), chunk)
            peak = highs[place, :]
            total = jnp.zeros((chunk, 128), jnp.float32)
            for lane in range(0, columns, 128):
                scaled = jnp.exp(logits[place, lane:lane + 128] - peak)
                scaled_exp[place, lane:lane + 128] = scaled.astype(jnp.bfloat16)
                total += scaled
            sums[place, :] = total
            return carry

        lax.fori_loop(0, length // chunk, scale, 0, unroll=2)
        place = pl.ds(block * length, length)
        target = pl.ds(first_row + block * length, length)
        copies.append(
            pltpu.make_async_copy(scaled_exp.at[place], exp_ref.at[target], sent.at[block])
        )
        copies[-1].start()
    totals = jnp.broadcast_to(jnp.sum(sums[...], axis=1, keepdims=True), sums.shape)
    stats_ref[...] = before_ref[...]
    for base, values in ((0, highs[...].T[0:1]), (half, totals.T[0:1])):
        for index, row in enumerate(stat_rows):
            stats_ref[base + row:base + row + 1, :length] = (
                values[:, index * length:(index + 1) * length]
            )
    for copy in copies:
        copy.wait()


def round_logits(blocks, stat_rows, held_weight, before, first_row, exp_rows, into):
    depth, columns = held_weight.shape
    length = blocks[0].shape[0]
    tokens = length * len(blocks)
    near = pl.BlockSpec(memory_space=pltpu.VMEM)
    held_weight = pltpu.with_memory_space_constraint(held_weight, pltpu.VMEM)
    far = pl.BlockSpec(memory_space=pltpu.HBM)
    joins = [] if into is None else [pltpu.with_memory_space_constraint(into, pltpu.HBM)]
    return pl.pallas_call(
        functools.partial(logits_kernel, stat_rows, first_row, len(joins)),
        in_specs=[near] * (len(blocks) + 2) + [far] * len(joins),
        input_output_aliases={len(blocks) + 2: 0} if joins else {},
        out_specs=[far, near],
        out_shape=[
            pltpu.HBM((exp_rows, columns), jnp.bfloat16),
            jax.ShapeDtypeStruct(before.shape, jnp.float32),
        ],
        scratch_shapes=[
            pltpu.VMEM((tokens, depth), jnp.bfloat16),
            pltpu.VMEM((tokens, columns), jnp.float32),
            pltpu.VMEM((tokens, columns), jnp.bfloat16),
            pltpu.VMEM((tokens, 128), jnp.float32),
            pltpu.VMEM((tokens, 128), jnp.float32),
            pltpu.SemaphoreType.DMA((len(blocks),)),
        ],
        compiler_params=pltpu.CompilerParams(vmem_limit_bytes=LOGITS_VMEM),
        cost_estimate=BRIEF,
        name="round_logits",
    )(*blocks, held_weight, before, *joins)


def turn_kernel(count, rep_ref, *refs):
    mine_ref, other_ref = refs[count:]
    step = pl.program_id(0)
    turned = jnp.concatenate([ref[...] for ref in refs[:count]], axis=0).T

    @pl.when(step == 0)
    def _():
        mine_ref[...] = turned

    @pl.when(step == 1)
    def _():
        other_ref[...] = turned


def turned_features(rep, blocks, rows):
    length = blocks[0].shape[0]
    tokens = length * len(blocks)
    whole = pl.BlockSpec((rows, tokens), lambda step, rep_ref: (0, 0))
    block = pl.BlockSpec((length, rows), lambda step, rep_ref: (0, rep_ref[0] ^ step))
    return pl.pallas_call(
        functools.partial(turn_kernel, len(blocks)),
        grid_spec=pltpu.PrefetchScalarGridSpec(
            num_scalar_prefetch=1,
            grid=(2,),
            in_specs=[block] * len(blocks),
            out_specs=[whole, whole],
        ),
        out_shape=[jax.ShapeDtypeStruct((rows, tokens), jnp.bfloat16)] * 2,
        compiler_params=pltpu.CompilerParams(vmem_limit_bytes=20 * 1024 * 1024),
        cost_estimate=BRIEF,
        name="turned_features",
    )(rep, *blocks)


def one_hot_kernel(count, *refs):
    feature_refs, refs = refs[:count], refs[count:]
    true_ref, sample_ref, true_out, sample_out = refs
    width = true_out.shape[1]
    features = jnp.concatenate([ref[...] for ref in feature_refs], axis=1)
    columns = pl.program_id(0) * width + lax.broadcasted_iota(
        jnp.int32, (width, features.shape[1]), 0
    )
    hot = jnp.concatenate([columns == true_ref[...], columns == sample_ref[...]], axis=0)
    totals = lax.dot_general(
        features, hot.astype(jnp.float32).astype(jnp.bfloat16),
        (((1,), (1,)), ((), ())), preferred_element_type=jnp.float32,
    )
    true_out[...] = totals[:, :width].astype(jnp.bfloat16)
    sample_out[...] = totals[:, width:].astype(jnp.bfloat16)


def one_hot_sums(features, ids, columns):
    rows = features[0].shape[0]
    width = min(256, columns)
    whole = lambda array: pl.BlockSpec(array.shape, lambda step: (0, 0))
    tile = pl.BlockSpec((rows, width), lambda step: (0, step))
    return pl.pallas_call(
        functools.partial(one_hot_kernel, len(features)),
        grid=(columns // width,),
        in_specs=[whole(array) for array in (*features, *ids)],
        out_specs=[tile, tile],
        out_shape=[pltpu.HBM((rows, columns), jnp.bfloat16)] * 2,
        compiler_params=pltpu.CompilerParams(vmem_limit_bytes=24 * 1024 * 1024),
        cost_estimate=BRIEF,
        name="one_hot_sums",
    )(*features, *ids)


def merge_kernel(own_ref, across_ref, core_ref, both_ref, merged_ref, first_ref):
    rows = own_ref.shape[0] // 2
    side = rows // 2
    for core, (near, far) in enumerate(((own_ref, across_ref), (core_ref, both_ref))):
        place = core * rows
        first, total = near[:rows], near[rows:]
        second = jnp.concatenate([far[side:rows], far[:side]], axis=0)
        other = jnp.concatenate([far[rows + side:], far[rows:rows + side]], axis=0)
        peak = jnp.maximum(first, second)
        merged_ref[place:place + rows] = peak
        merged_ref[2 * rows + place:3 * rows + place] = (
            total * jnp.exp(first - peak) + other * jnp.exp(second - peak)
        )
        first_ref[place:place + rows] = first


def merged_stats(own, across, core, both):
    rows, lanes = own.shape
    return pl.pallas_call(
        merge_kernel,
        out_shape=[
            jax.ShapeDtypeStruct((2 * rows, lanes), jnp.float32),
            jax.ShapeDtypeStruct((rows, lanes), jnp.float32),
        ],
        compiler_params=pltpu.CompilerParams(vmem_limit_bytes=4 * 1024 * 1024),
        cost_estimate=BRIEF,
        name="merged_stats",
    )(own, across, core, both)


def refresh_kernel(lines, length, block_rows, *refs):
    early_refs, late_refs, refs = refs[:2], refs[2:4], refs[4:]
    exp_refs, refs = refs[:6], refs[6:]
    stats_refs, refs = refs[:lines], refs[lines:]
    (first_ref, true_at, sample_at, true_sum, sample_sum, moment_ref, curvature_ref,
     moment_out, curvature_out, update_out, factors) = refs
    step = pl.program_id(0)
    width = moment_out.shape[1]
    early = early_refs[0].shape[1]
    late = late_refs[0].shape[1]

    @pl.when(step == 0)
    def _():
        rows = first_ref.shape[0]

        def turned(values, along):
            return jnp.concatenate([
                values[group + (turn + along) % lines:group + (turn + along) % lines + 1]
                for group in range(0, rows, lines) for turn in range(lines)
            ], axis=0) if along else values

        peaks = [turned(ref[:rows], along) for along, ref in enumerate(stats_refs)]
        totals = [turned(ref[rows:], along) for along, ref in enumerate(stats_refs)]
        peak = functools.reduce(jnp.maximum, peaks)
        total = sum(t * jnp.exp(p - peak) for p, t in zip(peaks, totals))
        factor = jnp.exp(first_ref[...] - peak) / total
        per_core = rows // 2
        full = jnp.concatenate([factor, jnp.zeros((128 - rows, 128), jnp.float32)], axis=0).T
        for core in range(2):
            for index, row in enumerate(block_rows):
                place = (core * len(block_rows) + index) * length
                at = core * per_core + row
                factors[place:place + length] = jnp.broadcast_to(
                    full[:length, at:at + 1], (length, 128)
                )

    def probs(ref, place, lane):
        scale = factors[place:place + ref.shape[0]]
        return ref[:, lane:lane + 128].astype(jnp.float32) * scale

    early_sides, true_sides, sample_sides = [], [], []
    for core in range(2):
        first_exp, *late_exps = exp_refs[3 * core:3 * core + 3]
        place = core * (early + late)
        early_sides.append(jnp.concatenate([
            probs(first_exp, place, lane).astype(jnp.bfloat16) for lane in range(0, width, 128)
        ], axis=1))
        place += early
        at = core * late
        for ref in late_exps:
            rows = slice(at, at + ref.shape[0])
            true_parts, sample_parts = [], []
            for lane in range(0, width, 128):
                prob = probs(ref, place, lane)
                column = step * width + lane
                true_hot = jnp.where(true_at[rows] == column, 1.0, 0.0)
                sample_hot = jnp.where(sample_at[rows] == column, 1.0, 0.0)
                true_parts.append((prob - true_hot).astype(jnp.bfloat16))
                sample_parts.append((prob - sample_hot).astype(jnp.bfloat16))
            true_sides.append(jnp.concatenate(true_parts, axis=1))
            sample_sides.append(jnp.concatenate(sample_parts, axis=1))
            place += ref.shape[0]
            at += ref.shape[0]
    early_features = jnp.concatenate([ref[...] for ref in early_refs], axis=1)
    late_features = jnp.concatenate([ref[...] for ref in late_refs], axis=1)

    def product(features, sides):
        return jnp.dot(
            features, jnp.concatenate(sides, axis=0), preferred_element_type=jnp.float32
        )

    shared = product(early_features, early_sides)
    gradient = product(late_features, true_sides) + (shared - true_sum[...].astype(jnp.float32))
    sample_grad = product(late_features, sample_sides) + (
        shared - sample_sum[...].astype(jnp.float32)
    )
    moment_out[...], curvature_out[...], update_out[...] = refresh(
        gradient, sample_grad, moment_ref[...], curvature_ref[...]
    )


def refresh_states(lines, length, block_rows, early, late, exps, stats, first,
                   late_ids, sums, moment, curvature):
    rows, columns = moment.shape
    width = min(256, columns)
    whole = lambda array: pl.BlockSpec(array.shape, lambda step: (0, 0))
    tile = pl.BlockSpec((rows, width), lambda step: (0, step))
    return pl.pallas_call(
        functools.partial(refresh_kernel, lines, length, block_rows),
        grid=(columns // width,),
        in_specs=[whole(array) for array in (*early, *late)]
        + [pl.BlockSpec((array.shape[0], width), lambda step: (0, step)) for array in exps]
        + [whole(array) for array in (*stats, first, *late_ids)]
        + [tile] * 4,
        out_specs=[tile] * 3,
        out_shape=[jax.ShapeDtypeStruct((rows, columns), jnp.bfloat16)] * 3,
        scratch_shapes=[pltpu.VMEM((2 * length * len(block_rows), 128), jnp.float32)],
        compiler_params=pltpu.CompilerParams(vmem_limit_bytes=36 * 1024 * 1024),
        cost_estimate=BRIEF,
        name="refresh_states",
    )(
        *early, *late, *in_hbm(exps[:3]), *exps[3:], *stats, first, *late_ids,
        *in_hbm(sums, [moment, curvature])
    )


def in_hbm(*lists):
    return [pltpu.with_memory_space_constraint(array, pltpu.HBM) for array in sum(map(list, lists), [])]


def after(value, *others):
    return lax.optimization_barrier((value, *others))[0]


def all_tokens(reps, shards, hidden, norm_gain, input_ids, sampled_ids, head_weight, moment, curvature):
    lines = shards // 2
    length = hidden.shape[0]
    rows, columns = moment.shape
    rep = lax.axis_index("rep")
    shard = lax.axis_index("shard")
    first_col = shard * columns
    group_len = length * shards

    def to_x(values):
        return lax.ppermute(values, "rep", swap_pairs(reps, 2))

    def to_core(values):
        return lax.ppermute(values, "rep", swap_pairs(reps, 1))

    def to_y(values):
        return lax.ppermute(values, "shard", swap_pairs(shards, 1))

    def to_y_core(values):
        pairs = [
            (rep_at * shards + at, (rep_at ^ 1) * shards + (at ^ 1))
            for rep_at in range(reps) for at in range(shards)
        ]
        return lax.ppermute(values, ("rep", "shard"), pairs)

    def to_z(values, along):
        return lax.ppermute(values, "shard", shift_pairs(lines, along, 0))

    split = lines // 2
    plain = [(0, 0), (0, 1), (1, 0)]
    groups = [[(*kind, turn) for kind in plain] for turn in range(split)]
    groups += [
        [(0, 0, split), (1, 1, 0)],
        [(0, 1, split), (1, 0, split), (0, 0, split + 1), (1, 1, 1)],
        [(0, 1, split + 1), (1, 0, split + 1), (1, 1, split), (1, 1, split + 1)],
    ]
    early_blocks, late_blocks = sum(groups[:split], []), sum(groups[split:], [])

    def stat_row(block):
        return (2 * block[0] + block[1]) * lines + block[2]

    normed = normalized(hidden, norm_gain)

    last = jnp.arange(input_ids.shape[0]) % group_len == group_len - 1
    targets = jnp.where(last, -1, jnp.roll(input_ids, -1) - first_col)
    ids = jnp.stack([targets, sampled_ids - first_col]).reshape(2, reps * shards, length)
    side, across, turn = (np.array(values) for values in zip(*(early_blocks + late_blocks)))
    holder = (rep ^ (2 * across[None] + np.arange(2)[:, None])).reshape(-1)
    place = 2 * ((shard // 2 - turn) % lines) + ((shard % 2) ^ side)
    ids = jnp.take(ids, holder * shards + jnp.tile(place, 2), axis=1)
    ids = ids.reshape(2, 2, len(side), length)
    early_ids = ids[:, :, :len(early_blocks)].reshape(2, 1, -1)
    late_ids = ids[:, :, len(early_blocks):].reshape(2, 1, -1)
    early_ids, late_ids = [early_ids[0], early_ids[1]], [late_ids[0], late_ids[1]]
    rep_scalar = rep.astype(jnp.int32).reshape(1)
    stats = jnp.zeros((8 * lines, 128), jnp.float32)

    held = {(0, 0, 0): normed}
    early_exp = None

    def logits(group, stats, *gates, first_row=0, exp_rows=None, into=None):
        blocks = [held[block] for block in group]
        blocks[0] = after(blocks[0], *gates)
        rows = [stat_row(block) for block in group]
        exp_rows = exp_rows or len(group) * length
        return round_logits(blocks, rows, head_weight, stats, first_row, exp_rows, into)

    def diagonal(turn):
        if turn % 2 == 0:
            return to_x(held[1, 0, turn])
        return to_y(held[0, 1, turn])

    for turn in range(lines):
        block = held[0, 0, turn]
        following = to_z(block, 1) if turn + 1 < lines else None
        held[0, 1, turn] = to_x(block)
        held[1, 0, turn] = to_y(block)
        if turn + 1 < lines:
            arrived = [following, held[0, 1, turn], held[1, 0, turn]]
            if turn == 0:
                head_weight, *late_ids = prepared(head_weight, *late_ids, *early_ids, stats)
                arrived += [*early_ids, *late_ids, rep_scalar, stats, head_weight]
            elif turn < split:
                arrived += [early_exp]
            else:
                middle_exp, stats = logits(
                    groups[split], stats, exp_rows=6 * length
                )
                arrived += [early_exp, middle_exp]
            arrived = lax.optimization_barrier(tuple(arrived))
            held[0, 0, turn + 1], held[0, 1, turn], held[1, 0, turn] = arrived[:3]
            if turn == 0:
                early_ids, late_ids = list(arrived[3:5]), list(arrived[5:7])
                rep_scalar, stats, head_weight = arrived[7:]
            else:
                early_exp = arrived[3]
                if turn == split:
                    middle_exp = arrived[4]
            held[1, 1, turn] = diagonal(turn)
        if turn < split:
            size = len(groups[turn]) * length
            early_exp, stats = logits(
                groups[turn], stats, held[0, 0, turn + 1],
                first_row=turn * size, exp_rows=split * size, into=early_exp,
            )

    early = [held[block] for block in early_blocks]
    early[0] = after(early[0], held[0, 0, lines - 1])
    early = turned_features(rep_scalar, early, rows)
    early = [early[0], to_core(early[1])]
    middle_exp, stats = logits(
        groups[split + 1], stats, held[0, 0, lines - 1], early[0],
        first_row=2 * length, exp_rows=6 * length, into=middle_exp,
    )
    held[0, 1, lines - 1] = after(held[0, 1, lines - 1], middle_exp)
    held[1, 1, lines - 1] = diagonal(lines - 1)
    early_ids[0] = after(early_ids[0], middle_exp, held[0, 1, lines - 1])
    sums = one_hot_sums(early, early_ids, columns)
    late = [held[block] for block in late_blocks]
    late[0] = after(late[0], *sums)
    late = turned_features(rep_scalar, late, rows)
    late = [late[0], to_core(late[1])]
    ready = lax.optimization_barrier((early_exp, middle_exp, late[0]))
    other_exps = [to_core(exp) for exp in ready[:2]]
    last_exp, stats = logits(groups[-1], stats, late[0], *sums)
    exps = [early_exp, middle_exp, last_exp]
    across_stats, core_stats, both_stats = to_y(stats), to_core(stats), to_y_core(stats)
    merged, first = merged_stats(
        after(stats, late[1], *other_exps), across_stats, core_stats, both_stats
    )
    all_stats = [merged] + [to_z(merged, -along) for along in range(1, lines)]
    other_exps.append(to_core(after(last_exp, merged)))
    return tuple(refresh_states(
        lines, length, [stat_row(block) for block in early_blocks + late_blocks], early, late,
        exps + other_exps, all_stats, first, late_ids, sums, moment, curvature,
    ))


def solution(mesh):
    in_specs = (
        P(("rep", "shard"), None),
        P(),
        P(),
        P(),
        P(None, "shard"),
        P("rep", "shard"),
        P("rep", "shard"),
    )
    out_specs = (P("rep", "shard"), P("rep", "shard"), P("rep", "shard"))
    reps, shards = mesh.shape["rep"], mesh.shape["shard"]

    def whole(hidden, *others):
        tokens, depth = hidden.shape
        length = tokens // (reps * shards)
        fits = hidden.size * 2 <= GATHER_BYTES and reps == 4 and shards == 8
        if fits and length == 64 and (depth // reps) % 128 == 0:
            plan = functools.partial(all_tokens, reps, shards)
        else:
            plan = by_groups

        return jax.shard_map(
            plan, mesh=mesh, in_specs=in_specs, out_specs=out_specs, check_vma=False
        )(hidden, *others)

    return whole
```

```python
import functools

import jax
import jax.numpy as jnp
import numpy as np
from jax import lax
from jax.experimental import pallas as pl
from jax.experimental.pallas import tpu as pltpu
from jax.sharding import PartitionSpec as P

EPS_NORM = 1e-05
BETA_ONE = 0.96
BETA_TWO = 0.95
RHO_SCALE = 0.05
GATHER_BYTES = 32 * 1024 * 1024
LOGITS_VMEM = 20 * 1024 * 1024
BRIEF = pl.CostEstimate(flops=1024, bytes_accessed=1024, transcendentals=0)


def normalize(hidden, norm_gain):
    values = hidden.astype(jnp.float32)
    row_scale = lax.rsqrt(jnp.mean(values * values, axis=-1, keepdims=True) + EPS_NORM)
    return (values * row_scale * norm_gain).astype(jnp.bfloat16)


def refresh(gradient, sample_grad, moment, curvature):
    moment_new = BETA_ONE * moment.astype(jnp.float32) + (1.0 - BETA_ONE) * gradient
    curvature_new = (
        BETA_TWO * curvature.astype(jnp.float32) + (1.0 - BETA_TWO) * sample_grad * sample_grad
    )
    update_direction = jnp.clip(moment_new / (RHO_SCALE * curvature_new), -1.0, 1.0)
    return (
        moment_new.astype(jnp.bfloat16),
        curvature_new.astype(jnp.bfloat16),
        update_direction.astype(jnp.bfloat16),
    )


def by_groups(hidden, norm_gain, input_ids, sampled_ids, head_weight, moment, curvature):
    normed = normalize(hidden, norm_gain)
    gathered = lax.all_gather(normed, "shard", axis=0, tiled=True)
    group_len = gathered.shape[0]
    columns = head_weight.shape[1]
    first_col = lax.axis_index("shard") * columns
    logits = jnp.dot(gathered, head_weight, preferred_element_type=jnp.float32)
    row_peak = lax.pmax(jnp.max(logits, axis=-1), "shard")
    scaled_exp = jnp.exp(logits - row_peak[:, None])
    row_sum = lax.psum(jnp.sum(scaled_exp, axis=-1), "shard")
    probabilities = (scaled_exp / row_sum[:, None]).astype(jnp.bfloat16)
    group_start = lax.axis_index("rep") * group_len
    token_ids = lax.dynamic_slice_in_dim(input_ids, group_start, group_len, 0)
    sample_ids = lax.dynamic_slice_in_dim(sampled_ids, group_start, group_len, 0)
    position = jnp.arange(group_len)
    shifted = jnp.roll(token_ids, -1) - first_col
    usable = (position < group_len - 1) & (shifted >= 0) & (shifted < columns)
    true_slot = jnp.where(usable, shifted, columns)
    sample_local = sample_ids - first_col
    inside = (sample_local >= 0) & (sample_local < columns)
    sample_slot = jnp.where(inside, sample_local, columns)
    shared = lax.dot_general(
        gathered, probabilities, (((0,), (0,)), ((), ())), preferred_element_type=jnp.float32
    )
    widened = gathered.astype(jnp.float32)
    true_sums = jax.ops.segment_sum(widened, true_slot, num_segments=columns + 1)[:columns]
    sample_sums = jax.ops.segment_sum(widened, sample_slot, num_segments=columns + 1)[:columns]
    true_part = (shared - true_sums.T).astype(jnp.bfloat16)
    sample_part = (shared - sample_sums.T).astype(jnp.bfloat16)
    gradient = lax.psum_scatter(true_part, "rep", scatter_dimension=0, tiled=True)
    sample_grad = lax.psum_scatter(sample_part, "rep", scatter_dimension=0, tiled=True)
    return refresh(
        gradient.astype(jnp.float32), sample_grad.astype(jnp.float32), moment, curvature
    )


def swap_pairs(count, bit):
    return [(index, index ^ bit) for index in range(count)]


def shift_pairs(lines, along, across):
    pairs = []
    for place in range(lines):
        for side in range(2):
            source = 2 * place + side
            pairs.append((source, 2 * ((place + along) % lines) + (side ^ across)))
    return pairs


def normalize_kernel(hidden_ref, gain_ref, normed_ref):
    normed_ref[...] = normalize(hidden_ref[...], gain_ref[...])


def normalized(hidden, norm_gain):
    return pl.pallas_call(
        normalize_kernel,
        out_shape=jax.ShapeDtypeStruct(hidden.shape, jnp.bfloat16),
        compiler_params=pltpu.CompilerParams(vmem_limit_bytes=8 * 1024 * 1024),
        cost_estimate=BRIEF,
        name="normalized",
    )(*in_hbm([hidden]), norm_gain)


def prepare_kernel(weight_ref, true_ids, sample_ids, *refs):
    held_ref, true_at, sample_at, arrived = refs[-4:]
    count = arrived.shape[0]
    band = weight_ref.shape[0] // count
    copies = [
        pltpu.make_async_copy(
            weight_ref.at[pl.ds(index * band, band)], held_ref.at[pl.ds(index * band, band)],
            arrived.at[index],
        )
        for index in range(count)
    ]
    for copy in copies:
        copy.start()
    lanes = lax.broadcasted_iota(jnp.int32, (128, 128), 1)
    for ids_ref, out_ref in ((true_ids, true_at), (sample_ids, sample_at)):
        for place in range(0, out_ref.shape[0], 128):
            ids = jnp.broadcast_to(ids_ref[:, place:place + 128], (128, 128)).T
            out_ref[place:place + 128] = ids - lanes
    for copy in copies:
        copy.wait()


def prepared(weight, true_ids, sample_ids, *earlier):
    near = pl.BlockSpec(memory_space=pltpu.VMEM)
    late = jax.ShapeDtypeStruct((true_ids.shape[1], 128), jnp.int32)
    return pl.pallas_call(
        prepare_kernel,
        in_specs=[pl.BlockSpec(memory_space=pltpu.HBM)] + [near] * (2 + len(earlier)),
        out_specs=[near] * 3,
        out_shape=[pltpu.VMEM(weight.shape, weight.dtype), late, late],
        scratch_shapes=[pltpu.SemaphoreType.DMA((4,))],
        compiler_params=pltpu.CompilerParams(vmem_limit_bytes=8 * 1024 * 1024),
        cost_estimate=BRIEF,
        name="prepared",
    )(pltpu.with_memory_space_constraint(weight, pltpu.HBM), true_ids, sample_ids, *earlier)


def logits_kernel(stat_rows, first_row, joins, *refs):
    count = len(stat_rows)
    block_refs, refs = refs[:count], refs[count:]
    if joins:
        refs = refs[:2] + refs[3:]
    weight_ref, before_ref, exp_ref, stats_ref, rows, logits, scaled_exp, highs, sums, sent = refs
    tokens, columns = logits.shape
    length = tokens // count
    half = stats_ref.shape[0] // 2
    for index, ref in enumerate(block_refs):
        rows[index * length:(index + 1) * length] = ref[...]
    highs[...] = jnp.full(highs.shape, -jnp.inf, jnp.float32)
    width = min(256, columns)

    def multiply(index, carry):
        place = pl.ds(pl.multiple_of(index * width, width), width)
        part = jnp.dot(rows[...], weight_ref[:, place], preferred_element_type=jnp.float32)
        logits[:, place] = part
        high = functools.reduce(
            jnp.maximum, [part[:, lane:lane + 128] for lane in range(0, width, 128)]
        )
        highs[...] = jnp.maximum(highs[...], high)
        return carry

    lax.fori_loop(0, columns // width, multiply, 0)
    highs[...] = jnp.broadcast_to(jnp.max(highs[...], axis=1, keepdims=True), highs.shape)
    chunk = 16
    copies = []
    for block in range(count):

        def scale(index, carry, block=block):
            place = pl.ds(pl.multiple_of(block * length + index * chunk, chunk), chunk)
            peak = highs[place, :]
            total = jnp.zeros((chunk, 128), jnp.float32)
            for lane in range(0, columns, 128):
                scaled = jnp.exp(logits[place, lane:lane + 128] - peak)
                scaled_exp[place, lane:lane + 128] = scaled.astype(jnp.bfloat16)
                total += scaled
            sums[place, :] = total
            return carry

        lax.fori_loop(0, length // chunk, scale, 0, unroll=2)
        place = pl.ds(block * length, length)
        target = pl.ds(first_row + block * length, length)
        copies.append(
            pltpu.make_async_copy(scaled_exp.at[place], exp_ref.at[target], sent.at[block])
        )
        copies[-1].start()
    totals = jnp.broadcast_to(jnp.sum(sums[...], axis=1, keepdims=True), sums.shape)
    stats_ref[...] = before_ref[...]
    for base, values in ((0, highs[...].T[0:1]), (half, totals.T[0:1])):
        for index, row in enumerate(stat_rows):
            stats_ref[base + row:base + row + 1, :length] = (
                values[:, index * length:(index + 1) * length]
            )
    for copy in copies:
        copy.wait()


def round_logits(blocks, stat_rows, held_weight, before, first_row, exp_rows, into):
    depth, columns = held_weight.shape
    length = blocks[0].shape[0]
    tokens = length * len(blocks)
    near = pl.BlockSpec(memory_space=pltpu.VMEM)
    held_weight = pltpu.with_memory_space_constraint(held_weight, pltpu.VMEM)
    far = pl.BlockSpec(memory_space=pltpu.HBM)
    joins = [] if into is None else [pltpu.with_memory_space_constraint(into, pltpu.HBM)]
    return pl.pallas_call(
        functools.partial(logits_kernel, stat_rows, first_row, len(joins)),
        in_specs=[near] * (len(blocks) + 2) + [far] * len(joins),
        input_output_aliases={len(blocks) + 2: 0} if joins else {},
        out_specs=[far, near],
        out_shape=[
            pltpu.HBM((exp_rows, columns), jnp.bfloat16),
            jax.ShapeDtypeStruct(before.shape, jnp.float32),
        ],
        scratch_shapes=[
            pltpu.VMEM((tokens, depth), jnp.bfloat16),
            pltpu.VMEM((tokens, columns), jnp.float32),
            pltpu.VMEM((tokens, columns), jnp.bfloat16),
            pltpu.VMEM((tokens, 128), jnp.float32),
            pltpu.VMEM((tokens, 128), jnp.float32),
            pltpu.SemaphoreType.DMA((len(blocks),)),
        ],
        compiler_params=pltpu.CompilerParams(vmem_limit_bytes=LOGITS_VMEM),
        cost_estimate=BRIEF,
        name="round_logits",
    )(*blocks, held_weight, before, *joins)


def turn_kernel(count, rep_ref, *refs):
    mine_ref, other_ref = refs[count:]
    step = pl.program_id(0)
    turned = jnp.concatenate([ref[...] for ref in refs[:count]], axis=0).T

    @pl.when(step == 0)
    def _():
        mine_ref[...] = turned

    @pl.when(step == 1)
    def _():
        other_ref[...] = turned


def turned_features(rep, blocks, rows):
    length = blocks[0].shape[0]
    tokens = length * len(blocks)
    whole = pl.BlockSpec((rows, tokens), lambda step, rep_ref: (0, 0))
    block = pl.BlockSpec((length, rows), lambda step, rep_ref: (0, rep_ref[0] ^ step))
    return pl.pallas_call(
        functools.partial(turn_kernel, len(blocks)),
        grid_spec=pltpu.PrefetchScalarGridSpec(
            num_scalar_prefetch=1,
            grid=(2,),
            in_specs=[block] * len(blocks),
            out_specs=[whole, whole],
        ),
        out_shape=[jax.ShapeDtypeStruct((rows, tokens), jnp.bfloat16)] * 2,
        compiler_params=pltpu.CompilerParams(vmem_limit_bytes=20 * 1024 * 1024),
        cost_estimate=BRIEF,
        name="turned_features",
    )(rep, *blocks)


def one_hot_kernel(count, *refs):
    feature_refs, refs = refs[:count], refs[count:]
    true_ref, sample_ref, true_out, sample_out = refs
    width = true_out.shape[1]
    features = jnp.concatenate([ref[...] for ref in feature_refs], axis=1)
    columns = pl.program_id(0) * width + lax.broadcasted_iota(
        jnp.int32, (width, features.shape[1]), 0
    )
    hot = jnp.concatenate([columns == true_ref[...], columns == sample_ref[...]], axis=0)
    totals = lax.dot_general(
        features, hot.astype(jnp.float32).astype(jnp.bfloat16),
        (((1,), (1,)), ((), ())), preferred_element_type=jnp.float32,
    )
    true_out[...] = totals[:, :width].astype(jnp.bfloat16)
    sample_out[...] = totals[:, width:].astype(jnp.bfloat16)


def one_hot_sums(features, ids, columns):
    rows = features[0].shape[0]
    width = min(256, columns)
    whole = lambda array: pl.BlockSpec(array.shape, lambda step: (0, 0))
    tile = pl.BlockSpec((rows, width), lambda step: (0, step))
    return pl.pallas_call(
        functools.partial(one_hot_kernel, len(features)),
        grid=(columns // width,),
        in_specs=[whole(array) for array in (*features, *ids)],
        out_specs=[tile, tile],
        out_shape=[pltpu.HBM((rows, columns), jnp.bfloat16)] * 2,
        compiler_params=pltpu.CompilerParams(vmem_limit_bytes=24 * 1024 * 1024),
        cost_estimate=BRIEF,
        name="one_hot_sums",
    )(*features, *ids)


def merge_kernel(own_ref, across_ref, core_ref, both_ref, merged_ref, first_ref):
    rows = own_ref.shape[0] // 2
    side = rows // 2
    for core, (near, far) in enumerate(((own_ref, across_ref), (core_ref, both_ref))):
        place = core * rows
        first, total = near[:rows], near[rows:]
        second = jnp.concatenate([far[side:rows], far[:side]], axis=0)
        other = jnp.concatenate([far[rows + side:], far[rows:rows + side]], axis=0)
        peak = jnp.maximum(first, second)
        merged_ref[place:place + rows] = peak
        merged_ref[2 * rows + place:3 * rows + place] = (
            total * jnp.exp(first - peak) + other * jnp.exp(second - peak)
        )
        first_ref[place:place + rows] = first


def merged_stats(own, across, core, both):
    rows, lanes = own.shape
    return pl.pallas_call(
        merge_kernel,
        out_shape=[
            jax.ShapeDtypeStruct((2 * rows, lanes), jnp.float32),
            jax.ShapeDtypeStruct((rows, lanes), jnp.float32),
        ],
        compiler_params=pltpu.CompilerParams(vmem_limit_bytes=4 * 1024 * 1024),
        cost_estimate=BRIEF,
        name="merged_stats",
    )(own, across, core, both)


def refresh_kernel(lines, length, block_rows, *refs):
    early_refs, late_refs, refs = refs[:2], refs[2:4], refs[4:]
    exp_refs, refs = refs[:6], refs[6:]
    stats_refs, refs = refs[:lines], refs[lines:]
    (first_ref, true_at, sample_at, true_sum, sample_sum, moment_ref, curvature_ref,
     moment_out, curvature_out, update_out, factors) = refs
    step = pl.program_id(0)
    width = moment_out.shape[1]
    early = early_refs[0].shape[1]
    late = late_refs[0].shape[1]

    @pl.when(step == 0)
    def _():
        rows = first_ref.shape[0]

        def turned(values, along):
            return jnp.concatenate([
                values[group + (turn + along) % lines:group + (turn + along) % lines + 1]
                for group in range(0, rows, lines) for turn in range(lines)
            ], axis=0) if along else values

        peaks = [turned(ref[:rows], along) for along, ref in enumerate(stats_refs)]
        totals = [turned(ref[rows:], along) for along, ref in enumerate(stats_refs)]
        peak = functools.reduce(jnp.maximum, peaks)
        total = sum(t * jnp.exp(p - peak) for p, t in zip(peaks, totals))
        factor = jnp.exp(first_ref[...] - peak) / total
        per_core = rows // 2
        full = jnp.concatenate([factor, jnp.zeros((128 - rows, 128), jnp.float32)], axis=0).T
        for core in range(2):
            for index, row in enumerate(block_rows):
                place = (core * len(block_rows) + index) * length
                at = core * per_core + row
                factors[place:place + length] = jnp.broadcast_to(
                    full[:length, at:at + 1], (length, 128)
                )

    def probs(ref, place, lane):
        scale = factors[place:place + ref.shape[0]]
        return ref[:, lane:lane + 128].astype(jnp.float32) * scale

    early_sides, true_sides, sample_sides = [], [], []
    for core in range(2):
        first_exp, *late_exps = exp_refs[3 * core:3 * core + 3]
        place = core * (early + late)
        early_sides.append(jnp.concatenate([
            probs(first_exp, place, lane).astype(jnp.bfloat16) for lane in range(0, width, 128)
        ], axis=1))
        place += early
        at = core * late
        for ref in late_exps:
            rows = slice(at, at + ref.shape[0])
            true_parts, sample_parts = [], []
            for lane in range(0, width, 128):
                prob = probs(ref, place, lane)
                column = step * width + lane
                true_hot = jnp.where(true_at[rows] == column, 1.0, 0.0)
                sample_hot = jnp.where(sample_at[rows] == column, 1.0, 0.0)
                true_parts.append((prob - true_hot).astype(jnp.bfloat16))
                sample_parts.append((prob - sample_hot).astype(jnp.bfloat16))
            true_sides.append(jnp.concatenate(true_parts, axis=1))
            sample_sides.append(jnp.concatenate(sample_parts, axis=1))
            place += ref.shape[0]
            at += ref.shape[0]
    early_features = jnp.concatenate([ref[...] for ref in early_refs], axis=1)
    late_features = jnp.concatenate([ref[...] for ref in late_refs], axis=1)

    def product(features, sides):
        return jnp.dot(
            features, jnp.concatenate(sides, axis=0), preferred_element_type=jnp.float32
        )

    shared = product(early_features, early_sides)
    gradient = product(late_features, true_sides) + (shared - true_sum[...].astype(jnp.float32))
    sample_grad = product(late_features, sample_sides) + (
        shared - sample_sum[...].astype(jnp.float32)
    )
    moment_out[...], curvature_out[...], update_out[...] = refresh(
        gradient, sample_grad, moment_ref[...], curvature_ref[...]
    )


def refresh_states(lines, length, block_rows, early, late, exps, stats, first,
                   late_ids, sums, moment, curvature):
    rows, columns = moment.shape
    width = min(256, columns)
    whole = lambda array: pl.BlockSpec(array.shape, lambda step: (0, 0))
    tile = pl.BlockSpec((rows, width), lambda step: (0, step))
    return pl.pallas_call(
        functools.partial(refresh_kernel, lines, length, block_rows),
        grid=(columns // width,),
        in_specs=[whole(array) for array in (*early, *late)]
        + [pl.BlockSpec((array.shape[0], width), lambda step: (0, step)) for array in exps]
        + [whole(array) for array in (*stats, first, *late_ids)]
        + [tile] * 4,
        out_specs=[tile] * 3,
        out_shape=[jax.ShapeDtypeStruct((rows, columns), jnp.bfloat16)] * 3,
        scratch_shapes=[pltpu.VMEM((2 * length * len(block_rows), 128), jnp.float32)],
        compiler_params=pltpu.CompilerParams(vmem_limit_bytes=36 * 1024 * 1024),
        cost_estimate=BRIEF,
        name="refresh_states",
    )(
        *early, *late, *in_hbm(exps[:3]), *exps[3:], *stats, first, *late_ids,
        *in_hbm(sums, [moment, curvature])
    )


def in_hbm(*lists):
    return [pltpu.with_memory_space_constraint(array, pltpu.HBM) for array in sum(map(list, lists), [])]


def after(value, *others):
    return lax.optimization_barrier((value, *others))[0]


def all_tokens(reps, shards, hidden, norm_gain, input_ids, sampled_ids, head_weight, moment, curvature):
    lines = shards // 2
    length = hidden.shape[0]
    rows, columns = moment.shape
    rep = lax.axis_index("rep")
    shard = lax.axis_index("shard")
    first_col = shard * columns
    group_len = length * shards

    def to_x(values):
        return lax.ppermute(values, "rep", swap_pairs(reps, 2))

    def to_core(values):
        return lax.ppermute(values, "rep", swap_pairs(reps, 1))

    def to_y(values):
        return lax.ppermute(values, "shard", swap_pairs(shards, 1))

    def to_y_core(values):
        pairs = [
            (rep_at * shards + at, (rep_at ^ 1) * shards + (at ^ 1))
            for rep_at in range(reps) for at in range(shards)
        ]
        return lax.ppermute(values, ("rep", "shard"), pairs)

    def to_z(values, along):
        return lax.ppermute(values, "shard", shift_pairs(lines, along, 0))

    split = lines // 2
    plain = [(0, 0), (0, 1), (1, 0)]
    groups = [[(*kind, turn) for kind in plain] for turn in range(split)]
    groups += [
        [(0, 0, split), (1, 1, 0)],
        [(0, 1, split), (1, 0, split), (0, 0, split + 1), (1, 1, 1)],
        [(0, 1, split + 1), (1, 0, split + 1), (1, 1, split), (1, 1, split + 1)],
    ]
    early_blocks, late_blocks = sum(groups[:split], []), sum(groups[split:], [])

    def stat_row(block):
        return (2 * block[0] + block[1]) * lines + block[2]

    normed = normalized(hidden, norm_gain)

    last = jnp.arange(input_ids.shape[0]) % group_len == group_len - 1
    targets = jnp.where(last, -1, jnp.roll(input_ids, -1) - first_col)
    ids = jnp.stack([targets, sampled_ids - first_col]).reshape(2, reps * shards, length)
    side, across, turn = (np.array(values) for values in zip(*(early_blocks + late_blocks)))
    holder = (rep ^ (2 * across[None] + np.arange(2)[:, None])).reshape(-1)
    place = 2 * ((shard // 2 - turn) % lines) + ((shard % 2) ^ side)
    ids = jnp.take(ids, holder * shards + jnp.tile(place, 2), axis=1)
    ids = ids.reshape(2, 2, len(side), length)
    early_ids = ids[:, :, :len(early_blocks)].reshape(2, 1, -1)
    late_ids = ids[:, :, len(early_blocks):].reshape(2, 1, -1)
    early_ids, late_ids = [early_ids[0], early_ids[1]], [late_ids[0], late_ids[1]]
    rep_scalar = rep.astype(jnp.int32).reshape(1)
    stats = jnp.zeros((8 * lines, 128), jnp.float32)

    held = {(0, 0, 0): normed}
    early_exp = None

    def logits(group, stats, *gates, first_row=0, exp_rows=None, into=None):
        blocks = [held[block] for block in group]
        at = -1 if group is groups[0] else 0
        blocks[at] = after(blocks[at], *gates)
        rows = [stat_row(block) for block in group]
        exp_rows = exp_rows or len(group) * length
        return round_logits(blocks, rows, head_weight, stats, first_row, exp_rows, into)

    def diagonal(turn):
        if turn % 2 == 0:
            return to_x(held[1, 0, turn])
        return to_y(held[0, 1, turn])

    for turn in range(lines):
        block = held[0, 0, turn]
        following = to_z(block, 1) if turn + 1 < lines else None
        held[0, 1, turn] = to_x(block)
        held[1, 0, turn] = to_y(block)
        if turn + 1 < lines:
            arrived = [following, held[0, 1, turn], held[1, 0, turn]]
            if turn == 0:
                arrived = [following, *early_ids, *late_ids, stats]
            elif turn < split:
                arrived += [early_exp]
            else:
                middle_exp, stats = logits(
                    groups[split], stats, exp_rows=6 * length
                )
                arrived += [early_exp, middle_exp]
            arrived = lax.optimization_barrier(tuple(arrived))
            held[0, 0, turn + 1] = arrived[0]
            if turn == 0:
                early_ids, late_ids = list(arrived[1:3]), list(arrived[3:5])
                stats, = arrived[5:]
                head_weight, *late_ids = prepared(head_weight, *late_ids, stats)
            else:
                held[0, 1, turn], held[1, 0, turn] = arrived[1:3]
                early_exp = arrived[3]
                if turn == split:
                    middle_exp = arrived[4]
            held[1, 1, turn] = diagonal(turn)
        if turn < split:
            size = len(groups[turn]) * length
            early_exp, stats = logits(
                groups[turn], stats, held[0, 0, turn + 1],
                first_row=turn * size, exp_rows=split * size, into=early_exp,
            )

    early = [held[block] for block in early_blocks]
    early[-1] = after(early[-1], held[0, 0, lines - 1])
    early = turned_features(rep_scalar, early, rows)
    early = [early[0], to_core(early[1])]
    middle_exp, stats = logits(
        groups[split + 1], stats, held[0, 0, lines - 1], early[0],
        first_row=2 * length, exp_rows=6 * length, into=middle_exp,
    )
    held[0, 1, lines - 1] = after(held[0, 1, lines - 1], middle_exp)
    held[1, 1, lines - 1] = diagonal(lines - 1)
    early_ids[0] = after(early_ids[0], middle_exp, held[0, 1, lines - 1])
    sums = one_hot_sums(early, early_ids, columns)
    late = [held[block] for block in late_blocks]
    late[0] = after(late[0], *sums)
    late = turned_features(rep_scalar, late, rows)
    late = [late[0], to_core(late[1])]
    ready = lax.optimization_barrier((early_exp, middle_exp, late[0]))
    other_exps = [to_core(exp) for exp in ready[:2]]
    last_exp, stats = logits(groups[-1], stats, late[0], *sums)
    exps = [early_exp, middle_exp, last_exp]
    across_stats, core_stats, both_stats = to_y(stats), to_core(stats), to_y_core(stats)
    merged, first = merged_stats(
        after(stats, late[1], *other_exps), across_stats, core_stats, both_stats
    )
    all_stats = [merged] + [to_z(merged, -along) for along in range(1, lines)]
    other_exps.append(to_core(after(last_exp, merged)))
    return tuple(refresh_states(
        lines, length, [stat_row(block) for block in early_blocks + late_blocks], early, late,
        exps + other_exps, all_stats, first, late_ids, sums, moment, curvature,
    ))


def solution(mesh):
    in_specs = (
        P(("rep", "shard"), None),
        P(),
        P(),
        P(),
        P(None, "shard"),
        P("rep", "shard"),
        P("rep", "shard"),
    )
    out_specs = (P("rep", "shard"), P("rep", "shard"), P("rep", "shard"))
    reps, shards = mesh.shape["rep"], mesh.shape["shard"]

    def whole(hidden, *others):
        tokens, depth = hidden.shape
        length = tokens // (reps * shards)
        fits = hidden.size * 2 <= GATHER_BYTES and reps == 4 and shards == 8
        if fits and length == 64 and (depth // reps) % 128 == 0:
            plan = functools.partial(all_tokens, reps, shards)
        else:
            plan = by_groups

        return jax.shard_map(
            plan, mesh=mesh, in_specs=in_specs, out_specs=out_specs, check_vma=False
        )(hidden, *others)

    return whole
```

```python
import functools

import jax
import jax.numpy as jnp
import numpy as np
from jax import lax
from jax.experimental import pallas as pl
from jax.experimental.pallas import tpu as pltpu
from jax.sharding import PartitionSpec as P

EPS_NORM = 1e-05
BETA_ONE = 0.96
BETA_TWO = 0.95
RHO_SCALE = 0.05
GATHER_BYTES = 32 * 1024 * 1024
LOGITS_VMEM = 20 * 1024 * 1024
BRIEF = pl.CostEstimate(flops=1024, bytes_accessed=1024, transcendentals=0)


def normalize(hidden, norm_gain):
    values = hidden.astype(jnp.float32)
    row_scale = lax.rsqrt(jnp.mean(values * values, axis=-1, keepdims=True) + EPS_NORM)
    return (values * row_scale * norm_gain).astype(jnp.bfloat16)


def refresh(gradient, sample_grad, moment, curvature):
    moment_new = BETA_ONE * moment.astype(jnp.float32) + (1.0 - BETA_ONE) * gradient
    curvature_new = (
        BETA_TWO * curvature.astype(jnp.float32) + (1.0 - BETA_TWO) * sample_grad * sample_grad
    )
    update_direction = jnp.clip(moment_new / (RHO_SCALE * curvature_new), -1.0, 1.0)
    return (
        moment_new.astype(jnp.bfloat16),
        curvature_new.astype(jnp.bfloat16),
        update_direction.astype(jnp.bfloat16),
    )


def by_groups(hidden, norm_gain, input_ids, sampled_ids, head_weight, moment, curvature):
    normed = normalize(hidden, norm_gain)
    gathered = lax.all_gather(normed, "shard", axis=0, tiled=True)
    group_len = gathered.shape[0]
    columns = head_weight.shape[1]
    first_col = lax.axis_index("shard") * columns
    logits = jnp.dot(gathered, head_weight, preferred_element_type=jnp.float32)
    row_peak = lax.pmax(jnp.max(logits, axis=-1), "shard")
    scaled_exp = jnp.exp(logits - row_peak[:, None])
    row_sum = lax.psum(jnp.sum(scaled_exp, axis=-1), "shard")
    probabilities = (scaled_exp / row_sum[:, None]).astype(jnp.bfloat16)
    group_start = lax.axis_index("rep") * group_len
    token_ids = lax.dynamic_slice_in_dim(input_ids, group_start, group_len, 0)
    sample_ids = lax.dynamic_slice_in_dim(sampled_ids, group_start, group_len, 0)
    position = jnp.arange(group_len)
    shifted = jnp.roll(token_ids, -1) - first_col
    usable = (position < group_len - 1) & (shifted >= 0) & (shifted < columns)
    true_slot = jnp.where(usable, shifted, columns)
    sample_local = sample_ids - first_col
    inside = (sample_local >= 0) & (sample_local < columns)
    sample_slot = jnp.where(inside, sample_local, columns)
    shared = lax.dot_general(
        gathered, probabilities, (((0,), (0,)), ((), ())), preferred_element_type=jnp.float32
    )
    widened = gathered.astype(jnp.float32)
    true_sums = jax.ops.segment_sum(widened, true_slot, num_segments=columns + 1)[:columns]
    sample_sums = jax.ops.segment_sum(widened, sample_slot, num_segments=columns + 1)[:columns]
    true_part = (shared - true_sums.T).astype(jnp.bfloat16)
    sample_part = (shared - sample_sums.T).astype(jnp.bfloat16)
    gradient = lax.psum_scatter(true_part, "rep", scatter_dimension=0, tiled=True)
    sample_grad = lax.psum_scatter(sample_part, "rep", scatter_dimension=0, tiled=True)
    return refresh(
        gradient.astype(jnp.float32), sample_grad.astype(jnp.float32), moment, curvature
    )


def swap_pairs(count, bit):
    return [(index, index ^ bit) for index in range(count)]


def shift_pairs(lines, along, across):
    pairs = []
    for place in range(lines):
        for side in range(2):
            source = 2 * place + side
            pairs.append((source, 2 * ((place + along) % lines) + (side ^ across)))
    return pairs


def normalize_kernel(hidden_ref, gain_ref, normed_ref):
    normed_ref[...] = normalize(hidden_ref[...], gain_ref[...])


def normalized(hidden, norm_gain):
    return pl.pallas_call(
        normalize_kernel,
        out_shape=jax.ShapeDtypeStruct(hidden.shape, jnp.bfloat16),
        compiler_params=pltpu.CompilerParams(vmem_limit_bytes=8 * 1024 * 1024),
        cost_estimate=BRIEF,
        name="normalized",
    )(*in_hbm([hidden]), norm_gain)


def prepare_kernel(weight_ref, true_ids, sample_ids, *refs):
    held_ref, true_at, sample_at, arrived = refs[-4:]
    count = arrived.shape[0]
    band = weight_ref.shape[0] // count
    copies = [
        pltpu.make_async_copy(
            weight_ref.at[pl.ds(index * band, band)], held_ref.at[pl.ds(index * band, band)],
            arrived.at[index],
        )
        for index in range(count)
    ]
    for copy in copies:
        copy.start()
    lanes = lax.broadcasted_iota(jnp.int32, (128, 128), 1)
    for ids_ref, out_ref in ((true_ids, true_at), (sample_ids, sample_at)):
        for place in range(0, out_ref.shape[0], 128):
            ids = jnp.broadcast_to(ids_ref[:, place:place + 128], (128, 128)).T
            out_ref[place:place + 128] = ids - lanes
    for copy in copies:
        copy.wait()


def prepared(weight, true_ids, sample_ids, *earlier):
    near = pl.BlockSpec(memory_space=pltpu.VMEM)
    late = jax.ShapeDtypeStruct((true_ids.shape[1], 128), jnp.int32)
    return pl.pallas_call(
        prepare_kernel,
        in_specs=[pl.BlockSpec(memory_space=pltpu.HBM)] + [near] * (2 + len(earlier)),
        out_specs=[near] * 3,
        out_shape=[pltpu.VMEM(weight.shape, weight.dtype), late, late],
        scratch_shapes=[pltpu.SemaphoreType.DMA((4,))],
        compiler_params=pltpu.CompilerParams(vmem_limit_bytes=8 * 1024 * 1024),
        cost_estimate=BRIEF,
        name="prepared",
    )(pltpu.with_memory_space_constraint(weight, pltpu.HBM), true_ids, sample_ids, *earlier)


def logits_kernel(stat_rows, first_row, joins, *refs):
    count = len(stat_rows)
    block_refs, refs = refs[:count], refs[count:]
    if joins:
        refs = refs[:2] + refs[3:]
    weight_ref, before_ref, exp_ref, stats_ref, rows, logits, scaled_exp, highs, sums, sent = refs
    tokens, columns = logits.shape
    length = tokens // count
    half = stats_ref.shape[0] // 2
    for index, ref in enumerate(block_refs):
        rows[index * length:(index + 1) * length] = ref[...]
    highs[...] = jnp.full(highs.shape, -jnp.inf, jnp.float32)
    width = min(256, columns)

    def multiply(index, carry):
        place = pl.ds(pl.multiple_of(index * width, width), width)
        part = jnp.dot(rows[...], weight_ref[:, place], preferred_element_type=jnp.float32)
        logits[:, place] = part
        high = functools.reduce(
            jnp.maximum, [part[:, lane:lane + 128] for lane in range(0, width, 128)]
        )
        highs[...] = jnp.maximum(highs[...], high)
        return carry

    lax.fori_loop(0, columns // width, multiply, 0)
    highs[...] = jnp.broadcast_to(jnp.max(highs[...], axis=1, keepdims=True), highs.shape)
    chunk = 16
    copies = []
    for block in range(count):

        def scale(index, carry, block=block):
            place = pl.ds(pl.multiple_of(block * length + index * chunk, chunk), chunk)
            peak = highs[place, :]
            total = jnp.zeros((chunk, 128), jnp.float32)
            for lane in range(0, columns, 128):
                scaled = jnp.exp(logits[place, lane:lane + 128] - peak)
                scaled_exp[place, lane:lane + 128] = scaled.astype(jnp.bfloat16)
                total += scaled
            sums[place, :] = total
            return carry

        lax.fori_loop(0, length // chunk, scale, 0, unroll=2)
        place = pl.ds(block * length, length)
        target = pl.ds(first_row + block * length, length)
        copies.append(
            pltpu.make_async_copy(scaled_exp.at[place], exp_ref.at[target], sent.at[block])
        )
        copies[-1].start()
    totals = jnp.broadcast_to(jnp.sum(sums[...], axis=1, keepdims=True), sums.shape)
    stats_ref[...] = before_ref[...]
    for base, values in ((0, highs[...].T[0:1]), (half, totals.T[0:1])):
        for index, row in enumerate(stat_rows):
            stats_ref[base + row:base + row + 1, :length] = (
                values[:, index * length:(index + 1) * length]
            )
    for copy in copies:
        copy.wait()


def round_logits(blocks, stat_rows, held_weight, before, first_row, exp_rows, into):
    depth, columns = held_weight.shape
    length = blocks[0].shape[0]
    tokens = length * len(blocks)
    near = pl.BlockSpec(memory_space=pltpu.VMEM)
    held_weight = pltpu.with_memory_space_constraint(held_weight, pltpu.VMEM)
    far = pl.BlockSpec(memory_space=pltpu.HBM)
    joins = [] if into is None else [pltpu.with_memory_space_constraint(into, pltpu.HBM)]
    return pl.pallas_call(
        functools.partial(logits_kernel, stat_rows, first_row, len(joins)),
        in_specs=[near] * (len(blocks) + 2) + [far] * len(joins),
        input_output_aliases={len(blocks) + 2: 0} if joins else {},
        out_specs=[far, near],
        out_shape=[
            pltpu.HBM((exp_rows, columns), jnp.bfloat16),
            jax.ShapeDtypeStruct(before.shape, jnp.float32),
        ],
        scratch_shapes=[
            pltpu.VMEM((tokens, depth), jnp.bfloat16),
            pltpu.VMEM((tokens, columns), jnp.float32),
            pltpu.VMEM((tokens, columns), jnp.bfloat16),
            pltpu.VMEM((tokens, 128), jnp.float32),
            pltpu.VMEM((tokens, 128), jnp.float32),
            pltpu.SemaphoreType.DMA((len(blocks),)),
        ],
        compiler_params=pltpu.CompilerParams(vmem_limit_bytes=LOGITS_VMEM),
        cost_estimate=BRIEF,
        name="round_logits",
    )(*blocks, held_weight, before, *joins)


def turn_kernel(count, rep_ref, *refs):
    mine_ref, other_ref = refs[count:]
    step = pl.program_id(0)
    turned = jnp.concatenate([ref[...] for ref in refs[:count]], axis=0).T

    @pl.when(step == 0)
    def _():
        mine_ref[...] = turned

    @pl.when(step == 1)
    def _():
        other_ref[...] = turned


def turned_features(rep, blocks, rows):
    length = blocks[0].shape[0]
    tokens = length * len(blocks)
    whole = pl.BlockSpec((rows, tokens), lambda step, rep_ref: (0, 0))
    block = pl.BlockSpec((length, rows), lambda step, rep_ref: (0, rep_ref[0] ^ step))
    return pl.pallas_call(
        functools.partial(turn_kernel, len(blocks)),
        grid_spec=pltpu.PrefetchScalarGridSpec(
            num_scalar_prefetch=1,
            grid=(2,),
            in_specs=[block] * len(blocks),
            out_specs=[whole, whole],
        ),
        out_shape=[jax.ShapeDtypeStruct((rows, tokens), jnp.bfloat16)] * 2,
        compiler_params=pltpu.CompilerParams(vmem_limit_bytes=20 * 1024 * 1024),
        cost_estimate=BRIEF,
        name="turned_features",
    )(rep, *blocks)


def one_hot_kernel(count, *refs):
    feature_refs, refs = refs[:count], refs[count:]
    true_ref, sample_ref, true_out, sample_out = refs
    width = true_out.shape[1]
    features = jnp.concatenate([ref[...] for ref in feature_refs], axis=1)
    columns = pl.program_id(0) * width + lax.broadcasted_iota(
        jnp.int32, (width, features.shape[1]), 0
    )
    hot = jnp.concatenate([columns == true_ref[...], columns == sample_ref[...]], axis=0)
    totals = lax.dot_general(
        features, hot.astype(jnp.float32).astype(jnp.bfloat16),
        (((1,), (1,)), ((), ())), preferred_element_type=jnp.float32,
    )
    true_out[...] = totals[:, :width].astype(jnp.bfloat16)
    sample_out[...] = totals[:, width:].astype(jnp.bfloat16)


def one_hot_sums(features, ids, columns):
    rows = features[0].shape[0]
    width = min(256, columns)
    whole = lambda array: pl.BlockSpec(array.shape, lambda step: (0, 0))
    tile = pl.BlockSpec((rows, width), lambda step: (0, step))
    return pl.pallas_call(
        functools.partial(one_hot_kernel, len(features)),
        grid=(columns // width,),
        in_specs=[whole(array) for array in (*features, *ids)],
        out_specs=[tile, tile],
        out_shape=[pltpu.HBM((rows, columns), jnp.bfloat16)] * 2,
        compiler_params=pltpu.CompilerParams(vmem_limit_bytes=24 * 1024 * 1024),
        cost_estimate=BRIEF,
        name="one_hot_sums",
    )(*features, *ids)


def merge_kernel(own_ref, across_ref, core_ref, both_ref, merged_ref, first_ref):
    rows = own_ref.shape[0] // 2
    side = rows // 2
    for core, (near, far) in enumerate(((own_ref, across_ref), (core_ref, both_ref))):
        place = core * rows
        first, total = near[:rows], near[rows:]
        second = jnp.concatenate([far[side:rows], far[:side]], axis=0)
        other = jnp.concatenate([far[rows + side:], far[rows:rows + side]], axis=0)
        peak = jnp.maximum(first, second)
        merged_ref[place:place + rows] = peak
        merged_ref[2 * rows + place:3 * rows + place] = (
            total * jnp.exp(first - peak) + other * jnp.exp(second - peak)
        )
        first_ref[place:place + rows] = first


def merged_stats(own, across, core, both):
    rows, lanes = own.shape
    return pl.pallas_call(
        merge_kernel,
        out_shape=[
            jax.ShapeDtypeStruct((2 * rows, lanes), jnp.float32),
            jax.ShapeDtypeStruct((rows, lanes), jnp.float32),
        ],
        compiler_params=pltpu.CompilerParams(vmem_limit_bytes=4 * 1024 * 1024),
        cost_estimate=BRIEF,
        name="merged_stats",
    )(own, across, core, both)


def refresh_kernel(lines, length, block_rows, *refs):
    early_refs, late_refs, refs = refs[:2], refs[2:4], refs[4:]
    exp_refs, refs = refs[:6], refs[6:]
    stats_refs, refs = refs[:lines], refs[lines:]
    (first_ref, true_at, sample_at, true_sum, sample_sum, moment_ref, curvature_ref,
     moment_out, curvature_out, update_out, factors) = refs
    step = pl.program_id(0)
    width = moment_out.shape[1]
    early = early_refs[0].shape[1]
    late = late_refs[0].shape[1]

    @pl.when(step == 0)
    def _():
        rows = first_ref.shape[0]

        def turned(values, along):
            return jnp.concatenate([
                values[group + (turn + along) % lines:group + (turn + along) % lines + 1]
                for group in range(0, rows, lines) for turn in range(lines)
            ], axis=0) if along else values

        peaks = [turned(ref[:rows], along) for along, ref in enumerate(stats_refs)]
        totals = [turned(ref[rows:], along) for along, ref in enumerate(stats_refs)]
        peak = functools.reduce(jnp.maximum, peaks)
        total = sum(t * jnp.exp(p - peak) for p, t in zip(peaks, totals))
        factor = jnp.exp(first_ref[...] - peak) / total
        per_core = rows // 2
        full = jnp.concatenate([factor, jnp.zeros((128 - rows, 128), jnp.float32)], axis=0).T
        for core in range(2):
            for index, row in enumerate(block_rows):
                place = (core * len(block_rows) + index) * length
                at = core * per_core + row
                factors[place:place + length] = jnp.broadcast_to(
                    full[:length, at:at + 1], (length, 128)
                )

    def probs(ref, place, lane):
        scale = factors[place:place + ref.shape[0]]
        return ref[:, lane:lane + 128].astype(jnp.float32) * scale

    early_sides, true_sides, sample_sides = [], [], []
    for core in range(2):
        first_exp, *late_exps = exp_refs[3 * core:3 * core + 3]
        place = core * (early + late)
        early_sides.append(jnp.concatenate([
            probs(first_exp, place, lane).astype(jnp.bfloat16) for lane in range(0, width, 128)
        ], axis=1))
        place += early
        at = core * late
        for ref in late_exps:
            rows = slice(at, at + ref.shape[0])
            true_parts, sample_parts = [], []
            for lane in range(0, width, 128):
                prob = probs(ref, place, lane)
                column = step * width + lane
                true_hot = jnp.where(true_at[rows] == column, 1.0, 0.0)
                sample_hot = jnp.where(sample_at[rows] == column, 1.0, 0.0)
                true_parts.append((prob - true_hot).astype(jnp.bfloat16))
                sample_parts.append((prob - sample_hot).astype(jnp.bfloat16))
            true_sides.append(jnp.concatenate(true_parts, axis=1))
            sample_sides.append(jnp.concatenate(sample_parts, axis=1))
            place += ref.shape[0]
            at += ref.shape[0]
    early_features = jnp.concatenate([ref[...] for ref in early_refs], axis=1)
    late_features = jnp.concatenate([ref[...] for ref in late_refs], axis=1)

    def product(features, sides):
        return jnp.dot(
            features, jnp.concatenate(sides, axis=0), preferred_element_type=jnp.float32
        )

    shared = product(early_features, early_sides)
    gradient = product(late_features, true_sides) + (shared - true_sum[...].astype(jnp.float32))
    sample_grad = product(late_features, sample_sides) + (
        shared - sample_sum[...].astype(jnp.float32)
    )
    moment_out[...], curvature_out[...], update_out[...] = refresh(
        gradient, sample_grad, moment_ref[...], curvature_ref[...]
    )


def refresh_states(lines, length, block_rows, early, late, exps, stats, first,
                   late_ids, sums, moment, curvature):
    rows, columns = moment.shape
    width = min(256, columns)
    whole = lambda array: pl.BlockSpec(array.shape, lambda step: (0, 0))
    tile = pl.BlockSpec((rows, width), lambda step: (0, step))
    return pl.pallas_call(
        functools.partial(refresh_kernel, lines, length, block_rows),
        grid=(columns // width,),
        in_specs=[whole(array) for array in (*early, *late)]
        + [pl.BlockSpec((array.shape[0], width), lambda step: (0, step)) for array in exps]
        + [whole(array) for array in (*stats, first, *late_ids)]
        + [tile] * 4,
        out_specs=[tile] * 3,
        out_shape=[jax.ShapeDtypeStruct((rows, columns), jnp.bfloat16)] * 3,
        scratch_shapes=[pltpu.VMEM((2 * length * len(block_rows), 128), jnp.float32)],
        compiler_params=pltpu.CompilerParams(vmem_limit_bytes=36 * 1024 * 1024),
        cost_estimate=BRIEF,
        name="refresh_states",
    )(
        *early, *late, *in_hbm(exps[:3]), *exps[3:], *stats, first, *late_ids,
        *in_hbm(sums, [moment, curvature])
    )


def in_hbm(*lists):
    return [pltpu.with_memory_space_constraint(array, pltpu.HBM) for array in sum(map(list, lists), [])]


def after(value, *others):
    return lax.optimization_barrier((value, *others))[0]


def all_tokens(reps, shards, hidden, norm_gain, input_ids, sampled_ids, head_weight, moment, curvature):
    lines = shards // 2
    length = hidden.shape[0]
    rows, columns = moment.shape
    rep = lax.axis_index("rep")
    shard = lax.axis_index("shard")
    first_col = shard * columns
    group_len = length * shards

    def to_x(values):
        return lax.ppermute(values, "rep", swap_pairs(reps, 2))

    def to_core(values):
        return lax.ppermute(values, "rep", swap_pairs(reps, 1))

    def to_y(values):
        return lax.ppermute(values, "shard", swap_pairs(shards, 1))

    def to_y_core(values):
        pairs = [
            (rep_at * shards + at, (rep_at ^ 1) * shards + (at ^ 1))
            for rep_at in range(reps) for at in range(shards)
        ]
        return lax.ppermute(values, ("rep", "shard"), pairs)

    def to_z(values, along):
        return lax.ppermute(values, "shard", shift_pairs(lines, along, 0))

    split = lines // 2
    plain = [(0, 0), (0, 1), (1, 0)]
    groups = [[(*kind, turn) for kind in plain] for turn in range(split)]
    groups += [
        [(0, 0, split), (1, 1, 0)],
        [(0, 1, split), (1, 0, split), (0, 0, split + 1)],
        [(0, 1, split + 1), (1, 0, split + 1)] + [(1, 1, turn) for turn in range(1, lines)],
    ]
    early_blocks, late_blocks = sum(groups[:split], []), sum(groups[split:], [])

    def stat_row(block):
        return (2 * block[0] + block[1]) * lines + block[2]

    normed = normalized(hidden, norm_gain)

    last = jnp.arange(input_ids.shape[0]) % group_len == group_len - 1
    targets = jnp.where(last, -1, jnp.roll(input_ids, -1) - first_col)
    ids = jnp.stack([targets, sampled_ids - first_col]).reshape(2, reps * shards, length)
    side, across, turn = (np.array(values) for values in zip(*(early_blocks + late_blocks)))
    holder = (rep ^ (2 * across[None] + np.arange(2)[:, None])).reshape(-1)
    place = 2 * ((shard // 2 - turn) % lines) + ((shard % 2) ^ side)
    ids = jnp.take(ids, holder * shards + jnp.tile(place, 2), axis=1)
    ids = ids.reshape(2, 2, len(side), length)
    early_ids = ids[:, :, :len(early_blocks)].reshape(2, 1, -1)
    late_ids = ids[:, :, len(early_blocks):].reshape(2, 1, -1)
    early_ids, late_ids = [early_ids[0], early_ids[1]], [late_ids[0], late_ids[1]]
    rep_scalar = rep.astype(jnp.int32).reshape(1)
    stats = jnp.zeros((8 * lines, 128), jnp.float32)

    held = {(0, 0, 0): normed}
    early_exp = None

    def logits(group, stats, *gates, first_row=0, exp_rows=None, into=None):
        blocks = [held[block] for block in group]
        at = -1 if group is groups[0] else 0
        blocks[at] = after(blocks[at], *gates)
        rows = [stat_row(block) for block in group]
        exp_rows = exp_rows or len(group) * length
        return round_logits(blocks, rows, head_weight, stats, first_row, exp_rows, into)

    def diagonal(turn):
        if turn == 1:
            return to_z(held[1, 1, 0], 1)
        if turn == 2:
            return to_x(held[1, 0, turn])
        return to_y(held[0, 1, turn])

    for turn in range(lines):
        block = held[0, 0, turn]
        following = to_z(block, 1) if turn + 1 < lines else None
        held[0, 1, turn] = to_x(block)
        held[1, 0, turn] = to_y(block)
        if turn + 1 < lines:
            arrived = [following, held[0, 1, turn], held[1, 0, turn]]
            if turn == 0:
                arrived = [following, *early_ids, *late_ids, stats]
            elif turn < split:
                arrived += [early_exp]
            else:
                middle_exp, stats = logits(
                    groups[split], stats, exp_rows=5 * length
                )
                arrived = [following, held[0, 1, turn], early_exp, middle_exp]
            arrived = lax.optimization_barrier(tuple(arrived))
            held[0, 0, turn + 1] = arrived[0]
            if turn == 0:
                early_ids, late_ids = list(arrived[1:3]), list(arrived[3:5])
                stats, = arrived[5:]
                head_weight, *late_ids = prepared(head_weight, *late_ids, stats)
            elif turn < split:
                held[0, 1, turn], held[1, 0, turn], early_exp = arrived[1:]
            else:
                held[0, 1, turn], early_exp, middle_exp = arrived[1:]
            held[1, 1, turn] = diagonal(turn)
        if turn < split:
            size = len(groups[turn]) * length
            early_exp, stats = logits(
                groups[turn], stats, held[0, 0, turn + 1],
                first_row=turn * size, exp_rows=split * size, into=early_exp,
            )

    early = [held[block] for block in early_blocks]
    early[-1] = after(early[-1], held[0, 0, lines - 1])
    early = turned_features(rep_scalar, early, rows)
    early = [early[0], to_core(early[1])]
    middle_exp, stats = logits(
        groups[split + 1], stats, held[0, 0, lines - 1], early[0],
        first_row=2 * length, exp_rows=5 * length, into=middle_exp,
    )
    held[0, 1, lines - 1] = after(held[0, 1, lines - 1], middle_exp)
    held[1, 1, lines - 1] = diagonal(lines - 1)
    early_ids[0] = after(early_ids[0], middle_exp, held[0, 1, lines - 1])
    sums = one_hot_sums(early, early_ids, columns)
    late = [held[block] for block in late_blocks]
    late[0] = after(late[0], *sums)
    late = turned_features(rep_scalar, late, rows)
    late = [late[0], to_core(late[1])]
    ready = lax.optimization_barrier((early_exp, middle_exp, late[0]))
    other_exps = [to_core(exp) for exp in ready[:2]]
    last_exp, stats = logits(groups[-1], stats, late[0], *sums)
    exps = [early_exp, middle_exp, last_exp]
    across_stats, core_stats, both_stats = to_y(stats), to_core(stats), to_y_core(stats)
    merged, first = merged_stats(
        after(stats, late[1], *other_exps), across_stats, core_stats, both_stats
    )
    all_stats = [merged] + [to_z(merged, -along) for along in range(1, lines)]
    other_exps.append(to_core(after(last_exp, merged)))
    return tuple(refresh_states(
        lines, length, [stat_row(block) for block in early_blocks + late_blocks], early, late,
        exps + other_exps, all_stats, first, late_ids, sums, moment, curvature,
    ))


def solution(mesh):
    in_specs = (
        P(("rep", "shard"), None),
        P(),
        P(),
        P(),
        P(None, "shard"),
        P("rep", "shard"),
        P("rep", "shard"),
    )
    out_specs = (P("rep", "shard"), P("rep", "shard"), P("rep", "shard"))
    reps, shards = mesh.shape["rep"], mesh.shape["shard"]

    def whole(hidden, *others):
        tokens, depth = hidden.shape
        length = tokens // (reps * shards)
        fits = hidden.size * 2 <= GATHER_BYTES and reps == 4 and shards == 8
        if fits and length == 64 and (depth // reps) % 128 == 0:
            plan = functools.partial(all_tokens, reps, shards)
        else:
            plan = by_groups

        return jax.shard_map(
            plan, mesh=mesh, in_specs=in_specs, out_specs=out_specs, check_vma=False
        )(hidden, *others)

    return whole
```

```python
import functools

import jax
import jax.numpy as jnp
import numpy as np
from jax import lax
from jax.experimental import pallas as pl
from jax.experimental.pallas import tpu as pltpu
from jax.sharding import PartitionSpec as P

EPS_NORM = 1e-05
BETA_ONE = 0.96
BETA_TWO = 0.95
RHO_SCALE = 0.05
GATHER_BYTES = 32 * 1024 * 1024
LOGITS_VMEM = 20 * 1024 * 1024
BRIEF = pl.CostEstimate(flops=1024, bytes_accessed=1024, transcendentals=0)


def normalize(hidden, norm_gain):
    values = hidden.astype(jnp.float32)
    row_scale = lax.rsqrt(jnp.mean(values * values, axis=-1, keepdims=True) + EPS_NORM)
    return (values * row_scale * norm_gain).astype(jnp.bfloat16)


def refresh(gradient, sample_grad, moment, curvature):
    moment_new = BETA_ONE * moment.astype(jnp.float32) + (1.0 - BETA_ONE) * gradient
    curvature_new = (
        BETA_TWO * curvature.astype(jnp.float32) + (1.0 - BETA_TWO) * sample_grad * sample_grad
    )
    update_direction = jnp.clip(moment_new / (RHO_SCALE * curvature_new), -1.0, 1.0)
    return (
        moment_new.astype(jnp.bfloat16),
        curvature_new.astype(jnp.bfloat16),
        update_direction.astype(jnp.bfloat16),
    )


def by_groups(hidden, norm_gain, input_ids, sampled_ids, head_weight, moment, curvature):
    normed = normalize(hidden, norm_gain)
    gathered = lax.all_gather(normed, "shard", axis=0, tiled=True)
    group_len = gathered.shape[0]
    columns = head_weight.shape[1]
    first_col = lax.axis_index("shard") * columns
    logits = jnp.dot(gathered, head_weight, preferred_element_type=jnp.float32)
    row_peak = lax.pmax(jnp.max(logits, axis=-1), "shard")
    scaled_exp = jnp.exp(logits - row_peak[:, None])
    row_sum = lax.psum(jnp.sum(scaled_exp, axis=-1), "shard")
    probabilities = (scaled_exp / row_sum[:, None]).astype(jnp.bfloat16)
    group_start = lax.axis_index("rep") * group_len
    token_ids = lax.dynamic_slice_in_dim(input_ids, group_start, group_len, 0)
    sample_ids = lax.dynamic_slice_in_dim(sampled_ids, group_start, group_len, 0)
    position = jnp.arange(group_len)
    shifted = jnp.roll(token_ids, -1) - first_col
    usable = (position < group_len - 1) & (shifted >= 0) & (shifted < columns)
    true_slot = jnp.where(usable, shifted, columns)
    sample_local = sample_ids - first_col
    inside = (sample_local >= 0) & (sample_local < columns)
    sample_slot = jnp.where(inside, sample_local, columns)
    shared = lax.dot_general(
        gathered, probabilities, (((0,), (0,)), ((), ())), preferred_element_type=jnp.float32
    )
    widened = gathered.astype(jnp.float32)
    true_sums = jax.ops.segment_sum(widened, true_slot, num_segments=columns + 1)[:columns]
    sample_sums = jax.ops.segment_sum(widened, sample_slot, num_segments=columns + 1)[:columns]
    true_part = (shared - true_sums.T).astype(jnp.bfloat16)
    sample_part = (shared - sample_sums.T).astype(jnp.bfloat16)
    gradient = lax.psum_scatter(true_part, "rep", scatter_dimension=0, tiled=True)
    sample_grad = lax.psum_scatter(sample_part, "rep", scatter_dimension=0, tiled=True)
    return refresh(
        gradient.astype(jnp.float32), sample_grad.astype(jnp.float32), moment, curvature
    )


def swap_pairs(count, bit):
    return [(index, index ^ bit) for index in range(count)]


def shift_pairs(lines, along, across):
    pairs = []
    for place in range(lines):
        for side in range(2):
            source = 2 * place + side
            pairs.append((source, 2 * ((place + along) % lines) + (side ^ across)))
    return pairs


def normalize_kernel(hidden_ref, gain_ref, normed_ref):
    normed_ref[...] = normalize(hidden_ref[...], gain_ref[...])


def normalized(hidden, norm_gain):
    return pl.pallas_call(
        normalize_kernel,
        out_shape=jax.ShapeDtypeStruct(hidden.shape, jnp.bfloat16),
        compiler_params=pltpu.CompilerParams(vmem_limit_bytes=8 * 1024 * 1024),
        cost_estimate=BRIEF,
        name="normalized",
    )(*in_hbm([hidden]), norm_gain)


def prepare_kernel(weight_ref, true_ids, sample_ids, *refs):
    held_ref, true_at, sample_at, arrived = refs[-4:]
    count = arrived.shape[0]
    band = weight_ref.shape[0] // count
    copies = [
        pltpu.make_async_copy(
            weight_ref.at[pl.ds(index * band, band)], held_ref.at[pl.ds(index * band, band)],
            arrived.at[index],
        )
        for index in range(count)
    ]
    for copy in copies:
        copy.start()
    lanes = lax.broadcasted_iota(jnp.int32, (128, 128), 1)
    for ids_ref, out_ref in ((true_ids, true_at), (sample_ids, sample_at)):
        for place in range(0, out_ref.shape[0], 128):
            ids = jnp.broadcast_to(ids_ref[:, place:place + 128], (128, 128)).T
            out_ref[place:place + 128] = ids - lanes
    for copy in copies:
        copy.wait()


def prepared(weight, true_ids, sample_ids, *earlier):
    near = pl.BlockSpec(memory_space=pltpu.VMEM)
    late = jax.ShapeDtypeStruct((true_ids.shape[1], 128), jnp.int32)
    return pl.pallas_call(
        prepare_kernel,
        in_specs=[pl.BlockSpec(memory_space=pltpu.HBM)] + [near] * (2 + len(earlier)),
        out_specs=[near] * 3,
        out_shape=[pltpu.VMEM(weight.shape, weight.dtype), late, late],
        scratch_shapes=[pltpu.SemaphoreType.DMA((4,))],
        compiler_params=pltpu.CompilerParams(vmem_limit_bytes=8 * 1024 * 1024),
        cost_estimate=BRIEF,
        name="prepared",
    )(pltpu.with_memory_space_constraint(weight, pltpu.HBM), true_ids, sample_ids, *earlier)


def logits_kernel(stat_rows, first_row, joins, *refs):
    count = len(stat_rows)
    block_refs, refs = refs[:count], refs[count:]
    if joins:
        refs = refs[:2] + refs[3:]
    weight_ref, before_ref, exp_ref, stats_ref, rows, logits, scaled_exp, highs, sums, sent = refs
    tokens, columns = logits.shape
    length = tokens // count
    half = stats_ref.shape[0] // 2
    for index, ref in enumerate(block_refs):
        rows[index * length:(index + 1) * length] = ref[...]
    highs[...] = jnp.full(highs.shape, -jnp.inf, jnp.float32)
    width = min(256, columns)

    def multiply(index, carry):
        place = pl.ds(pl.multiple_of(index * width, width), width)
        part = jnp.dot(rows[...], weight_ref[:, place], preferred_element_type=jnp.float32)
        logits[:, place] = part
        high = functools.reduce(
            jnp.maximum, [part[:, lane:lane + 128] for lane in range(0, width, 128)]
        )
        highs[...] = jnp.maximum(highs[...], high)
        return carry

    lax.fori_loop(0, columns // width, multiply, 0)
    highs[...] = jnp.broadcast_to(jnp.max(highs[...], axis=1, keepdims=True), highs.shape)
    chunk = 16
    copies = []
    for block in range(count):

        def scale(index, carry, block=block):
            place = pl.ds(pl.multiple_of(block * length + index * chunk, chunk), chunk)
            peak = highs[place, :]
            total = jnp.zeros((chunk, 128), jnp.float32)
            for lane in range(0, columns, 128):
                scaled = jnp.exp(logits[place, lane:lane + 128] - peak)
                scaled_exp[place, lane:lane + 128] = scaled.astype(jnp.bfloat16)
                total += scaled
            sums[place, :] = total
            return carry

        lax.fori_loop(0, length // chunk, scale, 0, unroll=2)
        place = pl.ds(block * length, length)
        target = pl.ds(first_row + block * length, length)
        copies.append(
            pltpu.make_async_copy(scaled_exp.at[place], exp_ref.at[target], sent.at[block])
        )
        copies[-1].start()
    totals = jnp.broadcast_to(jnp.sum(sums[...], axis=1, keepdims=True), sums.shape)
    stats_ref[...] = before_ref[...]
    for base, values in ((0, highs[...].T[0:1]), (half, totals.T[0:1])):
        for index, row in enumerate(stat_rows):
            stats_ref[base + row:base + row + 1, :length] = (
                values[:, index * length:(index + 1) * length]
            )
    for copy in copies:
        copy.wait()


def round_logits(blocks, stat_rows, held_weight, before, first_row, exp_rows, into):
    depth, columns = held_weight.shape
    length = blocks[0].shape[0]
    tokens = length * len(blocks)
    near = pl.BlockSpec(memory_space=pltpu.VMEM)
    held_weight = pltpu.with_memory_space_constraint(held_weight, pltpu.VMEM)
    far = pl.BlockSpec(memory_space=pltpu.HBM)
    joins = [] if into is None else [pltpu.with_memory_space_constraint(into, pltpu.HBM)]
    return pl.pallas_call(
        functools.partial(logits_kernel, stat_rows, first_row, len(joins)),
        in_specs=[near] * (len(blocks) + 2) + [far] * len(joins),
        input_output_aliases={len(blocks) + 2: 0} if joins else {},
        out_specs=[far, near],
        out_shape=[
            pltpu.HBM((exp_rows, columns), jnp.bfloat16),
            jax.ShapeDtypeStruct(before.shape, jnp.float32),
        ],
        scratch_shapes=[
            pltpu.VMEM((tokens, depth), jnp.bfloat16),
            pltpu.VMEM((tokens, columns), jnp.float32),
            pltpu.VMEM((tokens, columns), jnp.bfloat16),
            pltpu.VMEM((tokens, 128), jnp.float32),
            pltpu.VMEM((tokens, 128), jnp.float32),
            pltpu.SemaphoreType.DMA((len(blocks),)),
        ],
        compiler_params=pltpu.CompilerParams(vmem_limit_bytes=LOGITS_VMEM),
        cost_estimate=BRIEF,
        name="round_logits",
    )(*blocks, held_weight, before, *joins)


def turn_kernel(count, rep_ref, *refs):
    mine_ref, other_ref = refs[count:]
    step = pl.program_id(0)
    turned = jnp.concatenate([ref[...] for ref in refs[:count]], axis=0).T

    @pl.when(step == 0)
    def _():
        mine_ref[...] = turned

    @pl.when(step == 1)
    def _():
        other_ref[...] = turned


def turned_features(rep, blocks, rows):
    length = blocks[0].shape[0]
    tokens = length * len(blocks)
    whole = pl.BlockSpec((rows, tokens), lambda step, rep_ref: (0, 0))
    block = pl.BlockSpec((length, rows), lambda step, rep_ref: (0, rep_ref[0] ^ step))
    return pl.pallas_call(
        functools.partial(turn_kernel, len(blocks)),
        grid_spec=pltpu.PrefetchScalarGridSpec(
            num_scalar_prefetch=1,
            grid=(2,),
            in_specs=[block] * len(blocks),
            out_specs=[whole, whole],
        ),
        out_shape=[jax.ShapeDtypeStruct((rows, tokens), jnp.bfloat16)] * 2,
        compiler_params=pltpu.CompilerParams(vmem_limit_bytes=20 * 1024 * 1024),
        cost_estimate=BRIEF,
        name="turned_features",
    )(rep, *blocks)


def one_hot_kernel(count, *refs):
    feature_refs, refs = refs[:count], refs[count:]
    true_ref, sample_ref, true_out, sample_out = refs
    width = true_out.shape[1]
    features = jnp.concatenate([ref[...] for ref in feature_refs], axis=1)
    columns = pl.program_id(0) * width + lax.broadcasted_iota(
        jnp.int32, (width, features.shape[1]), 0
    )
    hot = jnp.concatenate([columns == true_ref[...], columns == sample_ref[...]], axis=0)
    totals = lax.dot_general(
        features, hot.astype(jnp.float32).astype(jnp.bfloat16),
        (((1,), (1,)), ((), ())), preferred_element_type=jnp.float32,
    )
    true_out[...] = totals[:, :width].astype(jnp.bfloat16)
    sample_out[...] = totals[:, width:].astype(jnp.bfloat16)


def one_hot_sums(features, ids, columns):
    rows = features[0].shape[0]
    width = min(256, columns)
    whole = lambda array: pl.BlockSpec(array.shape, lambda step: (0, 0))
    tile = pl.BlockSpec((rows, width), lambda step: (0, step))
    return pl.pallas_call(
        functools.partial(one_hot_kernel, len(features)),
        grid=(columns // width,),
        in_specs=[whole(array) for array in (*features, *ids)],
        out_specs=[tile, tile],
        out_shape=[pltpu.HBM((rows, columns), jnp.bfloat16)] * 2,
        compiler_params=pltpu.CompilerParams(vmem_limit_bytes=24 * 1024 * 1024),
        cost_estimate=BRIEF,
        name="one_hot_sums",
    )(*features, *ids)


def merge_kernel(own_ref, across_ref, core_ref, both_ref, merged_ref, first_ref):
    rows = own_ref.shape[0] // 2
    side = rows // 2
    for core, (near, far) in enumerate(((own_ref, across_ref), (core_ref, both_ref))):
        place = core * rows
        first, total = near[:rows], near[rows:]
        second = jnp.concatenate([far[side:rows], far[:side]], axis=0)
        other = jnp.concatenate([far[rows + side:], far[rows:rows + side]], axis=0)
        peak = jnp.maximum(first, second)
        merged_ref[place:place + rows] = peak
        merged_ref[2 * rows + place:3 * rows + place] = (
            total * jnp.exp(first - peak) + other * jnp.exp(second - peak)
        )
        first_ref[place:place + rows] = first


def merged_stats(own, across, core, both):
    rows, lanes = own.shape
    return pl.pallas_call(
        merge_kernel,
        out_shape=[
            jax.ShapeDtypeStruct((2 * rows, lanes), jnp.float32),
            jax.ShapeDtypeStruct((rows, lanes), jnp.float32),
        ],
        compiler_params=pltpu.CompilerParams(vmem_limit_bytes=4 * 1024 * 1024),
        cost_estimate=BRIEF,
        name="merged_stats",
    )(own, across, core, both)


def refresh_kernel(lines, length, block_rows, *refs):
    early_refs, late_refs, refs = refs[:2], refs[2:4], refs[4:]
    exp_refs, refs = refs[:6], refs[6:]
    stats_refs, refs = refs[:lines], refs[lines:]
    (first_ref, true_at, sample_at, true_sum, sample_sum, moment_ref, curvature_ref,
     moment_out, curvature_out, update_out, factors) = refs
    step = pl.program_id(0)
    width = moment_out.shape[1]
    early = early_refs[0].shape[1]
    late = late_refs[0].shape[1]

    @pl.when(step == 0)
    def _():
        rows = first_ref.shape[0]

        def turned(values, along):
            return jnp.concatenate([
                values[group + (turn + along) % lines:group + (turn + along) % lines + 1]
                for group in range(0, rows, lines) for turn in range(lines)
            ], axis=0) if along else values

        peaks = [turned(ref[:rows], along) for along, ref in enumerate(stats_refs)]
        totals = [turned(ref[rows:], along) for along, ref in enumerate(stats_refs)]
        peak = functools.reduce(jnp.maximum, peaks)
        total = sum(t * jnp.exp(p - peak) for p, t in zip(peaks, totals))
        factor = jnp.exp(first_ref[...] - peak) / total
        per_core = rows // 2
        full = jnp.concatenate([factor, jnp.zeros((128 - rows, 128), jnp.float32)], axis=0).T
        for core in range(2):
            for index, row in enumerate(block_rows):
                place = (core * len(block_rows) + index) * length
                at = core * per_core + row
                factors[place:place + length] = jnp.broadcast_to(
                    full[:length, at:at + 1], (length, 128)
                )

    def probs(ref, place, lane):
        scale = factors[place:place + ref.shape[0]]
        return ref[:, lane:lane + 128].astype(jnp.float32) * scale

    early_sides, true_sides, sample_sides = [], [], []
    for core in range(2):
        first_exp, *late_exps = exp_refs[3 * core:3 * core + 3]
        place = core * (early + late)
        early_sides.append(jnp.concatenate([
            probs(first_exp, place, lane).astype(jnp.bfloat16) for lane in range(0, width, 128)
        ], axis=1))
        place += early
        at = core * late
        for ref in late_exps:
            rows = slice(at, at + ref.shape[0])
            true_parts, sample_parts = [], []
            for lane in range(0, width, 128):
                prob = probs(ref, place, lane)
                column = step * width + lane
                true_hot = jnp.where(true_at[rows] == column, 1.0, 0.0)
                sample_hot = jnp.where(sample_at[rows] == column, 1.0, 0.0)
                true_parts.append((prob - true_hot).astype(jnp.bfloat16))
                sample_parts.append((prob - sample_hot).astype(jnp.bfloat16))
            true_sides.append(jnp.concatenate(true_parts, axis=1))
            sample_sides.append(jnp.concatenate(sample_parts, axis=1))
            place += ref.shape[0]
            at += ref.shape[0]
    early_features = jnp.concatenate([ref[...] for ref in early_refs], axis=1)
    late_features = jnp.concatenate([ref[...] for ref in late_refs], axis=1)

    def product(features, sides):
        return jnp.dot(
            features, jnp.concatenate(sides, axis=0), preferred_element_type=jnp.float32
        )

    shared = product(early_features, early_sides)
    gradient = product(late_features, true_sides) + (shared - true_sum[...].astype(jnp.float32))
    sample_grad = product(late_features, sample_sides) + (
        shared - sample_sum[...].astype(jnp.float32)
    )
    moment_out[...], curvature_out[...], update_out[...] = refresh(
        gradient, sample_grad, moment_ref[...], curvature_ref[...]
    )


def refresh_states(lines, length, block_rows, early, late, exps, stats, first,
                   late_ids, sums, moment, curvature):
    rows, columns = moment.shape
    width = min(256, columns)
    whole = lambda array: pl.BlockSpec(array.shape, lambda step: (0, 0))
    tile = pl.BlockSpec((rows, width), lambda step: (0, step))
    return pl.pallas_call(
        functools.partial(refresh_kernel, lines, length, block_rows),
        grid=(columns // width,),
        in_specs=[whole(array) for array in (*early, *late)]
        + [pl.BlockSpec((array.shape[0], width), lambda step: (0, step)) for array in exps]
        + [whole(array) for array in (*stats, first, *late_ids)]
        + [tile] * 4,
        out_specs=[tile] * 3,
        out_shape=[jax.ShapeDtypeStruct((rows, columns), jnp.bfloat16)] * 3,
        scratch_shapes=[pltpu.VMEM((2 * length * len(block_rows), 128), jnp.float32)],
        compiler_params=pltpu.CompilerParams(vmem_limit_bytes=36 * 1024 * 1024),
        cost_estimate=BRIEF,
        name="refresh_states",
    )(
        *early, *late, *in_hbm(exps[:3]), *exps[3:], *stats, first, *late_ids,
        *in_hbm(sums, [moment, curvature])
    )


def in_hbm(*lists):
    return [pltpu.with_memory_space_constraint(array, pltpu.HBM) for array in sum(map(list, lists), [])]


def after(value, *others):
    return lax.optimization_barrier((value, *others))[0]


def all_tokens(reps, shards, hidden, norm_gain, input_ids, sampled_ids, head_weight, moment, curvature):
    lines = shards // 2
    length = hidden.shape[0]
    rows, columns = moment.shape
    rep = lax.axis_index("rep")
    shard = lax.axis_index("shard")
    first_col = shard * columns
    group_len = length * shards

    def to_x(values):
        return lax.ppermute(values, "rep", swap_pairs(reps, 2))

    def to_core(values):
        return lax.ppermute(values, "rep", swap_pairs(reps, 1))

    def to_y(values):
        return lax.ppermute(values, "shard", swap_pairs(shards, 1))

    def to_y_core(values):
        pairs = [
            (rep_at * shards + at, (rep_at ^ 1) * shards + (at ^ 1))
            for rep_at in range(reps) for at in range(shards)
        ]
        return lax.ppermute(values, ("rep", "shard"), pairs)

    def to_z(values, along):
        return lax.ppermute(values, "shard", shift_pairs(lines, along, 0))

    split = lines // 2
    plain = [(0, 0), (0, 1), (1, 0)]
    groups = [[(*kind, turn) for kind in plain] for turn in range(split)]
    groups += [
        [(0, 0, split), (1, 1, 0)],
        [(0, 1, split), (1, 0, split), (0, 0, split + 1)],
        [(0, 1, split + 1), (1, 0, split + 1), (1, 1, 1)],
        [(1, 1, turn) for turn in range(split, lines)],
    ]
    early_blocks, late_blocks = sum(groups[:split], []), sum(groups[split:], [])

    def stat_row(block):
        return (2 * block[0] + block[1]) * lines + block[2]

    normed = normalized(hidden, norm_gain)

    last = jnp.arange(input_ids.shape[0]) % group_len == group_len - 1
    targets = jnp.where(last, -1, jnp.roll(input_ids, -1) - first_col)
    ids = jnp.stack([targets, sampled_ids - first_col]).reshape(2, reps * shards, length)
    side, across, turn = (np.array(values) for values in zip(*(early_blocks + late_blocks)))
    holder = (rep ^ (2 * across[None] + np.arange(2)[:, None])).reshape(-1)
    place = 2 * ((shard // 2 - turn) % lines) + ((shard % 2) ^ side)
    ids = jnp.take(ids, holder * shards + jnp.tile(place, 2), axis=1)
    ids = ids.reshape(2, 2, len(side), length)
    early_ids = ids[:, :, :len(early_blocks)].reshape(2, 1, -1)
    late_ids = ids[:, :, len(early_blocks):].reshape(2, 1, -1)
    early_ids, late_ids = [early_ids[0], early_ids[1]], [late_ids[0], late_ids[1]]
    rep_scalar = rep.astype(jnp.int32).reshape(1)
    stats = jnp.zeros((8 * lines, 128), jnp.float32)

    held = {(0, 0, 0): normed}
    early_exp = None

    def logits(group, stats, *gates, first_row=0, exp_rows=None, into=None):
        blocks = [held[block] for block in group]
        at = -1 if group is groups[0] else 0
        blocks[at] = after(blocks[at], *gates)
        rows = [stat_row(block) for block in group]
        exp_rows = exp_rows or len(group) * length
        return round_logits(blocks, rows, head_weight, stats, first_row, exp_rows, into)

    def diagonal(turn):
        if turn == 1:
            return to_z(held[1, 1, 0], 1)
        if turn % 2 == 0:
            return to_x(held[1, 0, turn])
        return to_y(held[0, 1, turn])

    for turn in range(lines):
        block = held[0, 0, turn]
        following = to_z(block, 1) if turn + 1 < lines else None
        held[0, 1, turn] = to_x(block)
        held[1, 0, turn] = to_y(block)
        if turn + 1 < lines:
            arrived = [following, held[0, 1, turn], held[1, 0, turn]]
            if turn == 0:
                arrived = [following, *early_ids, *late_ids, stats]
            elif turn < split:
                arrived += [early_exp]
            else:
                middle_exp, stats = logits(
                    groups[split], stats, exp_rows=5 * length
                )
                arrived = [following, held[0, 1, turn], early_exp, middle_exp]
            arrived = lax.optimization_barrier(tuple(arrived))
            held[0, 0, turn + 1] = arrived[0]
            if turn == 0:
                early_ids, late_ids = list(arrived[1:3]), list(arrived[3:5])
                stats, = arrived[5:]
                head_weight, *late_ids = prepared(head_weight, *late_ids, stats)
            elif turn < split:
                held[0, 1, turn], held[1, 0, turn], early_exp = arrived[1:]
            else:
                held[0, 1, turn], early_exp, middle_exp = arrived[1:]
            held[1, 1, turn] = diagonal(turn)
        if turn < split:
            size = len(groups[turn]) * length
            early_exp, stats = logits(
                groups[turn], stats, held[0, 0, turn + 1],
                first_row=turn * size, exp_rows=split * size, into=early_exp,
            )

    early = [held[block] for block in early_blocks]
    early[-1] = after(early[-1], held[0, 0, lines - 1])
    early = turned_features(rep_scalar, early, rows)
    early = [early[0], to_core(early[1])]
    middle_exp, stats = logits(
        groups[split + 1], stats, held[0, 0, lines - 1], early[0],
        first_row=2 * length, exp_rows=5 * length, into=middle_exp,
    )
    held[0, 1, lines - 1] = after(held[0, 1, lines - 1], middle_exp)
    held[1, 1, lines - 1] = diagonal(lines - 1)
    early_ids[0] = after(early_ids[0], middle_exp, held[0, 1, lines - 1])
    sums = one_hot_sums(early, early_ids, columns)
    last_exp, stats = logits(groups[split + 2], stats, *sums, exp_rows=5 * length)
    late = [held[block] for block in late_blocks]
    late[0] = after(late[0], last_exp)
    late = turned_features(rep_scalar, late, rows)
    late = [late[0], to_core(late[1])]
    ready = lax.optimization_barrier((early_exp, middle_exp, late[0]))
    other_exps = [to_core(exp) for exp in ready[:2]]
    last_exp, stats = logits(
        groups[-1], stats, late[0], first_row=3 * length, exp_rows=5 * length, into=last_exp
    )
    exps = [early_exp, middle_exp, last_exp]
    across_stats, core_stats, both_stats = to_y(stats), to_core(stats), to_y_core(stats)
    merged, first = merged_stats(
        after(stats, late[1], *other_exps), across_stats, core_stats, both_stats
    )
    all_stats = [merged] + [to_z(merged, -along) for along in range(1, lines)]
    other_exps.append(to_core(after(last_exp, merged)))
    return tuple(refresh_states(
        lines, length, [stat_row(block) for block in early_blocks + late_blocks], early, late,
        exps + other_exps, all_stats, first, late_ids, sums, moment, curvature,
    ))


def solution(mesh):
    in_specs = (
        P(("rep", "shard"), None),
        P(),
        P(),
        P(),
        P(None, "shard"),
        P("rep", "shard"),
        P("rep", "shard"),
    )
    out_specs = (P("rep", "shard"), P("rep", "shard"), P("rep", "shard"))
    reps, shards = mesh.shape["rep"], mesh.shape["shard"]

    def whole(hidden, *others):
        tokens, depth = hidden.shape
        length = tokens // (reps * shards)
        fits = hidden.size * 2 <= GATHER_BYTES and reps == 4 and shards == 8
        if fits and length == 64 and (depth // reps) % 128 == 0:
            plan = functools.partial(all_tokens, reps, shards)
        else:
            plan = by_groups

        return jax.shard_map(
            plan, mesh=mesh, in_specs=in_specs, out_specs=out_specs, check_vma=False
        )(hidden, *others)

    return whole
```

```python
import functools

import jax
import jax.numpy as jnp
import numpy as np
from jax import lax
from jax.experimental import pallas as pl
from jax.experimental.pallas import tpu as pltpu
from jax.sharding import PartitionSpec as P

EPS_NORM = 1e-05
BETA_ONE = 0.96
BETA_TWO = 0.95
RHO_SCALE = 0.05
GATHER_BYTES = 32 * 1024 * 1024
LOGITS_VMEM = 20 * 1024 * 1024
BRIEF = pl.CostEstimate(flops=1024, bytes_accessed=1024, transcendentals=0)


def normalize(hidden, norm_gain):
    values = hidden.astype(jnp.float32)
    row_scale = lax.rsqrt(jnp.mean(values * values, axis=-1, keepdims=True) + EPS_NORM)
    return (values * row_scale * norm_gain).astype(jnp.bfloat16)


def refresh(gradient, sample_grad, moment, curvature):
    moment_new = BETA_ONE * moment.astype(jnp.float32) + (1.0 - BETA_ONE) * gradient
    curvature_new = (
        BETA_TWO * curvature.astype(jnp.float32) + (1.0 - BETA_TWO) * sample_grad * sample_grad
    )
    update_direction = jnp.clip(moment_new / (RHO_SCALE * curvature_new), -1.0, 1.0)
    return (
        moment_new.astype(jnp.bfloat16),
        curvature_new.astype(jnp.bfloat16),
        update_direction.astype(jnp.bfloat16),
    )


def by_groups(hidden, norm_gain, input_ids, sampled_ids, head_weight, moment, curvature):
    normed = normalize(hidden, norm_gain)
    gathered = lax.all_gather(normed, "shard", axis=0, tiled=True)
    group_len = gathered.shape[0]
    columns = head_weight.shape[1]
    first_col = lax.axis_index("shard") * columns
    logits = jnp.dot(gathered, head_weight, preferred_element_type=jnp.float32)
    row_peak = lax.pmax(jnp.max(logits, axis=-1), "shard")
    scaled_exp = jnp.exp(logits - row_peak[:, None])
    row_sum = lax.psum(jnp.sum(scaled_exp, axis=-1), "shard")
    probabilities = (scaled_exp / row_sum[:, None]).astype(jnp.bfloat16)
    group_start = lax.axis_index("rep") * group_len
    token_ids = lax.dynamic_slice_in_dim(input_ids, group_start, group_len, 0)
    sample_ids = lax.dynamic_slice_in_dim(sampled_ids, group_start, group_len, 0)
    position = jnp.arange(group_len)
    shifted = jnp.roll(token_ids, -1) - first_col
    usable = (position < group_len - 1) & (shifted >= 0) & (shifted < columns)
    true_slot = jnp.where(usable, shifted, columns)
    sample_local = sample_ids - first_col
    inside = (sample_local >= 0) & (sample_local < columns)
    sample_slot = jnp.where(inside, sample_local, columns)
    shared = lax.dot_general(
        gathered, probabilities, (((0,), (0,)), ((), ())), preferred_element_type=jnp.float32
    )
    widened = gathered.astype(jnp.float32)
    true_sums = jax.ops.segment_sum(widened, true_slot, num_segments=columns + 1)[:columns]
    sample_sums = jax.ops.segment_sum(widened, sample_slot, num_segments=columns + 1)[:columns]
    true_part = (shared - true_sums.T).astype(jnp.bfloat16)
    sample_part = (shared - sample_sums.T).astype(jnp.bfloat16)
    gradient = lax.psum_scatter(true_part, "rep", scatter_dimension=0, tiled=True)
    sample_grad = lax.psum_scatter(sample_part, "rep", scatter_dimension=0, tiled=True)
    return refresh(
        gradient.astype(jnp.float32), sample_grad.astype(jnp.float32), moment, curvature
    )


def swap_pairs(count, bit):
    return [(index, index ^ bit) for index in range(count)]


def shift_pairs(lines, along, across):
    pairs = []
    for place in range(lines):
        for side in range(2):
            source = 2 * place + side
            pairs.append((source, 2 * ((place + along) % lines) + (side ^ across)))
    return pairs


def normalize_kernel(hidden_ref, gain_ref, normed_ref):
    normed_ref[...] = normalize(hidden_ref[...], gain_ref[...])


def normalized(hidden, norm_gain):
    return pl.pallas_call(
        normalize_kernel,
        out_shape=jax.ShapeDtypeStruct(hidden.shape, jnp.bfloat16),
        compiler_params=pltpu.CompilerParams(vmem_limit_bytes=8 * 1024 * 1024),
        cost_estimate=BRIEF,
        name="normalized",
    )(*in_hbm([hidden, norm_gain]))


def prepare_kernel(weight_ref, true_ids, sample_ids, *refs):
    held_ref, true_at, sample_at, arrived = refs[-4:]
    count = arrived.shape[0]
    band = weight_ref.shape[0] // count
    copies = [
        pltpu.make_async_copy(
            weight_ref.at[pl.ds(index * band, band)], held_ref.at[pl.ds(index * band, band)],
            arrived.at[index],
        )
        for index in range(count)
    ]
    for copy in copies:
        copy.start()
    lanes = lax.broadcasted_iota(jnp.int32, (128, 128), 1)
    for ids_ref, out_ref in ((true_ids, true_at), (sample_ids, sample_at)):
        for place in range(0, out_ref.shape[0], 128):
            ids = jnp.broadcast_to(ids_ref[:, place:place + 128], (128, 128)).T
            out_ref[place:place + 128] = ids - lanes
    for copy in copies:
        copy.wait()


def prepared(weight, true_ids, sample_ids, *earlier):
    near = pl.BlockSpec(memory_space=pltpu.VMEM)
    late = jax.ShapeDtypeStruct((true_ids.shape[1], 128), jnp.int32)
    return pl.pallas_call(
        prepare_kernel,
        in_specs=[pl.BlockSpec(memory_space=pltpu.HBM)] + [near] * (2 + len(earlier)),
        out_specs=[near] * 3,
        out_shape=[pltpu.VMEM(weight.shape, weight.dtype), late, late],
        scratch_shapes=[pltpu.SemaphoreType.DMA((4,))],
        compiler_params=pltpu.CompilerParams(vmem_limit_bytes=8 * 1024 * 1024),
        cost_estimate=BRIEF,
        name="prepared",
    )(pltpu.with_memory_space_constraint(weight, pltpu.HBM), true_ids, sample_ids, *earlier)


def logits_kernel(stat_rows, first_row, joins, *refs):
    count = len(stat_rows)
    block_refs, refs = refs[:count], refs[count:]
    if joins:
        refs = refs[:2] + refs[3:]
    weight_ref, before_ref, exp_ref, stats_ref, rows, logits, scaled_exp, highs, sums, sent = refs
    tokens, columns = logits.shape
    length = tokens // count
    half = stats_ref.shape[0] // 2
    for index, ref in enumerate(block_refs):
        rows[index * length:(index + 1) * length] = ref[...]
    highs[...] = jnp.full(highs.shape, -jnp.inf, jnp.float32)
    width = min(256, columns)

    def multiply(index, carry):
        place = pl.ds(pl.multiple_of(index * width, width), width)
        part = jnp.dot(rows[...], weight_ref[:, place], preferred_element_type=jnp.float32)
        logits[:, place] = part
        high = functools.reduce(
            jnp.maximum, [part[:, lane:lane + 128] for lane in range(0, width, 128)]
        )
        highs[...] = jnp.maximum(highs[...], high)
        return carry

    lax.fori_loop(0, columns // width, multiply, 0)
    highs[...] = jnp.broadcast_to(jnp.max(highs[...], axis=1, keepdims=True), highs.shape)
    chunk = 16
    copies = []
    for block in range(count):

        def scale(index, carry, block=block):
            place = pl.ds(pl.multiple_of(block * length + index * chunk, chunk), chunk)
            peak = highs[place, :]
            total = jnp.zeros((chunk, 128), jnp.float32)
            for lane in range(0, columns, 128):
                scaled = jnp.exp(logits[place, lane:lane + 128] - peak)
                scaled_exp[place, lane:lane + 128] = scaled.astype(jnp.bfloat16)
                total += scaled
            sums[place, :] = total
            return carry

        lax.fori_loop(0, length // chunk, scale, 0, unroll=2)
        place = pl.ds(block * length, length)
        target = pl.ds(first_row + block * length, length)
        copies.append(
            pltpu.make_async_copy(scaled_exp.at[place], exp_ref.at[target], sent.at[block])
        )
        copies[-1].start()
    totals = jnp.broadcast_to(jnp.sum(sums[...], axis=1, keepdims=True), sums.shape)
    stats_ref[...] = before_ref[...]
    for base, values in ((0, highs[...].T[0:1]), (half, totals.T[0:1])):
        for index, row in enumerate(stat_rows):
            stats_ref[base + row:base + row + 1, :length] = (
                values[:, index * length:(index + 1) * length]
            )
    for copy in copies:
        copy.wait()


def round_logits(blocks, stat_rows, held_weight, before, first_row, exp_rows, into):
    depth, columns = held_weight.shape
    length = blocks[0].shape[0]
    tokens = length * len(blocks)
    near = pl.BlockSpec(memory_space=pltpu.VMEM)
    held_weight = pltpu.with_memory_space_constraint(held_weight, pltpu.VMEM)
    far = pl.BlockSpec(memory_space=pltpu.HBM)
    joins = [] if into is None else [pltpu.with_memory_space_constraint(into, pltpu.HBM)]
    return pl.pallas_call(
        functools.partial(logits_kernel, stat_rows, first_row, len(joins)),
        in_specs=[near] * (len(blocks) + 2) + [far] * len(joins),
        input_output_aliases={len(blocks) + 2: 0} if joins else {},
        out_specs=[far, near],
        out_shape=[
            pltpu.HBM((exp_rows, columns), jnp.bfloat16),
            jax.ShapeDtypeStruct(before.shape, jnp.float32),
        ],
        scratch_shapes=[
            pltpu.VMEM((tokens, depth), jnp.bfloat16),
            pltpu.VMEM((tokens, columns), jnp.float32),
            pltpu.VMEM((tokens, columns), jnp.bfloat16),
            pltpu.VMEM((tokens, 128), jnp.float32),
            pltpu.VMEM((tokens, 128), jnp.float32),
            pltpu.SemaphoreType.DMA((len(blocks),)),
        ],
        compiler_params=pltpu.CompilerParams(vmem_limit_bytes=LOGITS_VMEM),
        cost_estimate=BRIEF,
        name="round_logits",
    )(*blocks, held_weight, before, *joins)


def turn_kernel(count, rep_ref, *refs):
    mine_ref, other_ref = refs[count:]
    step = pl.program_id(0)
    turned = jnp.concatenate([ref[...] for ref in refs[:count]], axis=0).T

    @pl.when(step == 0)
    def _():
        mine_ref[...] = turned

    @pl.when(step == 1)
    def _():
        other_ref[...] = turned


def turned_features(rep, blocks, rows):
    length = blocks[0].shape[0]
    tokens = length * len(blocks)
    whole = pl.BlockSpec((rows, tokens), lambda step, rep_ref: (0, 0))
    block = pl.BlockSpec((length, rows), lambda step, rep_ref: (0, rep_ref[0] ^ step))
    return pl.pallas_call(
        functools.partial(turn_kernel, len(blocks)),
        grid_spec=pltpu.PrefetchScalarGridSpec(
            num_scalar_prefetch=1,
            grid=(2,),
            in_specs=[block] * len(blocks),
            out_specs=[whole, whole],
        ),
        out_shape=[jax.ShapeDtypeStruct((rows, tokens), jnp.bfloat16)] * 2,
        compiler_params=pltpu.CompilerParams(vmem_limit_bytes=20 * 1024 * 1024),
        cost_estimate=BRIEF,
        name="turned_features",
    )(rep, *blocks)


def one_hot_kernel(count, *refs):
    feature_refs, refs = refs[:count], refs[count:]
    true_ref, sample_ref, true_out, sample_out = refs
    width = true_out.shape[1]
    features = jnp.concatenate([ref[...] for ref in feature_refs], axis=1)
    columns = pl.program_id(0) * width + lax.broadcasted_iota(
        jnp.int32, (width, features.shape[1]), 0
    )
    hot = jnp.concatenate([columns == true_ref[...], columns == sample_ref[...]], axis=0)
    totals = lax.dot_general(
        features, hot.astype(jnp.float32).astype(jnp.bfloat16),
        (((1,), (1,)), ((), ())), preferred_element_type=jnp.float32,
    )
    true_out[...] = totals[:, :width].astype(jnp.bfloat16)
    sample_out[...] = totals[:, width:].astype(jnp.bfloat16)


def one_hot_sums(features, ids, columns):
    rows = features[0].shape[0]
    width = min(256, columns)
    whole = lambda array: pl.BlockSpec(array.shape, lambda step: (0, 0))
    tile = pl.BlockSpec((rows, width), lambda step: (0, step))
    return pl.pallas_call(
        functools.partial(one_hot_kernel, len(features)),
        grid=(columns // width,),
        in_specs=[whole(array) for array in (*features, *ids)],
        out_specs=[tile, tile],
        out_shape=[pltpu.HBM((rows, columns), jnp.bfloat16)] * 2,
        compiler_params=pltpu.CompilerParams(vmem_limit_bytes=24 * 1024 * 1024),
        cost_estimate=BRIEF,
        name="one_hot_sums",
    )(*features, *ids)


def merge_kernel(own_ref, across_ref, core_ref, both_ref, merged_ref, first_ref):
    rows = own_ref.shape[0] // 2
    side = rows // 2
    for core, (near, far) in enumerate(((own_ref, across_ref), (core_ref, both_ref))):
        place = core * rows
        first, total = near[:rows], near[rows:]
        second = jnp.concatenate([far[side:rows], far[:side]], axis=0)
        other = jnp.concatenate([far[rows + side:], far[rows:rows + side]], axis=0)
        peak = jnp.maximum(first, second)
        merged_ref[place:place + rows] = peak
        merged_ref[2 * rows + place:3 * rows + place] = (
            total * jnp.exp(first - peak) + other * jnp.exp(second - peak)
        )
        first_ref[place:place + rows] = first


def merged_stats(own, across, core, both):
    rows, lanes = own.shape
    return pl.pallas_call(
        merge_kernel,
        out_shape=[
            jax.ShapeDtypeStruct((2 * rows, lanes), jnp.float32),
            jax.ShapeDtypeStruct((rows, lanes), jnp.float32),
        ],
        compiler_params=pltpu.CompilerParams(vmem_limit_bytes=4 * 1024 * 1024),
        cost_estimate=BRIEF,
        name="merged_stats",
    )(own, across, core, both)


def refresh_kernel(lines, length, block_rows, *refs):
    early_refs, late_refs, refs = refs[:2], refs[2:4], refs[4:]
    exp_refs, refs = refs[:6], refs[6:]
    stats_refs, refs = refs[:lines], refs[lines:]
    (first_ref, true_at, sample_at, true_sum, sample_sum, moment_ref, curvature_ref,
     moment_out, curvature_out, update_out, factors) = refs
    step = pl.program_id(0)
    width = moment_out.shape[1]
    early = early_refs[0].shape[1]
    late = late_refs[0].shape[1]

    @pl.when(step == 0)
    def _():
        rows = first_ref.shape[0]

        def turned(values, along):
            return jnp.concatenate([
                values[group + (turn + along) % lines:group + (turn + along) % lines + 1]
                for group in range(0, rows, lines) for turn in range(lines)
            ], axis=0) if along else values

        peaks = [turned(ref[:rows], along) for along, ref in enumerate(stats_refs)]
        totals = [turned(ref[rows:], along) for along, ref in enumerate(stats_refs)]
        peak = functools.reduce(jnp.maximum, peaks)
        total = sum(t * jnp.exp(p - peak) for p, t in zip(peaks, totals))
        factor = jnp.exp(first_ref[...] - peak) / total
        per_core = rows // 2
        full = jnp.concatenate([factor, jnp.zeros((128 - rows, 128), jnp.float32)], axis=0).T
        for core in range(2):
            for index, row in enumerate(block_rows):
                place = (core * len(block_rows) + index) * length
                at = core * per_core + row
                factors[place:place + length] = jnp.broadcast_to(
                    full[:length, at:at + 1], (length, 128)
                )

    def probs(ref, place, lane):
        scale = factors[place:place + ref.shape[0]]
        return ref[:, lane:lane + 128].astype(jnp.float32) * scale

    early_sides, true_sides, sample_sides = [], [], []
    for core in range(2):
        first_exp, *late_exps = exp_refs[3 * core:3 * core + 3]
        place = core * (early + late)
        early_sides.append(jnp.concatenate([
            probs(first_exp, place, lane).astype(jnp.bfloat16) for lane in range(0, width, 128)
        ], axis=1))
        place += early
        at = core * late
        for ref in late_exps:
            rows = slice(at, at + ref.shape[0])
            true_parts, sample_parts = [], []
            for lane in range(0, width, 128):
                prob = probs(ref, place, lane)
                column = step * width + lane
                true_hot = jnp.where(true_at[rows] == column, 1.0, 0.0)
                sample_hot = jnp.where(sample_at[rows] == column, 1.0, 0.0)
                true_parts.append((prob - true_hot).astype(jnp.bfloat16))
                sample_parts.append((prob - sample_hot).astype(jnp.bfloat16))
            true_sides.append(jnp.concatenate(true_parts, axis=1))
            sample_sides.append(jnp.concatenate(sample_parts, axis=1))
            place += ref.shape[0]
            at += ref.shape[0]
    early_features = jnp.concatenate([ref[...] for ref in early_refs], axis=1)
    late_features = jnp.concatenate([ref[...] for ref in late_refs], axis=1)

    def product(features, sides):
        return jnp.dot(
            features, jnp.concatenate(sides, axis=0), preferred_element_type=jnp.float32
        )

    shared = product(early_features, early_sides)
    gradient = product(late_features, true_sides) + (shared - true_sum[...].astype(jnp.float32))
    sample_grad = product(late_features, sample_sides) + (
        shared - sample_sum[...].astype(jnp.float32)
    )
    moment_out[...], curvature_out[...], update_out[...] = refresh(
        gradient, sample_grad, moment_ref[...], curvature_ref[...]
    )


def refresh_states(lines, length, block_rows, early, late, exps, stats, first,
                   late_ids, sums, moment, curvature):
    rows, columns = moment.shape
    width = min(256, columns)
    whole = lambda array: pl.BlockSpec(array.shape, lambda step: (0, 0))
    tile = pl.BlockSpec((rows, width), lambda step: (0, step))
    return pl.pallas_call(
        functools.partial(refresh_kernel, lines, length, block_rows),
        grid=(columns // width,),
        in_specs=[whole(array) for array in (*early, *late)]
        + [pl.BlockSpec((array.shape[0], width), lambda step: (0, step)) for array in exps]
        + [whole(array) for array in (*stats, first, *late_ids)]
        + [tile] * 4,
        out_specs=[tile] * 3,
        out_shape=[jax.ShapeDtypeStruct((rows, columns), jnp.bfloat16)] * 3,
        scratch_shapes=[pltpu.VMEM((2 * length * len(block_rows), 128), jnp.float32)],
        compiler_params=pltpu.CompilerParams(vmem_limit_bytes=36 * 1024 * 1024),
        cost_estimate=BRIEF,
        name="refresh_states",
    )(
        *early, *late, *in_hbm(exps[:3]), *exps[3:], *stats, first, *late_ids,
        *in_hbm(sums, [moment, curvature])
    )


def in_hbm(*lists):
    return [pltpu.with_memory_space_constraint(array, pltpu.HBM) for array in sum(map(list, lists), [])]


def after(value, *others):
    return lax.optimization_barrier((value, *others))[0]


def all_tokens(reps, shards, hidden, norm_gain, input_ids, sampled_ids, head_weight, moment, curvature):
    lines = shards // 2
    length = hidden.shape[0]
    rows, columns = moment.shape
    rep = lax.axis_index("rep")
    shard = lax.axis_index("shard")
    first_col = shard * columns
    group_len = length * shards

    def to_x(values):
        return lax.ppermute(values, "rep", swap_pairs(reps, 2))

    def to_core(values):
        return lax.ppermute(values, "rep", swap_pairs(reps, 1))

    def to_y(values):
        return lax.ppermute(values, "shard", swap_pairs(shards, 1))

    def to_y_core(values):
        pairs = [
            (rep_at * shards + at, (rep_at ^ 1) * shards + (at ^ 1))
            for rep_at in range(reps) for at in range(shards)
        ]
        return lax.ppermute(values, ("rep", "shard"), pairs)

    def to_z(values, along):
        return lax.ppermute(values, "shard", shift_pairs(lines, along, 0))

    split = lines // 2
    plain = [(0, 0), (0, 1), (1, 0)]
    groups = [[(*kind, turn) for kind in plain] for turn in range(split)]
    groups += [
        [(0, 0, split), (1, 1, 0)],
        [(0, 1, split), (1, 0, split), (0, 0, split + 1)],
        [(0, 1, split + 1), (1, 0, split + 1), (1, 1, 1)],
        [(1, 1, turn) for turn in range(split, lines)],
    ]
    early_blocks, late_blocks = sum(groups[:split], []), sum(groups[split:], [])

    def stat_row(block):
        return (2 * block[0] + block[1]) * lines + block[2]

    normed = normalized(hidden, norm_gain)

    last = jnp.arange(input_ids.shape[0]) % group_len == group_len - 1
    targets = jnp.where(last, -1, jnp.roll(input_ids, -1) - first_col)
    ids = jnp.stack([targets, sampled_ids - first_col]).reshape(2, reps * shards, length)
    side, across, turn = (np.array(values) for values in zip(*(early_blocks + late_blocks)))
    holder = (rep ^ (2 * across[None] + np.arange(2)[:, None])).reshape(-1)
    place = 2 * ((shard // 2 - turn) % lines) + ((shard % 2) ^ side)
    ids = jnp.take(ids, holder * shards + jnp.tile(place, 2), axis=1)
    ids = ids.reshape(2, 2, len(side), length)
    early_ids = ids[:, :, :len(early_blocks)].reshape(2, 1, -1)
    late_ids = ids[:, :, len(early_blocks):].reshape(2, 1, -1)
    early_ids, late_ids = [early_ids[0], early_ids[1]], [late_ids[0], late_ids[1]]
    rep_scalar = rep.astype(jnp.int32).reshape(1)
    stats = jnp.zeros((8 * lines, 128), jnp.float32)

    held = {(0, 0, 0): normed}
    early_exp = None

    def logits(group, stats, *gates, first_row=0, exp_rows=None, into=None):
        blocks = [held[block] for block in group]
        at = -1 if group is groups[0] else 0
        blocks[at] = after(blocks[at], *gates)
        rows = [stat_row(block) for block in group]
        exp_rows = exp_rows or len(group) * length
        return round_logits(blocks, rows, head_weight, stats, first_row, exp_rows, into)

    def diagonal(turn):
        if turn == 1:
            return to_z(held[1, 1, 0], 1)
        if turn == 2:
            return to_x(held[1, 0, turn])
        return to_y(held[0, 1, turn])

    for turn in range(lines):
        block = held[0, 0, turn]
        following = to_z(block, 1) if turn + 1 < lines else None
        held[0, 1, turn] = to_x(block)
        held[1, 0, turn] = to_y(block)
        if turn + 1 < lines:
            arrived = [following, held[0, 1, turn], held[1, 0, turn]]
            if turn == 0:
                arrived = [following, *early_ids, *late_ids, stats]
            elif turn < split:
                arrived += [early_exp]
            else:
                middle_exp, stats = logits(
                    groups[split], stats, exp_rows=5 * length
                )
                arrived = [following, held[0, 1, turn], early_exp, middle_exp]
            arrived = lax.optimization_barrier(tuple(arrived))
            held[0, 0, turn + 1] = arrived[0]
            if turn == 0:
                early_ids, late_ids = list(arrived[1:3]), list(arrived[3:5])
                stats, = arrived[5:]
                head_weight, *late_ids = prepared(head_weight, *late_ids, stats)
            elif turn < split:
                held[0, 1, turn], held[1, 0, turn], early_exp = arrived[1:]
            else:
                held[0, 1, turn], early_exp, middle_exp = arrived[1:]
            held[1, 1, turn] = diagonal(turn)
        if turn < split:
            size = len(groups[turn]) * length
            early_exp, stats = logits(
                groups[turn], stats, held[0, 0, turn + 1],
                first_row=turn * size, exp_rows=split * size, into=early_exp,
            )

    early = [held[block] for block in early_blocks]
    early[-1] = after(early[-1], held[0, 0, lines - 1])
    early = turned_features(rep_scalar, early, rows)
    early = [early[0], to_core(early[1])]
    middle_exp, stats = logits(
        groups[split + 1], stats, held[0, 0, lines - 1], early[0],
        first_row=2 * length, exp_rows=5 * length, into=middle_exp,
    )
    held[0, 1, lines - 1] = after(held[0, 1, lines - 1], middle_exp)
    held[1, 1, lines - 1] = diagonal(lines - 1)
    early_ids[0] = after(early_ids[0], middle_exp, held[0, 1, lines - 1])
    sums = one_hot_sums(early, early_ids, columns)
    last_exp, stats = logits(groups[split + 2], stats, *sums, exp_rows=5 * length)
    late = [held[block] for block in late_blocks]
    late[0] = after(late[0], last_exp)
    late = turned_features(rep_scalar, late, rows)
    late = [late[0], to_core(late[1])]
    ready = lax.optimization_barrier((early_exp, middle_exp, late[0]))
    other_exps = [to_core(exp) for exp in ready[:2]]
    last_exp, stats = logits(
        groups[-1], stats, late[0], first_row=3 * length, exp_rows=5 * length, into=last_exp
    )
    exps = [early_exp, middle_exp, last_exp]
    across_stats, core_stats, both_stats = to_y(stats), to_core(stats), to_y_core(stats)
    merged, first = merged_stats(
        after(stats, late[1], *other_exps), across_stats, core_stats, both_stats
    )
    all_stats = [merged] + [to_z(merged, -along) for along in range(1, lines)]
    other_exps.append(to_core(after(last_exp, merged)))
    return tuple(refresh_states(
        lines, length, [stat_row(block) for block in early_blocks + late_blocks], early, late,
        exps + other_exps, all_stats, first, late_ids, sums, moment, curvature,
    ))


def solution(mesh):
    in_specs = (
        P(("rep", "shard"), None),
        P(),
        P(),
        P(),
        P(None, "shard"),
        P("rep", "shard"),
        P("rep", "shard"),
    )
    out_specs = (P("rep", "shard"), P("rep", "shard"), P("rep", "shard"))
    reps, shards = mesh.shape["rep"], mesh.shape["shard"]

    def whole(hidden, *others):
        tokens, depth = hidden.shape
        length = tokens // (reps * shards)
        fits = hidden.size * 2 <= GATHER_BYTES and reps == 4 and shards == 8
        if fits and length == 64 and (depth // reps) % 128 == 0:
            plan = functools.partial(all_tokens, reps, shards)
        else:
            plan = by_groups

        return jax.shard_map(
            plan, mesh=mesh, in_specs=in_specs, out_specs=out_specs, check_vma=False
        )(hidden, *others)

    return whole
```

```python
import functools

import jax
import jax.numpy as jnp
import numpy as np
from jax import lax
from jax.experimental import pallas as pl
from jax.experimental.pallas import tpu as pltpu
from jax.sharding import PartitionSpec as P

EPS_NORM = 1e-05
BETA_ONE = 0.96
BETA_TWO = 0.95
RHO_SCALE = 0.05
GATHER_BYTES = 32 * 1024 * 1024
LOGITS_VMEM = 20 * 1024 * 1024
BRIEF = pl.CostEstimate(flops=1024, bytes_accessed=1024, transcendentals=0)


def normalize(hidden, norm_gain):
    values = hidden.astype(jnp.float32)
    row_scale = lax.rsqrt(jnp.mean(values * values, axis=-1, keepdims=True) + EPS_NORM)
    return (values * row_scale * norm_gain).astype(jnp.bfloat16)


def refresh(gradient, sample_grad, moment, curvature):
    moment_new = BETA_ONE * moment.astype(jnp.float32) + (1.0 - BETA_ONE) * gradient
    curvature_new = (
        BETA_TWO * curvature.astype(jnp.float32) + (1.0 - BETA_TWO) * sample_grad * sample_grad
    )
    update_direction = jnp.clip(moment_new / (RHO_SCALE * curvature_new), -1.0, 1.0)
    return (
        moment_new.astype(jnp.bfloat16),
        curvature_new.astype(jnp.bfloat16),
        update_direction.astype(jnp.bfloat16),
    )


def by_groups(hidden, norm_gain, input_ids, sampled_ids, head_weight, moment, curvature):
    normed = normalize(hidden, norm_gain)
    gathered = lax.all_gather(normed, "shard", axis=0, tiled=True)
    group_len = gathered.shape[0]
    columns = head_weight.shape[1]
    first_col = lax.axis_index("shard") * columns
    logits = jnp.dot(gathered, head_weight, preferred_element_type=jnp.float32)
    row_peak = lax.pmax(jnp.max(logits, axis=-1), "shard")
    scaled_exp = jnp.exp(logits - row_peak[:, None])
    row_sum = lax.psum(jnp.sum(scaled_exp, axis=-1), "shard")
    probabilities = (scaled_exp / row_sum[:, None]).astype(jnp.bfloat16)
    group_start = lax.axis_index("rep") * group_len
    token_ids = lax.dynamic_slice_in_dim(input_ids, group_start, group_len, 0)
    sample_ids = lax.dynamic_slice_in_dim(sampled_ids, group_start, group_len, 0)
    position = jnp.arange(group_len)
    shifted = jnp.roll(token_ids, -1) - first_col
    usable = (position < group_len - 1) & (shifted >= 0) & (shifted < columns)
    true_slot = jnp.where(usable, shifted, columns)
    sample_local = sample_ids - first_col
    inside = (sample_local >= 0) & (sample_local < columns)
    sample_slot = jnp.where(inside, sample_local, columns)
    shared = lax.dot_general(
        gathered, probabilities, (((0,), (0,)), ((), ())), preferred_element_type=jnp.float32
    )
    widened = gathered.astype(jnp.float32)
    true_sums = jax.ops.segment_sum(widened, true_slot, num_segments=columns + 1)[:columns]
    sample_sums = jax.ops.segment_sum(widened, sample_slot, num_segments=columns + 1)[:columns]
    true_part = (shared - true_sums.T).astype(jnp.bfloat16)
    sample_part = (shared - sample_sums.T).astype(jnp.bfloat16)
    gradient = lax.psum_scatter(true_part, "rep", scatter_dimension=0, tiled=True)
    sample_grad = lax.psum_scatter(sample_part, "rep", scatter_dimension=0, tiled=True)
    return refresh(
        gradient.astype(jnp.float32), sample_grad.astype(jnp.float32), moment, curvature
    )


def swap_pairs(count, bit):
    return [(index, index ^ bit) for index in range(count)]


def shift_pairs(lines, along, across):
    pairs = []
    for place in range(lines):
        for side in range(2):
            source = 2 * place + side
            pairs.append((source, 2 * ((place + along) % lines) + (side ^ across)))
    return pairs


def normalize_kernel(hidden_ref, gain_ref, normed_ref):
    normed_ref[...] = normalize(hidden_ref[...], gain_ref[...])


def normalized(hidden, norm_gain):
    return pl.pallas_call(
        normalize_kernel,
        out_shape=jax.ShapeDtypeStruct(hidden.shape, jnp.bfloat16),
        compiler_params=pltpu.CompilerParams(vmem_limit_bytes=8 * 1024 * 1024),
        cost_estimate=BRIEF,
        name="normalized",
    )(*in_hbm([hidden, norm_gain]))


def prepare_kernel(weight_ref, true_ids, sample_ids, *refs):
    held_ref, true_at, sample_at, arrived = refs[-4:]
    count = arrived.shape[0]
    band = weight_ref.shape[0] // count
    copies = [
        pltpu.make_async_copy(
            weight_ref.at[pl.ds(index * band, band)], held_ref.at[pl.ds(index * band, band)],
            arrived.at[index],
        )
        for index in range(count)
    ]
    for copy in copies:
        copy.start()
    lanes = lax.broadcasted_iota(jnp.int32, (128, 128), 1)
    for ids_ref, out_ref in ((true_ids, true_at), (sample_ids, sample_at)):
        for place in range(0, out_ref.shape[0], 128):
            ids = jnp.broadcast_to(ids_ref[:, place:place + 128], (128, 128)).T
            out_ref[place:place + 128] = ids - lanes
    for copy in copies:
        copy.wait()


def prepared(weight, true_ids, sample_ids, *earlier):
    near = pl.BlockSpec(memory_space=pltpu.VMEM)
    late = jax.ShapeDtypeStruct((true_ids.shape[1], 128), jnp.int32)
    return pl.pallas_call(
        prepare_kernel,
        in_specs=[pl.BlockSpec(memory_space=pltpu.HBM)] + [near] * (2 + len(earlier)),
        out_specs=[near] * 3,
        out_shape=[pltpu.VMEM(weight.shape, weight.dtype), late, late],
        scratch_shapes=[pltpu.SemaphoreType.DMA((4,))],
        compiler_params=pltpu.CompilerParams(vmem_limit_bytes=8 * 1024 * 1024),
        cost_estimate=BRIEF,
        name="prepared",
    )(pltpu.with_memory_space_constraint(weight, pltpu.HBM), true_ids, sample_ids, *earlier)


def logits_kernel(stat_rows, first_row, joins, *refs):
    count = len(stat_rows)
    block_refs, refs = refs[:count], refs[count:]
    if joins:
        refs = refs[:2] + refs[3:]
    weight_ref, before_ref, exp_ref, stats_ref, rows, logits, scaled_exp, highs, sums, sent = refs
    tokens, columns = logits.shape
    length = tokens // count
    half = stats_ref.shape[0] // 2
    for index, ref in enumerate(block_refs):
        rows[index * length:(index + 1) * length] = ref[...]
    highs[...] = jnp.full(highs.shape, -jnp.inf, jnp.float32)
    width = min(256, columns)

    def multiply(index, carry):
        place = pl.ds(pl.multiple_of(index * width, width), width)
        part = jnp.dot(rows[...], weight_ref[:, place], preferred_element_type=jnp.float32)
        logits[:, place] = part
        high = functools.reduce(
            jnp.maximum, [part[:, lane:lane + 128] for lane in range(0, width, 128)]
        )
        highs[...] = jnp.maximum(highs[...], high)
        return carry

    lax.fori_loop(0, columns // width, multiply, 0)
    highs[...] = jnp.broadcast_to(jnp.max(highs[...], axis=1, keepdims=True), highs.shape)
    chunk = 16
    copies = []
    for block in range(count):

        def scale(index, carry, block=block):
            place = pl.ds(pl.multiple_of(block * length + index * chunk, chunk), chunk)
            peak = highs[place, :]
            total = jnp.zeros((chunk, 128), jnp.float32)
            for lane in range(0, columns, 128):
                scaled = jnp.exp(logits[place, lane:lane + 128] - peak)
                scaled_exp[place, lane:lane + 128] = scaled.astype(jnp.bfloat16)
                total += scaled
            sums[place, :] = total
            return carry

        lax.fori_loop(0, length // chunk, scale, 0, unroll=2)
        place = pl.ds(block * length, length)
        target = pl.ds(first_row + block * length, length)
        copies.append(
            pltpu.make_async_copy(scaled_exp.at[place], exp_ref.at[target], sent.at[block])
        )
        copies[-1].start()
    totals = jnp.broadcast_to(jnp.sum(sums[...], axis=1, keepdims=True), sums.shape)
    stats_ref[...] = before_ref[...]
    for base, values in ((0, highs[...].T[0:1]), (half, totals.T[0:1])):
        for index, row in enumerate(stat_rows):
            stats_ref[base + row:base + row + 1, :length] = (
                values[:, index * length:(index + 1) * length]
            )
    for copy in copies:
        copy.wait()


def round_logits(blocks, stat_rows, held_weight, before, first_row, exp_rows, into):
    depth, columns = held_weight.shape
    length = blocks[0].shape[0]
    tokens = length * len(blocks)
    near = pl.BlockSpec(memory_space=pltpu.VMEM)
    held_weight = pltpu.with_memory_space_constraint(held_weight, pltpu.VMEM)
    far = pl.BlockSpec(memory_space=pltpu.HBM)
    joins = [] if into is None else [pltpu.with_memory_space_constraint(into, pltpu.HBM)]
    return pl.pallas_call(
        functools.partial(logits_kernel, stat_rows, first_row, len(joins)),
        in_specs=[near] * (len(blocks) + 2) + [far] * len(joins),
        input_output_aliases={len(blocks) + 2: 0} if joins else {},
        out_specs=[far, near],
        out_shape=[
            pltpu.HBM((exp_rows, columns), jnp.bfloat16),
            jax.ShapeDtypeStruct(before.shape, jnp.float32),
        ],
        scratch_shapes=[
            pltpu.VMEM((tokens, depth), jnp.bfloat16),
            pltpu.VMEM((tokens, columns), jnp.float32),
            pltpu.VMEM((tokens, columns), jnp.bfloat16),
            pltpu.VMEM((tokens, 128), jnp.float32),
            pltpu.VMEM((tokens, 128), jnp.float32),
            pltpu.SemaphoreType.DMA((len(blocks),)),
        ],
        compiler_params=pltpu.CompilerParams(vmem_limit_bytes=LOGITS_VMEM),
        cost_estimate=BRIEF,
        name="round_logits",
    )(*blocks, held_weight, before, *joins)


def turn_kernel(count, rep_ref, *refs):
    mine_ref, other_ref = refs[count:]
    step = pl.program_id(0)
    turned = jnp.concatenate([ref[...] for ref in refs[:count]], axis=0).T

    @pl.when(step == 0)
    def _():
        mine_ref[...] = turned

    @pl.when(step == 1)
    def _():
        other_ref[...] = turned


def turned_features(rep, blocks, rows):
    length = blocks[0].shape[0]
    tokens = length * len(blocks)
    whole = pl.BlockSpec((rows, tokens), lambda step, rep_ref: (0, 0))
    block = pl.BlockSpec((length, rows), lambda step, rep_ref: (0, rep_ref[0] ^ step))
    return pl.pallas_call(
        functools.partial(turn_kernel, len(blocks)),
        grid_spec=pltpu.PrefetchScalarGridSpec(
            num_scalar_prefetch=1,
            grid=(2,),
            in_specs=[block] * len(blocks),
            out_specs=[whole, whole],
        ),
        out_shape=[jax.ShapeDtypeStruct((rows, tokens), jnp.bfloat16)] * 2,
        compiler_params=pltpu.CompilerParams(vmem_limit_bytes=20 * 1024 * 1024),
        cost_estimate=BRIEF,
        name="turned_features",
    )(rep, *blocks)


def one_hot_kernel(count, *refs):
    feature_refs, refs = refs[:count], refs[count:]
    true_ref, sample_ref, true_out, sample_out = refs
    width = true_out.shape[1]
    features = jnp.concatenate([ref[...] for ref in feature_refs], axis=1)
    columns = pl.program_id(0) * width + lax.broadcasted_iota(
        jnp.int32, (width, features.shape[1]), 0
    )
    hot = jnp.concatenate([columns == true_ref[...], columns == sample_ref[...]], axis=0)
    totals = lax.dot_general(
        features, hot.astype(jnp.float32).astype(jnp.bfloat16),
        (((1,), (1,)), ((), ())), preferred_element_type=jnp.float32,
    )
    true_out[...] = totals[:, :width].astype(jnp.bfloat16)
    sample_out[...] = totals[:, width:].astype(jnp.bfloat16)


def one_hot_sums(features, ids, columns):
    rows = features[0].shape[0]
    width = min(256, columns)
    whole = lambda array: pl.BlockSpec(array.shape, lambda step: (0, 0))
    tile = pl.BlockSpec((rows, width), lambda step: (0, step))
    return pl.pallas_call(
        functools.partial(one_hot_kernel, len(features)),
        grid=(columns // width,),
        in_specs=[whole(array) for array in (*features, *ids)],
        out_specs=[tile, tile],
        out_shape=[pltpu.HBM((rows, columns), jnp.bfloat16)] * 2,
        compiler_params=pltpu.CompilerParams(vmem_limit_bytes=24 * 1024 * 1024),
        cost_estimate=BRIEF,
        name="one_hot_sums",
    )(*features, *ids)


def merge_kernel(own_ref, across_ref, core_ref, both_ref, merged_ref, first_ref):
    rows = own_ref.shape[0] // 2
    side = rows // 2
    for core, (near, far) in enumerate(((own_ref, across_ref), (core_ref, both_ref))):
        place = core * rows
        first, total = near[:rows], near[rows:]
        second = jnp.concatenate([far[side:rows], far[:side]], axis=0)
        other = jnp.concatenate([far[rows + side:], far[rows:rows + side]], axis=0)
        peak = jnp.maximum(first, second)
        merged_ref[place:place + rows] = peak
        merged_ref[2 * rows + place:3 * rows + place] = (
            total * jnp.exp(first - peak) + other * jnp.exp(second - peak)
        )
        first_ref[place:place + rows] = first


def merged_stats(own, across, core, both):
    rows, lanes = own.shape
    return pl.pallas_call(
        merge_kernel,
        out_shape=[
            jax.ShapeDtypeStruct((2 * rows, lanes), jnp.float32),
            jax.ShapeDtypeStruct((rows, lanes), jnp.float32),
        ],
        compiler_params=pltpu.CompilerParams(vmem_limit_bytes=4 * 1024 * 1024),
        cost_estimate=BRIEF,
        name="merged_stats",
    )(own, across, core, both)


def refresh_kernel(lines, length, block_rows, *refs):
    early_refs, late_refs, refs = refs[:2], refs[2:4], refs[4:]
    exp_refs, refs = refs[:6], refs[6:]
    stats_refs, refs = refs[:lines], refs[lines:]
    (first_ref, true_at, sample_at, true_sum, sample_sum, moment_ref, curvature_ref,
     moment_out, curvature_out, update_out, factors) = refs
    step = pl.program_id(0)
    width = moment_out.shape[1]
    early = early_refs[0].shape[1]
    late = late_refs[0].shape[1]

    @pl.when(step == 0)
    def _():
        rows = first_ref.shape[0]

        def turned(values, along):
            return jnp.concatenate([
                values[group + (turn + along) % lines:group + (turn + along) % lines + 1]
                for group in range(0, rows, lines) for turn in range(lines)
            ], axis=0) if along else values

        peaks = [turned(ref[:rows], along) for along, ref in enumerate(stats_refs)]
        totals = [turned(ref[rows:], along) for along, ref in enumerate(stats_refs)]
        peak = functools.reduce(jnp.maximum, peaks)
        total = sum(t * jnp.exp(p - peak) for p, t in zip(peaks, totals))
        factor = jnp.exp(first_ref[...] - peak) / total
        per_core = rows // 2
        full = jnp.concatenate([factor, jnp.zeros((128 - rows, 128), jnp.float32)], axis=0).T
        for core in range(2):
            for index, row in enumerate(block_rows):
                place = (core * len(block_rows) + index) * length
                at = core * per_core + row
                factors[place:place + length] = jnp.broadcast_to(
                    full[:length, at:at + 1], (length, 128)
                )

    def probs(ref, place, lane):
        scale = factors[place:place + ref.shape[0]]
        return ref[:, lane:lane + 128].astype(jnp.float32) * scale

    early_sides, true_sides, sample_sides = [], [], []
    for core in range(2):
        first_exp, *late_exps = exp_refs[3 * core:3 * core + 3]
        place = core * (early + late)
        early_sides.append(jnp.concatenate([
            probs(first_exp, place, lane).astype(jnp.bfloat16) for lane in range(0, width, 128)
        ], axis=1))
        place += early
        at = core * late
        for ref in late_exps:
            rows = slice(at, at + ref.shape[0])
            true_parts, sample_parts = [], []
            for lane in range(0, width, 128):
                prob = probs(ref, place, lane)
                column = step * width + lane
                true_hot = jnp.where(true_at[rows] == column, 1.0, 0.0)
                sample_hot = jnp.where(sample_at[rows] == column, 1.0, 0.0)
                true_parts.append((prob - true_hot).astype(jnp.bfloat16))
                sample_parts.append((prob - sample_hot).astype(jnp.bfloat16))
            true_sides.append(jnp.concatenate(true_parts, axis=1))
            sample_sides.append(jnp.concatenate(sample_parts, axis=1))
            place += ref.shape[0]
            at += ref.shape[0]
    early_features = jnp.concatenate([ref[...] for ref in early_refs], axis=1)
    late_features = jnp.concatenate([ref[...] for ref in late_refs], axis=1)

    def product(features, sides):
        return jnp.dot(
            features, jnp.concatenate(sides, axis=0), preferred_element_type=jnp.float32
        )

    shared = product(early_features, early_sides)
    gradient = product(late_features, true_sides) + (shared - true_sum[...].astype(jnp.float32))
    sample_grad = product(late_features, sample_sides) + (
        shared - sample_sum[...].astype(jnp.float32)
    )
    moment_out[...], curvature_out[...], update_out[...] = refresh(
        gradient, sample_grad, moment_ref[...], curvature_ref[...]
    )


def refresh_states(lines, length, block_rows, early, late, exps, stats, first,
                   late_ids, sums, moment, curvature):
    rows, columns = moment.shape
    width = min(256, columns)
    whole = lambda array: pl.BlockSpec(array.shape, lambda step: (0, 0))
    tile = pl.BlockSpec((rows, width), lambda step: (0, step))
    return pl.pallas_call(
        functools.partial(refresh_kernel, lines, length, block_rows),
        grid=(columns // width,),
        in_specs=[whole(array) for array in (*early, *late)]
        + [pl.BlockSpec((array.shape[0], width), lambda step: (0, step)) for array in exps]
        + [whole(array) for array in (*stats, first, *late_ids)]
        + [tile] * 4,
        out_specs=[tile] * 3,
        out_shape=[jax.ShapeDtypeStruct((rows, columns), jnp.bfloat16)] * 3,
        scratch_shapes=[pltpu.VMEM((2 * length * len(block_rows), 128), jnp.float32)],
        compiler_params=pltpu.CompilerParams(vmem_limit_bytes=36 * 1024 * 1024),
        cost_estimate=BRIEF,
        name="refresh_states",
    )(
        *early, *late, *in_hbm(exps[:3]), *exps[3:], *stats, first, *late_ids,
        *in_hbm(sums, [moment, curvature])
    )


def in_hbm(*lists):
    return [pltpu.with_memory_space_constraint(array, pltpu.HBM) for array in sum(map(list, lists), [])]


def after(value, *others):
    return lax.optimization_barrier((value, *others))[0]


def all_tokens(reps, shards, hidden, norm_gain, input_ids, sampled_ids, head_weight, moment, curvature):
    lines = shards // 2
    length = hidden.shape[0]
    rows, columns = moment.shape
    rep = lax.axis_index("rep")
    shard = lax.axis_index("shard")
    first_col = shard * columns
    group_len = length * shards

    def to_x(values):
        return lax.ppermute(values, "rep", swap_pairs(reps, 2))

    def to_core(values):
        return lax.ppermute(values, "rep", swap_pairs(reps, 1))

    def to_y(values):
        return lax.ppermute(values, "shard", swap_pairs(shards, 1))

    def to_y_core(values):
        pairs = [
            (rep_at * shards + at, (rep_at ^ 1) * shards + (at ^ 1))
            for rep_at in range(reps) for at in range(shards)
        ]
        return lax.ppermute(values, ("rep", "shard"), pairs)

    def to_z(values, along):
        return lax.ppermute(values, "shard", shift_pairs(lines, along, 0))

    split = lines // 2
    plain = [(0, 0), (0, 1), (1, 0)]
    groups = [[(*kind, turn) for kind in plain] for turn in range(split)]
    groups += [
        [(0, 0, split), (1, 1, 0)],
        [(0, 1, split), (1, 0, split), (0, 0, split + 1)],
        [(0, 1, split + 1), (1, 0, split + 1), (1, 1, 1)],
        [(1, 1, turn) for turn in range(lines - 1, split - 1, -1)],
    ]
    early_blocks, late_blocks = sum(groups[:split], []), sum(groups[split:], [])

    def stat_row(block):
        return (2 * block[0] + block[1]) * lines + block[2]

    normed = normalized(hidden, norm_gain)

    last = jnp.arange(input_ids.shape[0]) % group_len == group_len - 1
    targets = jnp.where(last, -1, jnp.roll(input_ids, -1) - first_col)
    ids = jnp.stack([targets, sampled_ids - first_col]).reshape(2, reps * shards, length)
    side, across, turn = (np.array(values) for values in zip(*(early_blocks + late_blocks)))
    holder = (rep ^ (2 * across[None] + np.arange(2)[:, None])).reshape(-1)
    place = 2 * ((shard // 2 - turn) % lines) + ((shard % 2) ^ side)
    ids = jnp.take(ids, holder * shards + jnp.tile(place, 2), axis=1)
    ids = ids.reshape(2, 2, len(side), length)
    early_ids = ids[:, :, :len(early_blocks)].reshape(2, 1, -1)
    late_ids = ids[:, :, len(early_blocks):].reshape(2, 1, -1)
    early_ids, late_ids = [early_ids[0], early_ids[1]], [late_ids[0], late_ids[1]]
    rep_scalar = rep.astype(jnp.int32).reshape(1)
    stats = jnp.zeros((8 * lines, 128), jnp.float32)

    held = {(0, 0, 0): normed}
    early_exp = None

    def logits(group, stats, *gates, first_row=0, exp_rows=None, into=None):
        blocks = [held[block] for block in group]
        at = -1 if group is groups[0] else 0
        blocks[at] = after(blocks[at], *gates)
        rows = [stat_row(block) for block in group]
        exp_rows = exp_rows or len(group) * length
        return round_logits(blocks, rows, head_weight, stats, first_row, exp_rows, into)

    def diagonal(turn):
        if turn == 1:
            return to_z(held[1, 1, 0], 1)
        if turn == 2:
            return to_x(held[1, 0, turn])
        return to_y(held[0, 1, turn])

    for turn in range(lines):
        block = held[0, 0, turn]
        following = to_z(block, 1) if turn + 1 < lines else None
        held[0, 1, turn] = to_x(block)
        held[1, 0, turn] = to_y(block)
        if turn + 1 < lines:
            arrived = [following, held[0, 1, turn], held[1, 0, turn]]
            if turn == 0:
                arrived = [following, *early_ids, *late_ids, stats]
            elif turn < split:
                arrived += [early_exp]
            else:
                middle_exp, stats = logits(
                    groups[split], stats, exp_rows=5 * length
                )
                arrived = [following, held[0, 1, turn], early_exp, middle_exp]
            arrived = lax.optimization_barrier(tuple(arrived))
            held[0, 0, turn + 1] = arrived[0]
            if turn == 0:
                early_ids, late_ids = list(arrived[1:3]), list(arrived[3:5])
                stats, = arrived[5:]
                head_weight, *late_ids = prepared(head_weight, *late_ids, stats)
            elif turn < split:
                held[0, 1, turn], held[1, 0, turn], early_exp = arrived[1:]
            else:
                held[0, 1, turn], early_exp, middle_exp = arrived[1:]
            held[1, 1, turn] = diagonal(turn)
        if turn < split:
            size = len(groups[turn]) * length
            early_exp, stats = logits(
                groups[turn], stats, held[0, 0, turn + 1],
                first_row=turn * size, exp_rows=split * size, into=early_exp,
            )

    early = [held[block] for block in early_blocks]
    early[-1] = after(early[-1], held[0, 0, lines - 1])
    early = turned_features(rep_scalar, early, rows)
    early = [early[0], to_core(early[1])]
    middle_exp, stats = logits(
        groups[split + 1], stats, held[0, 0, lines - 1], early[0],
        first_row=2 * length, exp_rows=5 * length, into=middle_exp,
    )
    held[0, 1, lines - 1] = after(held[0, 1, lines - 1], middle_exp)
    held[1, 1, lines - 1] = diagonal(lines - 1)
    early_ids[0] = after(early_ids[0], middle_exp, held[0, 1, lines - 1])
    sums = one_hot_sums(early, early_ids, columns)
    last_exp, stats = logits(groups[split + 2], stats, *sums, exp_rows=5 * length)
    last_exp, stats = logits(
        groups[-1], stats, first_row=3 * length, exp_rows=5 * length, into=last_exp
    )
    exps = [early_exp, middle_exp, last_exp]
    across_stats, core_stats, both_stats = to_y(stats), to_core(stats), to_y_core(stats)
    ready = lax.optimization_barrier((early_exp, middle_exp, stats))
    other_exps = [to_core(exp) for exp in ready[:2]]
    late = [held[block] for block in late_blocks]
    late[0] = after(late[0], across_stats)
    late = turned_features(rep_scalar, late, rows)
    late = [late[0], to_core(late[1])]
    merged, first = merged_stats(
        after(stats, *other_exps), across_stats, core_stats, both_stats
    )
    all_stats = [merged] + [to_z(merged, -along) for along in range(1, lines)]
    other_exps.append(to_core(after(last_exp, merged)))
    return tuple(refresh_states(
        lines, length, [stat_row(block) for block in early_blocks + late_blocks], early, late,
        exps + other_exps, all_stats, first, late_ids, sums, moment, curvature,
    ))


def solution(mesh):
    in_specs = (
        P(("rep", "shard"), None),
        P(),
        P(),
        P(),
        P(None, "shard"),
        P("rep", "shard"),
        P("rep", "shard"),
    )
    out_specs = (P("rep", "shard"), P("rep", "shard"), P("rep", "shard"))
    reps, shards = mesh.shape["rep"], mesh.shape["shard"]

    def whole(hidden, *others):
        tokens, depth = hidden.shape
        length = tokens // (reps * shards)
        fits = hidden.size * 2 <= GATHER_BYTES and reps == 4 and shards == 8
        if fits and length == 64 and (depth // reps) % 128 == 0:
            plan = functools.partial(all_tokens, reps, shards)
        else:
            plan = by_groups

        return jax.shard_map(
            plan, mesh=mesh, in_specs=in_specs, out_specs=out_specs, check_vma=False
        )(hidden, *others)

    return whole
```

```python
import functools

import jax
import jax.numpy as jnp
import numpy as np
from jax import lax
from jax.experimental import pallas as pl
from jax.experimental.pallas import tpu as pltpu
from jax.sharding import PartitionSpec as P

EPS_NORM = 1e-05
BETA_ONE = 0.96
BETA_TWO = 0.95
RHO_SCALE = 0.05
GATHER_BYTES = 32 * 1024 * 1024
LOGITS_VMEM = 20 * 1024 * 1024
BRIEF = pl.CostEstimate(flops=1024, bytes_accessed=1024, transcendentals=0)


def normalize(hidden, norm_gain):
    values = hidden.astype(jnp.float32)
    row_scale = lax.rsqrt(jnp.mean(values * values, axis=-1, keepdims=True) + EPS_NORM)
    return (values * row_scale * norm_gain).astype(jnp.bfloat16)


def refresh(gradient, sample_grad, moment, curvature):
    moment_new = BETA_ONE * moment.astype(jnp.float32) + (1.0 - BETA_ONE) * gradient
    curvature_new = (
        BETA_TWO * curvature.astype(jnp.float32) + (1.0 - BETA_TWO) * sample_grad * sample_grad
    )
    update_direction = jnp.clip(moment_new / (RHO_SCALE * curvature_new), -1.0, 1.0)
    return (
        moment_new.astype(jnp.bfloat16),
        curvature_new.astype(jnp.bfloat16),
        update_direction.astype(jnp.bfloat16),
    )


def by_groups(hidden, norm_gain, input_ids, sampled_ids, head_weight, moment, curvature):
    normed = normalize(hidden, norm_gain)
    gathered = lax.all_gather(normed, "shard", axis=0, tiled=True)
    group_len = gathered.shape[0]
    columns = head_weight.shape[1]
    first_col = lax.axis_index("shard") * columns
    logits = jnp.dot(gathered, head_weight, preferred_element_type=jnp.float32)
    row_peak = lax.pmax(jnp.max(logits, axis=-1), "shard")
    scaled_exp = jnp.exp(logits - row_peak[:, None])
    row_sum = lax.psum(jnp.sum(scaled_exp, axis=-1), "shard")
    probabilities = (scaled_exp / row_sum[:, None]).astype(jnp.bfloat16)
    group_start = lax.axis_index("rep") * group_len
    token_ids = lax.dynamic_slice_in_dim(input_ids, group_start, group_len, 0)
    sample_ids = lax.dynamic_slice_in_dim(sampled_ids, group_start, group_len, 0)
    position = jnp.arange(group_len)
    shifted = jnp.roll(token_ids, -1) - first_col
    usable = (position < group_len - 1) & (shifted >= 0) & (shifted < columns)
    true_slot = jnp.where(usable, shifted, columns)
    sample_local = sample_ids - first_col
    inside = (sample_local >= 0) & (sample_local < columns)
    sample_slot = jnp.where(inside, sample_local, columns)
    shared = lax.dot_general(
        gathered, probabilities, (((0,), (0,)), ((), ())), preferred_element_type=jnp.float32
    )
    widened = gathered.astype(jnp.float32)
    true_sums = jax.ops.segment_sum(widened, true_slot, num_segments=columns + 1)[:columns]
    sample_sums = jax.ops.segment_sum(widened, sample_slot, num_segments=columns + 1)[:columns]
    true_part = (shared - true_sums.T).astype(jnp.bfloat16)
    sample_part = (shared - sample_sums.T).astype(jnp.bfloat16)
    gradient = lax.psum_scatter(true_part, "rep", scatter_dimension=0, tiled=True)
    sample_grad = lax.psum_scatter(sample_part, "rep", scatter_dimension=0, tiled=True)
    return refresh(
        gradient.astype(jnp.float32), sample_grad.astype(jnp.float32), moment, curvature
    )


def swap_pairs(count, bit):
    return [(index, index ^ bit) for index in range(count)]


def shift_pairs(lines, along, across):
    pairs = []
    for place in range(lines):
        for side in range(2):
            source = 2 * place + side
            pairs.append((source, 2 * ((place + along) % lines) + (side ^ across)))
    return pairs


def normalize_kernel(hidden_ref, gain_ref, normed_ref):
    normed_ref[...] = normalize(hidden_ref[...], gain_ref[...])


def normalized(hidden, norm_gain):
    return pl.pallas_call(
        normalize_kernel,
        out_shape=jax.ShapeDtypeStruct(hidden.shape, jnp.bfloat16),
        compiler_params=pltpu.CompilerParams(vmem_limit_bytes=8 * 1024 * 1024),
        cost_estimate=BRIEF,
        name="normalized",
    )(*in_hbm([hidden, norm_gain]))


def prepare_kernel(weight_ref, true_ids, sample_ids, *refs):
    held_ref, true_at, sample_at, arrived = refs[-4:]
    count = arrived.shape[0]
    band = weight_ref.shape[0] // count
    copies = [
        pltpu.make_async_copy(
            weight_ref.at[pl.ds(index * band, band)], held_ref.at[pl.ds(index * band, band)],
            arrived.at[index],
        )
        for index in range(count)
    ]
    for copy in copies:
        copy.start()
    lanes = lax.broadcasted_iota(jnp.int32, (128, 128), 1)
    for ids_ref, out_ref in ((true_ids, true_at), (sample_ids, sample_at)):
        for place in range(0, out_ref.shape[0], 128):
            ids = jnp.broadcast_to(ids_ref[:, place:place + 128], (128, 128)).T
            out_ref[place:place + 128] = ids - lanes
    for copy in copies:
        copy.wait()


def prepared(weight, true_ids, sample_ids, *earlier):
    near = pl.BlockSpec(memory_space=pltpu.VMEM)
    late = jax.ShapeDtypeStruct((true_ids.shape[1], 128), jnp.int32)
    return pl.pallas_call(
        prepare_kernel,
        in_specs=[pl.BlockSpec(memory_space=pltpu.HBM)] + [near] * (2 + len(earlier)),
        out_specs=[near] * 3,
        out_shape=[pltpu.VMEM(weight.shape, weight.dtype), late, late],
        scratch_shapes=[pltpu.SemaphoreType.DMA((4,))],
        compiler_params=pltpu.CompilerParams(vmem_limit_bytes=8 * 1024 * 1024),
        cost_estimate=BRIEF,
        name="prepared",
    )(pltpu.with_memory_space_constraint(weight, pltpu.HBM), true_ids, sample_ids, *earlier)


def logits_kernel(stat_rows, first_row, joins, *refs):
    count = len(stat_rows)
    block_refs, refs = refs[:count], refs[count:]
    if joins:
        refs = refs[:2] + refs[3:]
    weight_ref, before_ref, exp_ref, stats_ref, rows, logits, scaled_exp, highs, sums, sent = refs
    tokens, columns = logits.shape
    length = tokens // count
    half = stats_ref.shape[0] // 2
    for index, ref in enumerate(block_refs):
        rows[index * length:(index + 1) * length] = ref[...]
    highs[...] = jnp.full(highs.shape, -jnp.inf, jnp.float32)
    width = min(256, columns)

    def multiply(index, carry):
        place = pl.ds(pl.multiple_of(index * width, width), width)
        part = jnp.dot(rows[...], weight_ref[:, place], preferred_element_type=jnp.float32)
        logits[:, place] = part
        high = functools.reduce(
            jnp.maximum, [part[:, lane:lane + 128] for lane in range(0, width, 128)]
        )
        highs[...] = jnp.maximum(highs[...], high)
        return carry

    lax.fori_loop(0, columns // width, multiply, 0)
    highs[...] = jnp.broadcast_to(jnp.max(highs[...], axis=1, keepdims=True), highs.shape)
    chunk = 16
    copies = []
    for block in range(count):

        def scale(index, carry, block=block):
            place = pl.ds(pl.multiple_of(block * length + index * chunk, chunk), chunk)
            peak = highs[place, :]
            total = jnp.zeros((chunk, 128), jnp.float32)
            for lane in range(0, columns, 128):
                scaled = jnp.exp(logits[place, lane:lane + 128] - peak)
                scaled_exp[place, lane:lane + 128] = scaled.astype(jnp.bfloat16)
                total += scaled
            sums[place, :] = total
            return carry

        lax.fori_loop(0, length // chunk, scale, 0, unroll=2)
        place = pl.ds(block * length, length)
        target = pl.ds(first_row + block * length, length)
        copies.append(
            pltpu.make_async_copy(scaled_exp.at[place], exp_ref.at[target], sent.at[block])
        )
        copies[-1].start()
    totals = jnp.broadcast_to(jnp.sum(sums[...], axis=1, keepdims=True), sums.shape)
    stats_ref[...] = before_ref[...]
    for base, values in ((0, highs[...].T[0:1]), (half, totals.T[0:1])):
        for index, row in enumerate(stat_rows):
            stats_ref[base + row:base + row + 1, :length] = (
                values[:, index * length:(index + 1) * length]
            )
    for copy in copies:
        copy.wait()


def round_logits(blocks, stat_rows, held_weight, before, first_row, exp_rows, into):
    depth, columns = held_weight.shape
    length = blocks[0].shape[0]
    tokens = length * len(blocks)
    near = pl.BlockSpec(memory_space=pltpu.VMEM)
    held_weight = pltpu.with_memory_space_constraint(held_weight, pltpu.VMEM)
    far = pl.BlockSpec(memory_space=pltpu.HBM)
    joins = [] if into is None else [pltpu.with_memory_space_constraint(into, pltpu.HBM)]
    return pl.pallas_call(
        functools.partial(logits_kernel, stat_rows, first_row, len(joins)),
        in_specs=[near] * (len(blocks) + 2) + [far] * len(joins),
        input_output_aliases={len(blocks) + 2: 0} if joins else {},
        out_specs=[far, near],
        out_shape=[
            pltpu.HBM((exp_rows, columns), jnp.bfloat16),
            jax.ShapeDtypeStruct(before.shape, jnp.float32),
        ],
        scratch_shapes=[
            pltpu.VMEM((tokens, depth), jnp.bfloat16),
            pltpu.VMEM((tokens, columns), jnp.float32),
            pltpu.VMEM((tokens, columns), jnp.bfloat16),
            pltpu.VMEM((tokens, 128), jnp.float32),
            pltpu.VMEM((tokens, 128), jnp.float32),
            pltpu.SemaphoreType.DMA((len(blocks),)),
        ],
        compiler_params=pltpu.CompilerParams(vmem_limit_bytes=LOGITS_VMEM),
        cost_estimate=BRIEF,
        name="round_logits",
    )(*blocks, held_weight, before, *joins)


def turn_kernel(count, rep_ref, *refs):
    mine_ref, other_ref = refs[count:]
    step = pl.program_id(0)
    turned = jnp.concatenate([ref[...] for ref in refs[:count]], axis=0).T

    @pl.when(step == 0)
    def _():
        mine_ref[...] = turned

    @pl.when(step == 1)
    def _():
        other_ref[...] = turned


def turned_features(rep, blocks, rows):
    length = blocks[0].shape[0]
    tokens = length * len(blocks)
    whole = pl.BlockSpec((rows, tokens), lambda step, rep_ref: (0, 0))
    block = pl.BlockSpec((length, rows), lambda step, rep_ref: (0, rep_ref[0] ^ step))
    return pl.pallas_call(
        functools.partial(turn_kernel, len(blocks)),
        grid_spec=pltpu.PrefetchScalarGridSpec(
            num_scalar_prefetch=1,
            grid=(2,),
            in_specs=[block] * len(blocks),
            out_specs=[whole, whole],
        ),
        out_shape=[jax.ShapeDtypeStruct((rows, tokens), jnp.bfloat16)] * 2,
        compiler_params=pltpu.CompilerParams(vmem_limit_bytes=20 * 1024 * 1024),
        cost_estimate=BRIEF,
        name="turned_features",
    )(rep, *blocks)


def one_hot_kernel(count, *refs):
    feature_refs, refs = refs[:count], refs[count:]
    true_ref, sample_ref, true_out, sample_out = refs
    width = true_out.shape[1]
    features = jnp.concatenate([ref[...] for ref in feature_refs], axis=1)
    columns = pl.program_id(0) * width + lax.broadcasted_iota(
        jnp.int32, (width, features.shape[1]), 0
    )
    hot = jnp.concatenate([columns == true_ref[...], columns == sample_ref[...]], axis=0)
    totals = lax.dot_general(
        features, hot.astype(jnp.float32).astype(jnp.bfloat16),
        (((1,), (1,)), ((), ())), preferred_element_type=jnp.float32,
    )
    true_out[...] = totals[:, :width].astype(jnp.bfloat16)
    sample_out[...] = totals[:, width:].astype(jnp.bfloat16)


def one_hot_sums(features, ids, columns):
    rows = features[0].shape[0]
    width = min(256, columns)
    whole = lambda array: pl.BlockSpec(array.shape, lambda step: (0, 0))
    tile = pl.BlockSpec((rows, width), lambda step: (0, step))
    return pl.pallas_call(
        functools.partial(one_hot_kernel, len(features)),
        grid=(columns // width,),
        in_specs=[whole(array) for array in (*features, *ids)],
        out_specs=[tile, tile],
        out_shape=[pltpu.HBM((rows, columns), jnp.bfloat16)] * 2,
        compiler_params=pltpu.CompilerParams(vmem_limit_bytes=24 * 1024 * 1024),
        cost_estimate=BRIEF,
        name="one_hot_sums",
    )(*features, *ids)


def merge_kernel(own_ref, across_ref, core_ref, both_ref, merged_ref, first_ref):
    rows = own_ref.shape[0] // 2
    side = rows // 2
    for core, (near, far) in enumerate(((own_ref, across_ref), (core_ref, both_ref))):
        place = core * rows
        first, total = near[:rows], near[rows:]
        second = jnp.concatenate([far[side:rows], far[:side]], axis=0)
        other = jnp.concatenate([far[rows + side:], far[rows:rows + side]], axis=0)
        peak = jnp.maximum(first, second)
        merged_ref[place:place + rows] = peak
        merged_ref[2 * rows + place:3 * rows + place] = (
            total * jnp.exp(first - peak) + other * jnp.exp(second - peak)
        )
        first_ref[place:place + rows] = first


def merged_stats(own, across, core, both):
    rows, lanes = own.shape
    return pl.pallas_call(
        merge_kernel,
        out_shape=[
            jax.ShapeDtypeStruct((2 * rows, lanes), jnp.float32),
            jax.ShapeDtypeStruct((rows, lanes), jnp.float32),
        ],
        compiler_params=pltpu.CompilerParams(vmem_limit_bytes=4 * 1024 * 1024),
        cost_estimate=BRIEF,
        name="merged_stats",
    )(own, across, core, both)


def refresh_kernel(lines, length, block_rows, *refs):
    early_refs, late_refs, refs = refs[:2], refs[2:4], refs[4:]
    exp_refs, refs = refs[:6], refs[6:]
    stats_refs, refs = refs[:lines], refs[lines:]
    (first_ref, true_at, sample_at, true_sum, sample_sum, moment_ref, curvature_ref,
     moment_out, curvature_out, update_out, factors) = refs
    step = pl.program_id(0)
    width = moment_out.shape[1]
    early = early_refs[0].shape[1]
    late = late_refs[0].shape[1]

    @pl.when(step == 0)
    def _():
        rows = first_ref.shape[0]

        def turned(values, along):
            return jnp.concatenate([
                values[group + (turn + along) % lines:group + (turn + along) % lines + 1]
                for group in range(0, rows, lines) for turn in range(lines)
            ], axis=0) if along else values

        peaks = [turned(ref[:rows], along) for along, ref in enumerate(stats_refs)]
        totals = [turned(ref[rows:], along) for along, ref in enumerate(stats_refs)]
        peak = functools.reduce(jnp.maximum, peaks)
        total = sum(t * jnp.exp(p - peak) for p, t in zip(peaks, totals))
        factor = jnp.exp(first_ref[...] - peak) / total
        per_core = rows // 2
        full = jnp.concatenate([factor, jnp.zeros((128 - rows, 128), jnp.float32)], axis=0).T
        for core in range(2):
            for index, row in enumerate(block_rows):
                place = (core * len(block_rows) + index) * length
                at = core * per_core + row
                factors[place:place + length] = jnp.broadcast_to(
                    full[:length, at:at + 1], (length, 128)
                )

    def probs(ref, place, lane):
        scale = factors[place:place + ref.shape[0]]
        return ref[:, lane:lane + 128].astype(jnp.float32) * scale

    early_sides, true_sides, sample_sides = [], [], []
    for core in range(2):
        first_exp, *late_exps = exp_refs[3 * core:3 * core + 3]
        place = core * (early + late)
        early_sides.append(jnp.concatenate([
            probs(first_exp, place, lane).astype(jnp.bfloat16) for lane in range(0, width, 128)
        ], axis=1))
        place += early
        at = core * late
        for ref in late_exps:
            rows = slice(at, at + ref.shape[0])
            true_parts, sample_parts = [], []
            for lane in range(0, width, 128):
                prob = probs(ref, place, lane)
                column = step * width + lane
                true_hot = jnp.where(true_at[rows] == column, 1.0, 0.0)
                sample_hot = jnp.where(sample_at[rows] == column, 1.0, 0.0)
                true_parts.append((prob - true_hot).astype(jnp.bfloat16))
                sample_parts.append((prob - sample_hot).astype(jnp.bfloat16))
            true_sides.append(jnp.concatenate(true_parts, axis=1))
            sample_sides.append(jnp.concatenate(sample_parts, axis=1))
            place += ref.shape[0]
            at += ref.shape[0]
    early_features = jnp.concatenate([ref[...] for ref in early_refs], axis=1)
    late_features = jnp.concatenate([ref[...] for ref in late_refs], axis=1)

    def product(features, sides):
        return jnp.dot(
            features, jnp.concatenate(sides, axis=0), preferred_element_type=jnp.float32
        )

    shared = product(early_features, early_sides)
    gradient = product(late_features, true_sides) + (shared - true_sum[...].astype(jnp.float32))
    sample_grad = product(late_features, sample_sides) + (
        shared - sample_sum[...].astype(jnp.float32)
    )
    moment_out[...], curvature_out[...], update_out[...] = refresh(
        gradient, sample_grad, moment_ref[...], curvature_ref[...]
    )


def refresh_states(lines, length, block_rows, early, late, exps, stats, first,
                   late_ids, sums, moment, curvature):
    rows, columns = moment.shape
    width = min(256, columns)
    whole = lambda array: pl.BlockSpec(array.shape, lambda step: (0, 0))
    tile = pl.BlockSpec((rows, width), lambda step: (0, step))
    return pl.pallas_call(
        functools.partial(refresh_kernel, lines, length, block_rows),
        grid=(columns // width,),
        in_specs=[whole(array) for array in (*early, *late)]
        + [pl.BlockSpec((array.shape[0], width), lambda step: (0, step)) for array in exps]
        + [whole(array) for array in (*stats, first, *late_ids)]
        + [tile] * 4,
        out_specs=[tile] * 3,
        out_shape=[jax.ShapeDtypeStruct((rows, columns), jnp.bfloat16)] * 3,
        scratch_shapes=[pltpu.VMEM((2 * length * len(block_rows), 128), jnp.float32)],
        compiler_params=pltpu.CompilerParams(vmem_limit_bytes=36 * 1024 * 1024),
        cost_estimate=BRIEF,
        name="refresh_states",
    )(
        *early, *late, *in_hbm(exps[:3]), *exps[3:], *stats, first, *late_ids,
        *in_hbm(sums, [moment, curvature])
    )


def in_hbm(*lists):
    return [pltpu.with_memory_space_constraint(array, pltpu.HBM) for array in sum(map(list, lists), [])]


def after(value, *others):
    return lax.optimization_barrier((value, *others))[0]


def all_tokens(reps, shards, hidden, norm_gain, input_ids, sampled_ids, head_weight, moment, curvature):
    lines = shards // 2
    length = hidden.shape[0]
    rows, columns = moment.shape
    rep = lax.axis_index("rep")
    shard = lax.axis_index("shard")
    first_col = shard * columns
    group_len = length * shards

    def to_x(values):
        return lax.ppermute(values, "rep", swap_pairs(reps, 2))

    def to_core(values):
        return lax.ppermute(values, "rep", swap_pairs(reps, 1))

    def to_y(values):
        return lax.ppermute(values, "shard", swap_pairs(shards, 1))

    def to_y_core(values):
        pairs = [
            (rep_at * shards + at, (rep_at ^ 1) * shards + (at ^ 1))
            for rep_at in range(reps) for at in range(shards)
        ]
        return lax.ppermute(values, ("rep", "shard"), pairs)

    def to_z(values, along):
        return lax.ppermute(values, "shard", shift_pairs(lines, along, 0))

    split = lines // 2
    plain = [(0, 0), (0, 1), (1, 0)]
    groups = [[(*kind, turn) for kind in plain] for turn in range(split)]
    groups += [
        [(0, 0, split), (1, 1, 0)],
        [(0, 1, split), (1, 0, split), (0, 0, split + 1)],
        [(0, 1, split + 1), (1, 0, split + 1), (1, 1, 1)],
        [(1, 1, turn) for turn in range(lines - 1, split - 1, -1)],
    ]
    early_blocks, late_blocks = sum(groups[:split], []), sum(groups[split:], [])

    def stat_row(block):
        return (2 * block[0] + block[1]) * lines + block[2]

    normed = normalized(hidden, norm_gain)

    last = jnp.arange(input_ids.shape[0]) % group_len == group_len - 1
    targets = jnp.where(last, -1, jnp.roll(input_ids, -1) - first_col)
    ids = jnp.stack([targets, sampled_ids - first_col]).reshape(2, reps * shards, length)
    side, across, turn = (np.array(values) for values in zip(*(early_blocks + late_blocks)))
    holder = (rep ^ (2 * across[None] + np.arange(2)[:, None])).reshape(-1)
    place = 2 * ((shard // 2 - turn) % lines) + ((shard % 2) ^ side)
    ids = jnp.take(ids, holder * shards + jnp.tile(place, 2), axis=1)
    ids = ids.reshape(2, 2, len(side), length)
    early_ids = ids[:, :, :len(early_blocks)].reshape(2, 1, -1)
    late_ids = ids[:, :, len(early_blocks):].reshape(2, 1, -1)
    early_ids, late_ids = [early_ids[0], early_ids[1]], [late_ids[0], late_ids[1]]
    rep_scalar = rep.astype(jnp.int32).reshape(1)
    stats = jnp.zeros((8 * lines, 128), jnp.float32)

    held = {(0, 0, 0): normed}
    early_exp = None

    def logits(group, stats, *gates, first_row=0, exp_rows=None, into=None):
        blocks = [held[block] for block in group]
        at = -1 if group is groups[0] else 0
        blocks[at] = after(blocks[at], *gates)
        rows = [stat_row(block) for block in group]
        exp_rows = exp_rows or len(group) * length
        return round_logits(blocks, rows, head_weight, stats, first_row, exp_rows, into)

    def diagonal(turn):
        if turn == 1:
            return to_z(held[1, 1, 0], 1)
        if turn == 2:
            return to_x(held[1, 0, turn])
        return to_y(held[0, 1, turn])

    for turn in range(lines):
        block = held[0, 0, turn]
        following = to_z(block, 1) if turn + 1 < lines else None
        held[0, 1, turn] = to_x(block)
        held[1, 0, turn] = to_y(block)
        if turn + 1 < lines:
            arrived = [following, held[0, 1, turn], held[1, 0, turn]]
            if turn == 0:
                arrived = [following, *early_ids, *late_ids, stats]
            elif turn < split:
                arrived += [early_exp]
            else:
                middle_exp, stats = logits(
                    groups[split], stats, exp_rows=5 * length
                )
                arrived = [following, held[0, 1, turn], early_exp, middle_exp]
            arrived = lax.optimization_barrier(tuple(arrived))
            held[0, 0, turn + 1] = arrived[0]
            if turn == 0:
                early_ids, late_ids = list(arrived[1:3]), list(arrived[3:5])
                stats, = arrived[5:]
                head_weight, *late_ids = prepared(head_weight, *late_ids, stats)
            elif turn < split:
                held[0, 1, turn], held[1, 0, turn], early_exp = arrived[1:]
            else:
                held[0, 1, turn], early_exp, middle_exp = arrived[1:]
            held[1, 1, turn] = diagonal(turn)
        if turn < split:
            size = len(groups[turn]) * length
            early_exp, stats = logits(
                groups[turn], stats, held[0, 0, turn + 1],
                first_row=turn * size, exp_rows=split * size, into=early_exp,
            )

    early = [held[block] for block in early_blocks]
    early[-1] = after(early[-1], held[0, 0, lines - 1])
    early = turned_features(rep_scalar, early, rows)
    early = [early[0], to_core(early[1])]
    middle_exp, stats = logits(
        groups[split + 1], stats, held[0, 0, lines - 1], early[0],
        first_row=2 * length, exp_rows=5 * length, into=middle_exp,
    )
    held[0, 1, lines - 1] = after(held[0, 1, lines - 1], middle_exp)
    held[1, 1, lines - 1] = diagonal(lines - 1)
    early_ids[0] = after(early_ids[0], middle_exp, held[0, 1, lines - 1])
    sums = one_hot_sums(early, early_ids, columns)
    last_exp, stats = logits(groups[split + 2], stats, *sums, exp_rows=5 * length)
    last_exp, stats = logits(
        groups[-1], stats, first_row=3 * length, exp_rows=5 * length, into=last_exp
    )
    exps = [early_exp, middle_exp, last_exp]
    across_stats, core_stats, both_stats = to_y(stats), to_core(stats), to_y_core(stats)
    ready = lax.optimization_barrier((early_exp, middle_exp, stats))
    other_exps = [to_core(exp) for exp in ready[:2]]
    late = [held[block] for block in late_blocks]
    late[0] = after(late[0], across_stats)
    late = turned_features(rep_scalar, late, rows)
    late = [late[0], to_core(late[1])]
    merged, first = merged_stats(
        after(stats, other_exps[0]), across_stats, core_stats, both_stats
    )
    all_stats = [merged] + [to_z(merged, -along) for along in range(1, lines)]
    other_exps.append(to_core(after(last_exp, merged)))
    return tuple(refresh_states(
        lines, length, [stat_row(block) for block in early_blocks + late_blocks], early, late,
        exps + other_exps, all_stats, first, late_ids, sums, moment, curvature,
    ))


def solution(mesh):
    in_specs = (
        P(("rep", "shard"), None),
        P(),
        P(),
        P(),
        P(None, "shard"),
        P("rep", "shard"),
        P("rep", "shard"),
    )
    out_specs = (P("rep", "shard"), P("rep", "shard"), P("rep", "shard"))
    reps, shards = mesh.shape["rep"], mesh.shape["shard"]

    def whole(hidden, *others):
        tokens, depth = hidden.shape
        length = tokens // (reps * shards)
        fits = hidden.size * 2 <= GATHER_BYTES and reps == 4 and shards == 8
        if fits and length == 64 and (depth // reps) % 128 == 0:
            plan = functools.partial(all_tokens, reps, shards)
        else:
            plan = by_groups

        return jax.shard_map(
            plan, mesh=mesh, in_specs=in_specs, out_specs=out_specs, check_vma=False
        )(hidden, *others)

    return whole
```
